32 devices in a mesh: batch: 16 (over z, y, x), tensor: 2 (over core).
Axes of the slice: x: 2, y: 2, z: 4, core: 2. Of those that a mesh axis runs over, the one named last changes fastest.
Arguments:
- hidden_in: bfloat16 [81920, 768], P(('batch', 'tensor')), may hold values from -6 to 6
- lengths: int32 [160, 8], P('batch'), may hold values from 1 to 256, 512 in all within a row
- attn_gain: float32 [768], replicated, may hold values from 0.1 to 1.9
- attn_query: bfloat16 [768, 768], P(None, 'tensor'), may hold values from -0.21875 to 0.21875
- attn_key: bfloat16 [768, 768], P(None, 'tensor'), may hold values from -0.21875 to 0.21875
- attn_value: bfloat16 [768, 768], P(None, 'tensor'), may hold values from -0.21875 to 0.21875
- attn_out: bfloat16 [768, 768], P('tensor'), may hold values from -1.75 to 1.75
- ffn_gain: float32 [768], replicated, may hold values from 0.1 to 1.9
- ffn_in: bfloat16 [768, 3072], P(None, 'tensor'), may hold values from -0.21875 to 0.21875
- ffn_out: bfloat16 [3072, 768], P('tensor'), may hold values from -0.109375 to 0.109375
- side_state: bfloat16 [81920, 96], P(('batch', 'tensor')), may hold values from -6 to 6
- gate_alpha: float32 [96], replicated, may hold values from -0.3 to 0.3
- down_w: bfloat16 [768, 96], replicated, may hold values from -0.21875 to 0.21875
- side_attn_gain: float32 [96], replicated, may hold values from 0.1 to 1.9
- side_query: bfloat16 [96, 96], replicated, may hold values from -0.625 to 0.625
- side_key: bfloat16 [96, 96], replicated, may hold values from -0.625 to 0.625
- side_value: bfloat16 [96, 96], replicated, may hold values from -0.625 to 0.625
- side_proj: bfloat16 [96, 96], replicated, may hold values from -3.5 to 3.5
- side_ffn_gain: float32 [96], replicated, may hold values from 0.1 to 1.9
- side_expand: bfloat16 [96, 384], replicated, may hold values from -0.625 to 0.625
- side_shrink: bfloat16 [384, 96], replicated, may hold values from -0.3125 to 0.3125
- cotangent: bfloat16 [81920, 96], P(('batch', 'tensor')), may hold values from -6 to 6
Outputs:
- backbone_out: bfloat16 [81920, 768], P(('batch', 'tensor'))
- side_out: float32 [81920, 96], P(('batch', 'tensor'))
- state_grad: float32 [81920, 96], P(('batch', 'tensor'))
- down_grad: float32 [768, 96], replicated
- alpha_grad: float32 [96], replicated
- attn_gain_grad: float32 [96], replicated
- query_weight_grad: float32 [96, 96], replicated
- key_weight_grad: float32 [96, 96], replicated
- value_weight_grad: float32 [96, 96], replicated
- proj_grad: float32 [96, 96], replicated
- ffn_gain_grad: float32 [96], replicated
- expand_grad: float32 [96, 384], replicated
- shrink_grad: float32 [384, 96], replicated
The draws below stay inside these ranges and needn't reach their ends.
Inputs may be any that keep to these rules, and one draw needn't show every extreme that they name: Each row's 8 lengths add up to 512, and the longest of each row is exactly 256.
All inputs are finite; a program needn't handle non-finite values.
Results may differ from the reference program's by a relative error of at most 0.03.
Values may be sent and summed in bfloat16 or wider, within the bound.
No kernel may reach another device: no remote copies, remote signals or barrier semaphores. Data moves between devices by JAX's collectives and lax.ppermute only.
A program may use at most 128 MiB of HBM per device.

```python
import math
import jax
import jax.numpy as jnp
import numpy as np
from jax import lax

D = 768
HEADS = 12
HEAD_DIM = 64
FF = 3072
DS = 96
SIDE_HEADS = 12
SIDE_HEAD_DIM = 8
SFF = 384
ROW_LEN = 512
SEGS = 8
MAXLEN = 256
ROWS = 160
TOKENS = 81920


def block_levels(rng, shape, shards, smallest, top_value):
    def one(dim, shards_of):
        draws = jax.random.uniform(jax.random.fold_in(jax.random.fold_in(rng, 6), dim), (shards_of,), jnp.float32, smallest / len(shards), top_value / len(shards))
        return jnp.repeat(jnp.exp(draws), shape[dim] // shards_of).reshape((-1,) + (1,) * (len(shape) - dim - 1))

    level = one(*shards[0])
    for cut in shards[1:]:
        level = level * one(*cut)
    return level


def profile(number_of, total, most, lean):
    weights = [(1 << 20) // math.isqrt(rank ** lean) + 1 for rank in range(2, number_of + 1)]
    spare, holding = total - most - (number_of - 1), [1] * (number_of - 1)
    while spare > 0:
        movable = [i for i in range(number_of - 1) if holding[i] < most]
        pool, budget = sum([weights[i] for i in movable]), spare
        for i in movable:
            more = min(most - holding[i], max(1, budget * weights[i] // pool), spare)
            holding[i] = holding[i] + more
            spare = spare - more
    return np.array([most] + holding)


def ragged(rng, count, total, most, slope):
    if count == 2:
        one = jax.random.randint(rng, (), max(1, total - most), min(most, total - 1) + 1)
        return jnp.stack([one, total - one])
    tallies = jnp.asarray(profile(count, total, most, slope), jnp.int32)
    pairs = (count - 1) // 2
    giver, sink = tallies[1:1 + 2 * pairs:2], tallies[2:2 + 2 * pairs:2]
    room = jnp.minimum(giver - 1, most - sink)
    shifted = jax.random.randint(jax.random.fold_in(rng, 1), (pairs,), 0, 1 << 20) % (room + 1)
    tallies = tallies.at[1:1 + 2 * pairs:2].set(giver - shifted).at[2:2 + 2 * pairs:2].set(sink + shifted)
    return tallies[jax.random.permutation(jax.random.fold_in(rng, 2), count)]


def scatter_about(own_key, shape, scale, bound, cuts=(), kind=jnp.bfloat16):
    level = block_levels(own_key, shape, cuts, -0.22, 0.18) if cuts else 1.0
    drawn = jax.random.normal(own_key, shape, jnp.float32) * scale * level
    return jnp.minimum(jnp.maximum(drawn, -bound), bound).astype(kind)


def setup_inputs(seed: int = 0) -> dict:
    keys = jax.random.split(jax.random.key(seed), 23)
    return {
        "hidden_in": scatter_about(keys[0], (TOKENS, D), 1.0, 6.0, ((0, 32),)),
        "lengths": jax.vmap(lambda own: ragged(own, SEGS, ROW_LEN, MAXLEN, 2))(jax.random.split(keys[1], ROWS)).reshape((ROWS, SEGS)).astype(jnp.int32),
        "attn_gain": jnp.clip(1.0 + 0.18 * jax.random.normal(keys[2], (D,), jnp.float32), 0.1, 1.9),
        "attn_query": scatter_about(keys[3], (D, D), D ** -0.5, 0.21875, ((1, 2),)),
        "attn_key": scatter_about(keys[4], (D, D), D ** -0.5, 0.21875, ((1, 2),)),
        "attn_value": scatter_about(keys[5], (D, D), D ** -0.5, 0.21875, ((1, 2),)),
        "attn_out": scatter_about(keys[6], (D, D), (D // 64) ** -0.5, 1.75, ((0, 2),)),
        "ffn_gain": jnp.clip(1.0 + 0.18 * jax.random.normal(keys[7], (D,), jnp.float32), 0.1, 1.9),
        "ffn_in": scatter_about(keys[8], (D, FF), D ** -0.5, 0.21875, ((1, 2),)),
        "ffn_out": scatter_about(keys[9], (FF, D), FF ** -0.5, 0.109375, ((0, 2),)),
        "side_state": scatter_about(keys[10], (TOKENS, DS), 1.0, 6.0, ((0, 32),)),
        "gate_alpha": jnp.clip(jax.random.uniform(keys[11], (DS,), jnp.float32, -0.3, 0.3), -0.3, 0.3),
        "down_w": scatter_about(keys[12], (D, DS), D ** -0.5, 0.21875),
        "side_attn_gain": jnp.clip(1.0 + 0.18 * jax.random.normal(keys[13], (DS,), jnp.float32), 0.1, 1.9),
        "side_query": scatter_about(keys[14], (DS, DS), DS ** -0.5, 0.625),
        "side_key": scatter_about(keys[15], (DS, DS), DS ** -0.5, 0.625),
        "side_value": scatter_about(keys[16], (DS, DS), DS ** -0.5, 0.625),
        "side_proj": scatter_about(keys[17], (DS, DS), (DS // 32) ** -0.5, 3.5),
        "side_ffn_gain": jnp.clip(1.0 + 0.18 * jax.random.normal(keys[18], (DS,), jnp.float32), 0.1, 1.9),
        "side_expand": scatter_about(keys[19], (DS, SFF), DS ** -0.5, 0.625),
        "side_shrink": scatter_about(keys[20], (SFF, DS), SFF ** -0.5, 0.3125),
        "cotangent": scatter_about(keys[21], (TOKENS, DS), 1.0, 6.0, ((0, 32),)),
    }


epsilon = 1e-06

@jax.custom_vjp
def low(v):
    return lax.optimization_barrier(v.astype(jnp.bfloat16)).astype(jnp.float32)

@jax.custom_vjp
def low_back(v):
    return v

def low_keep(v):
    return (low(v), None)

def low_pass(kept, grad):
    return (grad,)

def back_keep(v):
    return (v, None)

def back_low(kept, grad):
    return (low(grad),)
low.defvjp(low_keep, low_pass)
low_back.defvjp(back_keep, back_low)

def matmul(first_operand, second_operand):
    return jnp.dot(first_operand, second_operand, precision=lax.Precision.HIGHEST, preferred_element_type=jnp.float32)

def inverse_rms(features):
    return lax.rsqrt(lax.optimization_barrier(jnp.mean(features * features, axis=-1, keepdims=True)) + epsilon)

def segment_ids(row_lengths):
    segment_ends = jnp.cumsum(row_lengths, axis=1).astype(jnp.int32)
    places = lax.broadcasted_iota(jnp.int32, (1, ROW_LEN, 1), 1)
    return lax.optimization_barrier(jnp.sum((places >= segment_ends[:, None, :]).astype(jnp.int32), axis=2)).astype(jnp.int32)

def attend(query_heads, key_heads, value_heads, segment_row, head_dim):
    scores = jnp.einsum('qhd,khd->hqk', query_heads, key_heads, precision=lax.Precision.HIGHEST) * head_dim ** (-0.5)
    scores = low_back(scores)
    same_doc = (segment_row[:, None] == segment_row[None, :])[None]
    scores = jnp.where(same_doc, scores, -1e+30)
    row_max = lax.optimization_barrier(jnp.max(scores, axis=-1, keepdims=True))
    raised = jnp.exp(scores - row_max)
    weights = low(raised / lax.optimization_barrier(jnp.sum(raised, axis=-1, keepdims=True)))
    return jnp.einsum('hqk,khd->qhd', weights, value_heads, precision=lax.Precision.HIGHEST)

def frozen_rows(row_block, block_ids, attn_gain, attn_query, attn_key, attn_value, attn_out, ffn_gain, ffn_in, ffn_out):
    flattened = row_block.reshape(-1, D)
    normed = low(flattened * inverse_rms(flattened) * attn_gain)
    split_shape = (-1, ROW_LEN, HEADS, HEAD_DIM)
    query_heads = low(matmul(normed, attn_query)).reshape(split_shape)
    key_heads = low(matmul(normed, attn_key)).reshape(split_shape)
    value_heads = low(matmul(normed, attn_value)).reshape(split_shape)
    context = lax.map(lambda element: attend(element[0], element[1], element[2], element[3], HEAD_DIM), (query_heads, key_heads, value_heads, block_ids))
    context = low(context.reshape(-1, D))
    middle = flattened + matmul(context, attn_out)
    normed = low(middle * inverse_rms(middle) * ffn_gain)
    hidden = low(jax.nn.gelu(matmul(normed, ffn_in)))
    return (middle + matmul(hidden, ffn_out)).astype(jnp.bfloat16)

def side_forward(trainable, side_input, backbone, block_ids):
    down_w, gate_alpha, side_attn_gain, side_query, side_key, side_value, side_proj, side_ffn_gain, side_expand, side_shrink = trainable
    mixing = jax.nn.sigmoid(gate_alpha / 0.1)
    lowered = low_back(matmul(backbone, down_w))
    inputs = mixing * lowered + (1.0 - mixing) * side_input
    normed = low(inputs * inverse_rms(inputs) * side_attn_gain)
    split_shape = (-1, ROW_LEN, SIDE_HEADS, SIDE_HEAD_DIM)
    query_heads = low_back(low(matmul(normed, side_query))).reshape(split_shape)
    key_heads = low_back(low(matmul(normed, side_key))).reshape(split_shape)
    value_heads = low_back(low(matmul(normed, side_value))).reshape(split_shape)
    one_row = jax.checkpoint(lambda element: attend(element[0], element[1], element[2], element[3], SIDE_HEAD_DIM))
    context = lax.map(one_row, (query_heads, key_heads, value_heads, block_ids))
    context = low_back(low(context.reshape(-1, DS)))
    middle = inputs + low_back(matmul(context, side_proj))
    normed = low(middle * inverse_rms(middle) * side_ffn_gain)
    hidden = low(jax.nn.gelu(low_back(matmul(normed, side_expand))))
    return middle + low_back(matmul(hidden, side_shrink))

def reference(hidden_in, lengths, attn_gain, attn_query, attn_key, attn_value, attn_out, ffn_gain, ffn_in, ffn_out, side_state, gate_alpha, down_w, side_attn_gain, side_query, side_key, side_value, side_proj, side_ffn_gain, side_expand, side_shrink, cotangent):
    to_float = lambda array: array.astype(jnp.float32)
    blocks = ROWS // 4
    segment = segment_ids(lengths).reshape(blocks, 4, ROW_LEN)
    frozen = tuple((to_float(member) for member in (attn_gain, attn_query, attn_key, attn_value, attn_out, ffn_gain, ffn_in, ffn_out)))
    row_blocks = to_float(hidden_in).reshape(blocks, 4, ROW_LEN, D)
    backbone = lax.map(lambda element: frozen_rows(element[0], element[1], *frozen), (row_blocks, segment))
    trainable = tuple((to_float(member) for member in (down_w, gate_alpha, side_attn_gain, side_query, side_key, side_value, side_proj, side_ffn_gain, side_expand, side_shrink)))
    side_inputs = to_float(side_state).reshape(blocks, 4 * ROW_LEN, DS)
    upstreams = to_float(cotangent).reshape(blocks, 4 * ROW_LEN, DS)

    def advance(totals, element):
        side_input, block_out, block_ids, upstream = element

        def forward(weights, start_input):
            return side_forward(weights, start_input, to_float(block_out), block_ids)
        result, pullback = jax.vjp(forward, trainable, side_input)
        weight_grads, input_grad = pullback(upstream)
        return (jax.tree.map(jnp.add, totals, weight_grads), (result, input_grad))
    totals = jax.tree.map(jnp.zeros_like, trainable)
    totals, (side_out, state_grad) = lax.scan(advance, totals, (side_inputs, backbone, segment, upstreams))
    return (backbone.reshape(-1, D), side_out.reshape(-1, DS), state_grad.reshape(-1, DS), totals[0], totals[1], totals[2], totals[3], totals[4], totals[5], totals[6], totals[7], totals[8], totals[9])
```

```python
import jax
import jax.numpy as jnp
from jax import lax
from jax.experimental import pallas as pl
from jax.experimental.pallas import tpu as pltpu
from jax.sharding import PartitionSpec as P

BF = jnp.bfloat16
F32 = jnp.float32
D = 768
HEAD_DIM = 64
DS = 96
SIDE_HEADS = 12
SIDE_HEAD_DIM = 8
SFF = 384
ROW_LEN = 512
SEGS = 8
HALF = 256
GRAD_LANES = 2048
LOG2E = 1.4426950408889634
EPS = 1e-06
VMEM_LIMIT = 63 * 1024 * 1024


def dot(a, b, ca=1, cb=0):
    return lax.dot_general(a, b, (((ca,), (cb,)), ((), ())), preferred_element_type=F32)


def gelu(x):
    x2 = x * x
    u = x * (x2 * (0.7978845608028654 * 0.044715) + 0.7978845608028654)
    h = 0.5 * x
    return h + h * jnp.tanh(u)


def gelu_and_slope(x):
    x2 = x * x
    u = x * (x2 * (0.7978845608028654 * 0.044715) + 0.7978845608028654)
    t = jnp.tanh(u)
    h = 0.5 * x
    du = 0.7978845608028654 * 3.0 * 0.044715 * x2 + 0.7978845608028654
    return h + h * t, 0.5 + 0.5 * t + h * (1.0 - t * t) * du


def row_starts(lens_ref, r):
    starts, begin = [], jnp.int32(0)
    long_start = jnp.int32(0)
    for j in range(SEGS):
        n = lens_ref[r * SEGS + j]
        starts.append((begin, n))
        long_start = jnp.where(n == HALF, begin, long_start)
        begin = begin + n
    return long_start, [((b - long_start) & (ROW_LEN - 1), n) for b, n in starts]


def fill_bias(bias_ref, docs):
    q = lax.broadcasted_iota(jnp.int32, (1, HALF), 1) + HALF
    low = jnp.zeros((1, HALF), jnp.int32)
    high = jnp.zeros((1, HALF), jnp.int32)
    for b, n in docs:
        inside = (q >= b) & (q < b + n)
        low = jnp.where(inside, b, low)
        high = jnp.where(inside, b + n, high)
    k = lax.broadcasted_iota(jnp.int32, (HALF, HALF), 0) + HALF
    bias_ref[...] = jnp.where((k >= low) & (k < high), 0.0, -1e30)


def turn_rows(src_ref, shift):
    n = src_ref.shape[1]
    part = shift & 7
    first = lax.shift_right_logical(shift, 3)
    groups = []
    for g in range(ROW_LEN // 8 + 1):
        start = pl.multiple_of(((first + g) & (ROW_LEN // 8 - 1)) * 8, 8)
        groups.append(src_ref[pl.ds(start, 8), :])
    wide = jnp.concatenate(groups, axis=0).reshape(ROW_LEN // 8 + 1, 8, n)
    back = (8 - part) & 7
    wide = pltpu.roll(wide, back, 1)
    place = lax.broadcasted_iota(jnp.int32, (ROW_LEN // 8, 8, n), 1)
    turned = jnp.where(place < 8 - part, wide[:-1], wide[1:])
    return turned.reshape(ROW_LEN, n)


def frozen_heads(normed, wqkv_ref, qkv_ref, vt_ref, ctxt_ref, bias_ref, wo):
    cols = wqkv_ref.shape[1] // 3
    pairs = cols // 128
    qkv_ref[...] = dot(normed, wqkv_ref[...]).astype(BF)
    vt_ref[...] = qkv_ref[:, 2 * cols :].T
    lane = lax.broadcasted_iota(jnp.int32, (1, 128), 1)
    keep = [(lane < 64).astype(F32).astype(BF), (lane >= 64).astype(F32).astype(BF)]
    for half in range(2):
        rows = slice(half * HALF, (half + 1) * HALF)
        for p in range(pairs):
            q2 = qkv_ref[rows, p * 128 : (p + 1) * 128]
            k2 = qkv_ref[rows, cols + p * 128 : cols + (p + 1) * 128]
            for j in range(2):
                s = dot(k2 * keep[j], q2, 1, 1) * (LOG2E / 8.0)
                if half:
                    s = s + bias_ref[...]
                e = jnp.exp2(s - jnp.max(s, axis=0, keepdims=True))
                inv = 1.0 / jnp.sum(e, axis=0, keepdims=True)
                hrow = slice(p * 128 + j * 64, p * 128 + (j + 1) * 64)
                mixed = dot(vt_ref[hrow, rows], e.astype(BF)) * inv
                ctxt_ref[hrow, rows] = mixed.astype(BF)
    return dot(ctxt_ref[...].T, wo)


def first_kernel(lens_ref, x_ref, gain_ref, wq_ref, wk_ref, wv_ref, wo_ref, normed_ref, mid_ref, wqkv_ref, qkv_ref, vt_ref, ctxt_ref, bias_ref, xf_ref):
    r = pl.program_id(0)
    cols = wq_ref.shape[1]

    @pl.when(r == 0)
    def _():
        wqkv_ref[:, :cols] = wq_ref[...]
        wqkv_ref[:, cols : 2 * cols] = wk_ref[...]
        wqkv_ref[:, 2 * cols :] = wv_ref[...]

    shift, docs = row_starts(lens_ref, r)
    fill_bias(bias_ref, docs)
    xf_ref[...] = x_ref[...].astype(F32)
    x = turn_rows(xf_ref, shift)
    xf_ref[...] = x
    normed = (x * lax.rsqrt(jnp.mean(x * x, axis=1, keepdims=True) + EPS) * gain_ref[...]).astype(BF)
    normed_ref[...] = normed
    mid_ref[...] = xf_ref[...] + frozen_heads(normed, wqkv_ref, qkv_ref, vt_ref, ctxt_ref, bias_ref, wo_ref[...])


def second_kernel(lens_ref, normed_ref, part_ref, wq_ref, wk_ref, wv_ref, wo_ref, mid_ref, wqkv_ref, qkv_ref, vt_ref, ctxt_ref, bias_ref):
    r = pl.program_id(0)
    cols = wq_ref.shape[1]

    @pl.when(r == 0)
    def _():
        wqkv_ref[:, :cols] = wq_ref[...]
        wqkv_ref[:, cols : 2 * cols] = wk_ref[...]
        wqkv_ref[:, 2 * cols :] = wv_ref[...]

    _, docs = row_starts(lens_ref, r)
    fill_bias(bias_ref, docs)
    mid_ref[...] = part_ref[...] + frozen_heads(normed_ref[...], wqkv_ref, qkv_ref, vt_ref, ctxt_ref, bias_ref, wo_ref[...])


def third_kernel(
    lens_ref,
    mid_ref,
    fgain_ref,
    w1a_ref,
    w1b_ref,
    w2a_ref,
    w2b_ref,
    side_ref,
    cot_ref,
    vecs_ref,
    downt_ref,
    sq_ref,
    sk_ref,
    sv_ref,
    proj_ref,
    expand_ref,
    shrinkt_ref,
    bb_ref,
    out_ref,
    state_ref,
    grads_ref,
    hid_ref,
    bias_ref,
    f_ref,
    cols_ref,
    wqkvt_ref,
    e_ref,
    ds_ref,
    inv_ref,
    ctxt_ref,
    dq_ref,
    qm_ref,
    acc_ref,
):
    r = pl.program_id(0)

    @pl.when(r == 0)
    def _():
        grads_ref[...] = jnp.zeros_like(grads_ref)
        acc_ref[...] = jnp.zeros_like(acc_ref)
        vt = vecs_ref[...].T
        for i in range(3):
            cols_ref[i] = jnp.broadcast_to(vt[:DS, i : i + 1], (DS, ROW_LEN))
        wqkvt_ref[:DS] = sq_ref[...].T
        wqkvt_ref[DS : 2 * DS] = sk_ref[...].T
        wqkvt_ref[2 * DS :] = sv_ref[...].T

    shift, docs = row_starts(lens_ref, r)
    fill_bias(bias_ref, docs)

    middle = mid_ref[...]
    normed = (middle * lax.rsqrt(jnp.mean(middle * middle, axis=1, keepdims=True) + EPS) * fgain_ref[...]).astype(BF)
    units = w1a_ref.shape[1]
    for i, w in enumerate((w1a_ref, w1b_ref)):
        for c in range(units // 256):
            hid_ref[:, i * units + c * 256 : i * units + (c + 1) * 256] = gelu(dot(normed, w[:, c * 256 : (c + 1) * 256])).astype(BF)
    f_ref[...] = mid_ref[...] + dot(hid_ref[:, :units], w2a_ref[...]) + dot(hid_ref[:, units:], w2b_ref[...])
    bb = f_ref[...].astype(BF)
    bb_ref[...] = turn_rows(f_ref, (ROW_LEN - shift) & (ROW_LEN - 1)).astype(BF)

    alpha = cols_ref[0]
    gain1 = cols_ref[1]
    gain2 = cols_ref[2]
    mixing = 1.0 / (1.0 + jnp.exp(alpha * -10.0))
    forward = (ROW_LEN - shift) & (ROW_LEN - 1)
    side = pltpu.roll(side_ref[...].astype(F32), forward, 1)
    cot = pltpu.roll(cot_ref[...].astype(F32), forward, 1)
    cotb = cot.astype(BF)
    lowered = dot(downt_ref[...], bb, 1, 1)
    inputs = mixing * lowered + (1.0 - mixing) * side
    scale1 = lax.rsqrt(jnp.mean(inputs * inputs, axis=0, keepdims=True) + EPS)
    fnt = (inputs * scale1 * gain1).astype(BF)
    qkvt = dot(wqkvt_ref[...], fnt).astype(BF)
    qt, kt, vt = qkvt[:DS], qkvt[DS : 2 * DS], qkvt[2 * DS :]
    lane = lax.broadcasted_iota(jnp.int32, (1, DS), 1)
    masks = [((lane >= 8 * h) & (lane < 8 * h + 8)).astype(F32).astype(BF) for h in range(SIDE_HEADS)]
    lane2 = lax.broadcasted_iota(jnp.int32, (1, 128), 1)
    masks2 = [
        (((lane2 >= 8 * h) & (lane2 < 8 * h + 8)) | (lane2 == DS + h) | (lane2 == DS + 16 + h)).astype(F32).astype(BF)
        for h in range(SIDE_HEADS)
    ]
    q, k, v = qt.T, kt.T, vt.T
    for half in range(2):
        rows = slice(half * HALF, (half + 1) * HALF)
        kh, qh = k[rows], qt[:, rows]
        for h in range(SIDE_HEADS):
            s = dot(kh * masks[h], qh) * (LOG2E * SIDE_HEAD_DIM**-0.5)
            if half:
                s = s + bias_ref[...]
            e = jnp.exp2(s - jnp.max(s, axis=0, keepdims=True))
            inv = 1.0 / jnp.sum(e, axis=0, keepdims=True)
            eb = e.astype(BF)
            e_ref[rows, h * HALF : (h + 1) * HALF] = eb
            mixed = dot(vt[16 * (h // 2) : 16 * (h // 2 + 1), rows], eb)
            low = 8 * (h % 2)
            ctxt_ref[8 * h : 8 * h + 8, rows] = mixed[low : low + 8] * inv
            inv_ref[8 * h : 8 * h + 8, rows] = jnp.broadcast_to(inv, (8, HALF))
    ctx = ctxt_ref[...]
    ctxb = ctx.astype(BF)
    middle_side = inputs + dot(proj_ref[...], ctxb, 0, 0)
    scale2 = lax.rsqrt(jnp.mean(middle_side * middle_side, axis=0, keepdims=True) + EPS)
    snt = (middle_side * scale2 * gain2).astype(BF)
    expanded = dot(expand_ref[...], snt, 0, 0)
    activated, slope = gelu_and_slope(expanded)
    activated = activated.astype(BF)
    side_out = middle_side + dot(shrinkt_ref[...], activated)
    out_ref[...] = pltpu.roll(side_out, shift, 1)

    activated_grad = dot(shrinkt_ref[...], cotb, 0, 0)
    expanded_grad = (activated_grad * slope).astype(BF)
    second_grad = dot(expand_ref[...], expanded_grad)
    w2 = second_grad * gain2
    ms = middle_side * scale2
    mean2 = jnp.mean(w2 * middle_side, axis=0, keepdims=True)
    middle_grad = cot + scale2 * w2 - ms * (scale2 * scale2) * mean2
    acc_ref[0] += second_grad * ms
    branch = middle_grad.astype(BF)
    context_grad = dot(proj_ref[...], branch).astype(BF).astype(F32)
    dop = (context_grad * inv_ref[...]).astype(BF)
    centre = jnp.sum((dop.astype(F32) * ctx).reshape(SIDE_HEADS, 8, ROW_LEN), axis=1)
    centre = jnp.concatenate([centre, jnp.zeros((4, ROW_LEN), F32)], axis=0)
    chigh = centre.astype(BF)
    clow = (centre - chigh.astype(F32)).astype(BF)
    dstack = jnp.concatenate([dop, -chigh, -clow], axis=0)
    vones = jnp.concatenate([v, jnp.ones((ROW_LEN, 32), BF)], axis=1)
    dopt = dop.T
    dks, dvs = [], []
    for half in range(2):
        rows = slice(half * HALF, (half + 1) * HALF)
        for h in range(SIDE_HEADS):
            cut = slice(h * HALF, (h + 1) * HALF)
            dp = dot(vones[rows] * masks2[h], dstack[:, rows])
            dsb = (e_ref[rows, cut].astype(F32) * dp).astype(BF)
            ds_ref[:, cut] = dsb
            mixed = dot(kt[16 * (h // 2) : 16 * (h // 2 + 1), rows], dsb)
            low = 8 * (h % 2)
            dq_ref[8 * h : 8 * h + 8, rows] = mixed[low : low + 8]
            qm_ref[0, cut, :] = q[rows] * masks[h]
            qm_ref[1, cut, :] = dopt[rows] * masks[h]
        dks.append(dot(ds_ref[...], qm_ref[0]))
        dvs.append(dot(e_ref[rows, :], qm_ref[1]))
    dqt = (dq_ref[...] * SIDE_HEAD_DIM**-0.5).astype(BF)
    dkt = (jnp.concatenate(dks, axis=0) * SIDE_HEAD_DIM**-0.5).astype(BF).T
    dvt = jnp.concatenate(dvs, axis=0).astype(BF).T
    dqkvt = jnp.concatenate([dqt, dkt, dvt], axis=0)
    first_grad = dot(wqkvt_ref[...], dqkvt, 0, 0)
    w1 = first_grad * gain1
    ins = inputs * scale1
    mean1 = jnp.mean(w1 * inputs, axis=0, keepdims=True)
    input_grad = middle_grad + scale1 * w1 - ins * (scale1 * scale1) * mean1
    acc_ref[1] += first_grad * ins
    acc_ref[2] += input_grad * (lowered - side)
    state_ref[...] = pltpu.roll((1.0 - mixing) * input_grad, shift, 1)
    grads_ref[:, 0:D] += dot((mixing * input_grad).astype(BF), bb)
    grads_ref[:, D : D + SFF] += dot(snt, expanded_grad, 1, 1)
    grads_ref[:, D + SFF : D + 2 * SFF] += dot(cotb, activated, 1, 1)
    low = D + 2 * SFF
    grads_ref[:, low : low + 3 * DS] += dot(fnt, dqkvt, 1, 1)
    grads_ref[:, low + 3 * DS : low + 4 * DS] += dot(ctxb, branch, 1, 1)

    @pl.when(r == pl.num_programs(0) - 1)
    def _():
        total = [jnp.sum(acc_ref[i], axis=1, keepdims=True) for i in range(3)]
        total[2] = total[2] * (mixing * (1.0 - mixing))[:, 0:1] * 10.0
        lane = lax.broadcasted_iota(jnp.int32, (DS, 128), 1)
        grads_ref[:, low + 4 * DS :] = jnp.where(lane == 0, total[0], jnp.where(lane == 1, total[1], jnp.where(lane == 2, total[2], 0.0)))


def whole(shape):
    return pl.BlockSpec(shape, lambda r, lens: (0,) * len(shape), pipeline_mode=pl.Buffered(1))


def params():
    return pltpu.CompilerParams(vmem_limit_bytes=VMEM_LIMIT, dimension_semantics=("arbitrary",))


def swap(x):
    return lax.ppermute(x, "tensor", [(0, 1), (1, 0)])


def sum_over(x, batch):
    t = lax.axis_index("tensor")
    h = x.shape[0] // 2
    x = x.astype(BF)
    mine = lax.dynamic_slice_in_dim(x, t * h, h, 0)
    other = lax.dynamic_slice_in_dim(x, (1 - t) * h, h, 0)
    part = mine.astype(F32) + swap(other).astype(F32)
    bit = 1
    while bit < batch:
        sent = part.astype(BF)
        got = lax.ppermute(sent, "batch", [(i, i ^ bit) for i in range(batch)])
        part = sent.astype(F32) + got.astype(F32)
        bit *= 2
    sent = part.astype(BF)
    got = swap(sent)
    return jnp.where(t == 0, jnp.concatenate([sent, got]), jnp.concatenate([got, sent])).astype(F32)


def make_body(batch):
    def body(
        hidden_in,
        lengths,
        attn_gain,
        attn_query,
        attn_key,
        attn_value,
        attn_out,
        ffn_gain,
        ffn_in,
        ffn_out,
        side_state,
        gate_alpha,
        down_w,
        side_attn_gain,
        side_query,
        side_key,
        side_value,
        side_proj,
        side_ffn_gain,
        side_expand,
        side_shrink,
        cotangent,
    ):
        tokens = hidden_in.shape[0]
        rows = tokens // ROW_LEN
        cols = attn_query.shape[1]
        units = ffn_in.shape[1]
        t = lax.axis_index("tensor")
        lens = lax.dynamic_slice_in_dim(lengths, t * rows, rows, 0).reshape(-1)
        far = [swap(w) for w in (attn_query, attn_key, attn_value, attn_out, ffn_in, ffn_out)]
        tile = pl.BlockSpec((ROW_LEN, D), lambda r, lens: (r, 0))
        scratch = [
            pltpu.VMEM((D, 3 * cols), BF),
            pltpu.VMEM((ROW_LEN, 3 * cols), BF),
            pltpu.VMEM((cols, ROW_LEN), BF),
            pltpu.VMEM((cols, ROW_LEN), BF),
            pltpu.VMEM((HALF, HALF), F32),
        ]
        attn_specs = [whole((D, cols))] * 3 + [whole((cols, D))]
        normed, mid = pl.pallas_call(
            first_kernel,
            grid_spec=pltpu.PrefetchScalarGridSpec(
                num_scalar_prefetch=1,
                grid=(rows,),
                in_specs=[tile, whole((1, D))] + attn_specs,
                out_specs=[tile, tile],
                scratch_shapes=scratch + [pltpu.VMEM((ROW_LEN, D), F32)],
            ),
            out_shape=[jax.ShapeDtypeStruct((tokens, D), BF), jax.ShapeDtypeStruct((tokens, D), F32)],
            compiler_params=params(),
            name="own_heads",
        )(lens, hidden_in, attn_gain.reshape(1, D), attn_query, attn_key, attn_value, attn_out)
        mid = pl.pallas_call(
            second_kernel,
            grid_spec=pltpu.PrefetchScalarGridSpec(
                num_scalar_prefetch=1,
                grid=(rows,),
                in_specs=[tile, tile] + attn_specs,
                out_specs=tile,
                scratch_shapes=scratch,
            ),
            out_shape=jax.ShapeDtypeStruct((tokens, D), F32),
            compiler_params=params(),
            name="far_heads",
        )(lens, normed, mid, *far[:4])
        vecs = jnp.zeros((8, 128), F32)
        vecs = vecs.at[0, :DS].set(gate_alpha).at[1, :DS].set(side_attn_gain).at[2, :DS].set(side_ffn_gain)
        side_tile = pl.BlockSpec((DS, ROW_LEN), lambda r, lens: (0, r))
        backbone, side_out, state_grad, grads = pl.pallas_call(
            third_kernel,
            grid_spec=pltpu.PrefetchScalarGridSpec(
                num_scalar_prefetch=1,
                grid=(rows,),
                in_specs=[
                    tile,
                    whole((1, D)),
                    whole((D, units)),
                    whole((D, units)),
                    whole((units, D)),
                    whole((units, D)),
                    side_tile,
                    side_tile,
                    whole((8, 128)),
                    whole((DS, D)),
                    whole((DS, DS)),
                    whole((DS, DS)),
                    whole((DS, DS)),
                    whole((DS, DS)),
                    whole((DS, SFF)),
                    whole((DS, SFF)),
                ],
                out_specs=[tile, side_tile, side_tile, pl.BlockSpec((DS, GRAD_LANES), lambda r, lens: (0, 0))],
                scratch_shapes=[
                    pltpu.VMEM((ROW_LEN, 2 * units), BF),
                    pltpu.VMEM((HALF, HALF), F32),
                    pltpu.VMEM((ROW_LEN, D), F32),
                    pltpu.VMEM((3, DS, ROW_LEN), F32),
                    pltpu.VMEM((3 * DS, DS), BF),
                    pltpu.VMEM((ROW_LEN, SIDE_HEADS * HALF), BF),
                    pltpu.VMEM((HALF, SIDE_HEADS * HALF), BF),
                    pltpu.VMEM((DS, ROW_LEN), F32),
                    pltpu.VMEM((DS, ROW_LEN), F32),
                    pltpu.VMEM((DS, ROW_LEN), F32),
                    pltpu.VMEM((2, SIDE_HEADS * HALF, DS), BF),
                    pltpu.VMEM((3, DS, ROW_LEN), F32),
                ],
            ),
            out_shape=[
                jax.ShapeDtypeStruct((tokens, D), BF),
                jax.ShapeDtypeStruct((DS, tokens), F32),
                jax.ShapeDtypeStruct((DS, tokens), F32),
                jax.ShapeDtypeStruct((DS, GRAD_LANES), F32),
            ],
            compiler_params=params(),
            name="forward_and_back",
        )(
            lens,
            mid,
            ffn_gain.reshape(1, D),
            ffn_in,
            far[4],
            ffn_out,
            far[5],
            side_state.T,
            cotangent.T,
            vecs,
            down_w.T,
            side_query,
            side_key,
            side_value,
            side_proj,
            side_expand,
            side_shrink.T,
        )
        g = sum_over(grads, batch)
        low = D + 2 * SFF
        return (
            backbone,
            side_out.T,
            state_grad.T,
            g[:, :D].T,
            g[:, low + 4 * DS + 2],
            g[:, low + 4 * DS + 1],
            g[:, low : low + DS],
            g[:, low + DS : low + 2 * DS],
            g[:, low + 2 * DS : low + 3 * DS],
            g[:, low + 3 * DS : low + 4 * DS],
            g[:, low + 4 * DS],
            g[:, D : D + SFF],
            g[:, D + SFF : low].T,
        )

    return body


def solution(mesh):
    split = P(("batch", "tensor"), None)
    return jax.shard_map(
        make_body(mesh.shape["batch"]),
        mesh=mesh,
        in_specs=(
            split,
            P("batch", None),
            P(),
            P(None, "tensor"),
            P(None, "tensor"),
            P(None, "tensor"),
            P("tensor", None),
            P(),
            P(None, "tensor"),
            P("tensor", None),
            split,
            P(),
            P(),
            P(),
            P(),
            P(),
            P(),
            P(),
            P(),
            P(),
            P(),
            split,
        ),
        out_specs=(split, split, split) + (P(),) * 10,
        check_vma=False,
    )
```

```python
import jax
import jax.numpy as jnp
from jax import lax
from jax.experimental import pallas as pl
from jax.experimental.pallas import tpu as pltpu
from jax.sharding import PartitionSpec as P

BF = jnp.bfloat16
F32 = jnp.float32
D = 768
HEAD_DIM = 64
DS = 96
SIDE_HEADS = 12
SIDE_HEAD_DIM = 8
SFF = 384
ROW_LEN = 512
SEGS = 8
HALF = 256
GRAD_LANES = 2048
LOG2E = 1.4426950408889634
EPS = 1e-06


def dot(a, b, ca=1, cb=0):
    return lax.dot_general(a, b, (((ca,), (cb,)), ((), ())), preferred_element_type=F32)


def gelu(x):
    x2 = x * x
    u = x * (x2 * (0.7978845608028654 * 0.044715) + 0.7978845608028654)
    h = 0.5 * x
    return h + h * jnp.tanh(u)


def gelu_and_slope(x):
    x2 = x * x
    u = x * (x2 * (0.7978845608028654 * 0.044715) + 0.7978845608028654)
    t = jnp.tanh(u)
    h = 0.5 * x
    du = 0.7978845608028654 * 3.0 * 0.044715 * x2 + 0.7978845608028654
    return h + h * t, 0.5 + 0.5 * t + h * (1.0 - t * t) * du


def row_starts(first_ref, lens_ref, r):
    starts, begin = [], jnp.int32(0)
    long_start = jnp.int32(0)
    for j in range(SEGS):
        n = lens_ref[j, first_ref[0] + r]
        starts.append((begin, n))
        long_start = jnp.where(n == HALF, begin, long_start)
        begin = begin + n
    return long_start, [((b - long_start) & (ROW_LEN - 1), n) for b, n in starts]


def fill_bias(bias_ref, docs):
    q = lax.broadcasted_iota(jnp.int32, (1, HALF), 1) + HALF
    low = jnp.zeros((1, HALF), jnp.int32)
    high = jnp.zeros((1, HALF), jnp.int32)
    for b, n in docs:
        inside = (q >= b) & (q < b + n)
        low = jnp.where(inside, b, low)
        high = jnp.where(inside, b + n, high)
    k = lax.broadcasted_iota(jnp.int32, (HALF, HALF), 0) + HALF
    bias_ref[...] = jnp.where((k >= low) & (k < high), 0.0, -1e30)


def turn_rows(src_ref, shift):
    n = src_ref.shape[1]
    part = shift & 7
    first = lax.shift_right_logical(shift, 3)
    groups = []
    for g in range(ROW_LEN // 8 + 1):
        start = pl.multiple_of(((first + g) & (ROW_LEN // 8 - 1)) * 8, 8)
        groups.append(src_ref[pl.ds(start, 8), :])
    wide = jnp.concatenate(groups, axis=0).reshape(ROW_LEN // 8 + 1, 8, n)
    back = (8 - part) & 7
    wide = pltpu.roll(wide, back, 1)
    place = lax.broadcasted_iota(jnp.int32, (ROW_LEN // 8, 8, n), 1)
    turned = jnp.where(place < 8 - part, wide[:-1], wide[1:])
    return turned.reshape(ROW_LEN, n)


def exponentials(s, half, bias_ref, safe):
    if half:
        s = s + bias_ref[...]
    if safe:
        s = s - jnp.max(s, axis=0, keepdims=True)
    e = jnp.exp2(s)
    return e.astype(BF), jnp.sum(e, axis=0, keepdims=True)


def out_of_range(sums):
    low, high = sums[0], sums[0]
    for one in sums[1:]:
        low, high = jnp.minimum(low, one), jnp.maximum(high, one)
    fine = (jnp.min(low) > 1e-20) & (jnp.max(high) < 1e20)
    return jnp.logical_not(fine)


def frozen_attention(qkv_ref, vt_ref, e_ref, ctxt_ref, bias_ref, safe):
    cols = qkv_ref.shape[1] // 3
    lane = lax.broadcasted_iota(jnp.int32, (1, 128), 1)
    keep = [(lane < 64).astype(F32).astype(BF), (lane >= 64).astype(F32).astype(BF)]
    blocks = [(half, p, j) for half in range(2) for p in range(cols // 128) for j in range(2)]
    sums = []
    for n, (half, p, j) in enumerate(blocks):
        rows = slice(half * HALF, (half + 1) * HALF)
        q2 = qkv_ref[rows, p * 128 : (p + 1) * 128]
        k2 = qkv_ref[rows, cols + p * 128 : cols + (p + 1) * 128]
        s = dot(k2 * keep[j], q2, 1, 1) * (LOG2E / 8.0)
        e_ref[n], total = exponentials(s, half, bias_ref, safe)
        sums.append(total)
    for n, (half, p, j) in enumerate(blocks):
        rows = slice(half * HALF, (half + 1) * HALF)
        head = slice(p * 128 + j * 64, p * 128 + (j + 1) * 64)
        ctxt_ref[head, rows] = (dot(vt_ref[head, rows], e_ref[n]) * (1.0 / sums[n])).astype(BF)
    return sums


def add_heads(mid_ref, wo_ref, qkv_ref, vt_ref, e_ref, ctxt_ref, bias_ref):
    sums = frozen_attention(qkv_ref, vt_ref, e_ref, ctxt_ref, bias_ref, False)
    bad = out_of_range(sums)

    @pl.when(bad)
    def _():
        frozen_attention(qkv_ref, vt_ref, e_ref, ctxt_ref, bias_ref, True)

    mid_ref[...] += dot(ctxt_ref[...].T, wo_ref[...])


def join_weights(wqkv_ref, parts):
    cols = parts[0].shape[1]
    for i, part in enumerate(parts):
        wqkv_ref[:, i * cols : (i + 1) * cols] = part[...]


def turn_and_norm(first_ref, lens_ref, r, x_ref, gain_ref, raw_ref, xf_ref, normed_ref):
    shift, _ = row_starts(first_ref, lens_ref, r)
    raw_ref[...] = x_ref[...].astype(F32)
    x = turn_rows(raw_ref, shift)
    xf_ref[...] = x
    normed_ref[...] = (x * lax.rsqrt(jnp.mean(x * x, axis=1, keepdims=True) + EPS) * gain_ref[...].reshape(1, D)).astype(BF)


def first_kernel(first_ref, lens_ref, x_ref, next_ref, gain_ref, wq_ref, wk_ref, wv_ref, wo_ref, normed_ref, mid_ref, wqkv_ref, qkv_ref, vt_ref, e_ref, ctxt_ref, bias_ref, raw_ref, xf_ref, nb_ref):
    r = pl.program_id(0)
    rows = pl.num_programs(0)

    @pl.when(r == 0)
    def _():
        join_weights(wqkv_ref, (wq_ref, wk_ref, wv_ref))
        turn_and_norm(first_ref, lens_ref, 0, x_ref, gain_ref, raw_ref, xf_ref, nb_ref)

    _, docs = row_starts(first_ref, lens_ref, r)
    fill_bias(bias_ref, docs)
    mid_ref[...] = xf_ref[...]
    normed_ref[...] = nb_ref[...]
    qkv_ref[...] = dot(nb_ref[...], wqkv_ref[...]).astype(BF)
    vt_ref[...] = qkv_ref[:, 2 * wq_ref.shape[1] :].T
    turn_and_norm(first_ref, lens_ref, jnp.minimum(r + 1, rows - 1), next_ref, gain_ref, raw_ref, xf_ref, nb_ref)
    add_heads(mid_ref, wo_ref, qkv_ref, vt_ref, e_ref, ctxt_ref, bias_ref)


def second_kernel(first_ref, lens_ref, normed_ref, part_ref, wq_ref, wk_ref, wv_ref, wo_ref, mid_ref, wqkv_ref, qkv_ref, vt_ref, e_ref, ctxt_ref, bias_ref):
    r = pl.program_id(0)

    @pl.when(r == 0)
    def _():
        join_weights(wqkv_ref, (wq_ref, wk_ref, wv_ref))

    _, docs = row_starts(first_ref, lens_ref, r)
    fill_bias(bias_ref, docs)
    mid_ref[...] = part_ref[...]
    qkv_ref[...] = dot(normed_ref[...], wqkv_ref[...]).astype(BF)
    vt_ref[...] = qkv_ref[:, 2 * wq_ref.shape[1] :].T
    add_heads(mid_ref, wo_ref, qkv_ref, vt_ref, e_ref, ctxt_ref, bias_ref)


def side_blocks():
    return [(half, h) for half in range(2) for h in range(SIDE_HEADS)]


def head_rows(product, h):
    low = SIDE_HEAD_DIM * (h % 2)
    return product[low : low + SIDE_HEAD_DIM]


def pair(h):
    return slice(2 * SIDE_HEAD_DIM * (h // 2), 2 * SIDE_HEAD_DIM * (h // 2 + 1))


def side_forward(k, qt, vt, masks, bias_ref, e_ref, inv_ref, ctxt_ref, safe):
    sums = []
    for n, (half, h) in enumerate(side_blocks()):
        rows = slice(half * HALF, (half + 1) * HALF)
        s = dot(k[rows] * masks[h], qt[:, rows]) * (LOG2E * SIDE_HEAD_DIM**-0.5)
        e_ref[n], total = exponentials(s, half, bias_ref, safe)
        sums.append(total)
    for n, (half, h) in enumerate(side_blocks()):
        rows = slice(half * HALF, (half + 1) * HALF)
        own = slice(SIDE_HEAD_DIM * h, SIDE_HEAD_DIM * (h + 1))
        inv = 1.0 / sums[n]
        ctxt_ref[own, rows] = head_rows(dot(vt[pair(h), rows], e_ref[n]), h) * inv
        inv_ref[own, rows] = jnp.broadcast_to(inv, (SIDE_HEAD_DIM, HALF))
    return sums


def third_kernel(
    first_ref,
    lens_ref,
    mid_ref,
    fgain_ref,
    w1a_ref,
    w1b_ref,
    w2a_ref,
    w2b_ref,
    side_ref,
    cot_ref,
    alpha_ref,
    gain1_ref,
    gain2_ref,
    downt_ref,
    sq_ref,
    sk_ref,
    sv_ref,
    proj_ref,
    expand_ref,
    shrinkt_ref,
    bb_ref,
    out_ref,
    state_ref,
    mine_ref,
    other_ref,
    grads_ref,
    hid_ref,
    bias_ref,
    f_ref,
    cols_ref,
    wqkvt_ref,
    e_ref,
    et_ref,
    ds_ref,
    dst_ref,
    inv_ref,
    ctxt_ref,
    qkvt_ref,
    dq_ref,
    acc_ref,
):
    r = pl.program_id(0)

    @pl.when(r == 0)
    def _():
        grads_ref[...] = jnp.zeros_like(grads_ref)
        acc_ref[...] = jnp.zeros_like(acc_ref)
        for i, ref in enumerate((alpha_ref, gain1_ref, gain2_ref)):
            cols_ref[i] = jnp.broadcast_to(jnp.broadcast_to(ref[...].reshape(1, DS), (8, DS)).T[:, 0:1], (DS, ROW_LEN))
        wqkvt_ref[:DS] = sq_ref[...].T
        wqkvt_ref[DS : 2 * DS] = sk_ref[...].T
        wqkvt_ref[2 * DS :] = sv_ref[...].T

    shift, docs = row_starts(first_ref, lens_ref, r)
    fill_bias(bias_ref, docs)

    middle = mid_ref[...]
    normed = (middle * lax.rsqrt(jnp.mean(middle * middle, axis=1, keepdims=True) + EPS) * fgain_ref[...].reshape(1, D)).astype(BF)
    units = w1a_ref.shape[1]
    for i, w in enumerate((w1a_ref, w1b_ref)):
        for c in range(units // 256):
            hid_ref[:, i * units + c * 256 : i * units + (c + 1) * 256] = gelu(dot(normed, w[:, c * 256 : (c + 1) * 256])).astype(BF)
    f_ref[...] = mid_ref[...] + dot(hid_ref[:, :units], w2a_ref[...]) + dot(hid_ref[:, units:], w2b_ref[...])
    bb = f_ref[...].astype(BF)
    bb_ref[...] = turn_rows(f_ref, (ROW_LEN - shift) & (ROW_LEN - 1)).astype(BF)

    alpha = cols_ref[0]
    gain1 = cols_ref[1]
    gain2 = cols_ref[2]
    mixing = 1.0 / (1.0 + jnp.exp(alpha * -10.0))
    forward = (ROW_LEN - shift) & (ROW_LEN - 1)
    side = pltpu.roll(side_ref[...].astype(F32), forward, 1)
    cot = pltpu.roll(cot_ref[...].astype(F32), forward, 1)
    cotb = cot.astype(BF)
    lowered = dot(downt_ref[...], bb, 1, 1)
    inputs = mixing * lowered + (1.0 - mixing) * side
    scale1 = lax.rsqrt(jnp.mean(inputs * inputs, axis=0, keepdims=True) + EPS)
    fnt = (inputs * scale1 * gain1).astype(BF)
    qkvt_ref[...] = dot(wqkvt_ref[...], fnt).astype(BF)
    qt, kt, vt = qkvt_ref[:DS], qkvt_ref[DS : 2 * DS], qkvt_ref[2 * DS :]
    lane = lax.broadcasted_iota(jnp.int32, (1, DS), 1)
    masks = [((lane >= 8 * h) & (lane < 8 * h + 8)).astype(F32).astype(BF) for h in range(SIDE_HEADS)]
    lane2 = lax.broadcasted_iota(jnp.int32, (1, 128), 1)
    masks2 = [
        (((lane2 >= 8 * h) & (lane2 < 8 * h + 8)) | (lane2 == DS + h) | (lane2 == DS + 16 + h)).astype(F32).astype(BF)
        for h in range(SIDE_HEADS)
    ]
    k, v = kt.T, vt.T
    sums = side_forward(k, qt, vt, masks, bias_ref, e_ref, inv_ref, ctxt_ref, False)
    bad = out_of_range(sums)

    @pl.when(bad)
    def _():
        qt, kt, vt = qkvt_ref[:DS], qkvt_ref[DS : 2 * DS], qkvt_ref[2 * DS :]
        side_forward(kt.T, qt, vt, masks, bias_ref, e_ref, inv_ref, ctxt_ref, True)

    ctx = ctxt_ref[...]
    ctxb = ctx.astype(BF)
    middle_side = inputs + dot(proj_ref[...], ctxb, 0, 0)
    scale2 = lax.rsqrt(jnp.mean(middle_side * middle_side, axis=0, keepdims=True) + EPS)
    snt = (middle_side * scale2 * gain2).astype(BF)
    expanded = dot(expand_ref[...], snt, 0, 0)
    activated, slope = gelu_and_slope(expanded)
    activated = activated.astype(BF)
    side_out = middle_side + dot(shrinkt_ref[...], activated)
    out_ref[...] = pltpu.roll(side_out, shift, 1)

    activated_grad = dot(shrinkt_ref[...], cotb, 0, 0)
    expanded_grad = (activated_grad * slope).astype(BF)
    second_grad = dot(expand_ref[...], expanded_grad)
    w2 = second_grad * gain2
    ms = middle_side * scale2
    mean2 = jnp.mean(w2 * middle_side, axis=0, keepdims=True)
    middle_grad = cot + scale2 * w2 - ms * (scale2 * scale2) * mean2
    acc_ref[0] += second_grad * ms
    branch = middle_grad.astype(BF)
    context_grad = dot(proj_ref[...], branch).astype(BF).astype(F32)
    dop = (context_grad * inv_ref[...]).astype(BF)
    centre = jnp.sum((dop.astype(F32) * ctx).reshape(SIDE_HEADS, 8, ROW_LEN), axis=1)
    centre = jnp.concatenate([centre, jnp.zeros((4, ROW_LEN), F32)], axis=0)
    chigh = centre.astype(BF)
    clow = (centre - chigh.astype(F32)).astype(BF)
    dstack = jnp.concatenate([dop, -chigh, -clow], axis=0)
    vones = jnp.concatenate([v, jnp.ones((ROW_LEN, 32), BF)], axis=1)
    for n, (half, h) in enumerate(side_blocks()):
        rows = slice(half * HALF, (half + 1) * HALF)
        dp = dot(vones[rows] * masks2[h], dstack[:, rows])
        ds_ref[n] = (e_ref[n].astype(F32) * dp).astype(BF)
        et_ref[n] = e_ref[n].T
    for n, (half, h) in enumerate(side_blocks()):
        rows = slice(half * HALF, (half + 1) * HALF)
        dq_ref[8 * h : 8 * h + 8, rows] = head_rows(dot(kt[pair(h), rows], ds_ref[n]), h) * SIDE_HEAD_DIM**-0.5
        dst_ref[n] = ds_ref[n].T
    for n, (half, h) in enumerate(side_blocks()):
        rows = slice(half * HALF, (half + 1) * HALF)
        low = 2 * DS + 8 * h
        dq_ref[low : low + 8, rows] = head_rows(dot(dop[pair(h), rows], et_ref[n]), h)
    for n, (half, h) in enumerate(side_blocks()):
        rows = slice(half * HALF, (half + 1) * HALF)
        low = DS + 8 * h
        dq_ref[low : low + 8, rows] = head_rows(dot(qt[pair(h), rows], dst_ref[n]), h) * SIDE_HEAD_DIM**-0.5
    dqkvt = dq_ref[...].astype(BF)
    first_grad = dot(wqkvt_ref[...], dqkvt, 0, 0)
    w1 = first_grad * gain1
    ins = inputs * scale1
    mean1 = jnp.mean(w1 * inputs, axis=0, keepdims=True)
    input_grad = middle_grad + scale1 * w1 - ins * (scale1 * scale1) * mean1
    acc_ref[1] += first_grad * ins
    acc_ref[2] += input_grad * (lowered - side)
    state_ref[...] = pltpu.roll((1.0 - mixing) * input_grad, shift, 1)
    grads_ref[:, 0:D] += dot((mixing * input_grad).astype(BF), bb)
    grads_ref[:, D : D + SFF] += dot(snt, expanded_grad, 1, 1)
    grads_ref[:, D + SFF : D + 2 * SFF] += dot(cotb, activated, 1, 1)
    low = D + 2 * SFF
    grads_ref[:, low : low + 3 * DS] += dot(fnt, dqkvt, 1, 1)
    grads_ref[:, low + 3 * DS : low + 4 * DS] += dot(ctxb, branch, 1, 1)

    @pl.when(r == pl.num_programs(0) - 1)
    def _():
        total = [jnp.sum(acc_ref[i], axis=1, keepdims=True) for i in range(3)]
        total[2] = total[2] * (mixing * (1.0 - mixing))[:, 0:1] * 10.0
        lane = lax.broadcasted_iota(jnp.int32, (DS, 128), 1)
        grads_ref[:, low + 4 * DS :] = jnp.where(lane == 0, total[0], jnp.where(lane == 1, total[1], jnp.where(lane == 2, total[2], 0.0)))
        half = DS // 2
        tensor = (first_ref[0] != 0).astype(jnp.int32)
        mine_ref[...] = grads_ref[pl.ds(pl.multiple_of(tensor * half, 8), half), :].astype(BF)
        other_ref[...] = grads_ref[pl.ds(pl.multiple_of((1 - tensor) * half, 8), half), :].astype(BF)


def whole(shape):
    return pl.BlockSpec(shape, lambda r, *_: (0,) * len(shape), pipeline_mode=pl.Buffered(1))


def params(limit):
    return pltpu.CompilerParams(vmem_limit_bytes=limit * 1024 * 1024, dimension_semantics=("arbitrary",))


def swap(x):
    return lax.ppermute(x, "tensor", [(0, 1), (1, 0)])


def sum_over(mine, other, batch):
    def trade(x, bit):
        return lax.ppermute(x, "batch", [(i, i ^ bit) for i in range(batch)])

    place = lax.axis_index("batch")
    part = mine.astype(F32) + swap(other).astype(F32)
    bits = [1 << i for i in range(batch.bit_length() - 1)]
    split = bits[:2]
    for bit in split:
        low, high = jnp.split(part.astype(BF), 2, axis=1)
        upper = (place & bit) != 0
        got = trade(jnp.where(upper, low, high), bit)
        part = jnp.where(upper, high, low).astype(F32) + got.astype(F32)
    for bit in bits[2:]:
        sent = part.astype(BF)
        part = sent.astype(F32) + trade(sent, bit).astype(F32)
    sent = part.astype(BF)
    for bit in reversed(split):
        got = trade(sent, bit)
        upper = (place & bit) != 0
        sent = jnp.concatenate([jnp.where(upper, got, sent), jnp.where(upper, sent, got)], axis=1)
    got = swap(sent)
    upper = lax.axis_index("tensor") != 0
    return jnp.concatenate([jnp.where(upper, got, sent), jnp.where(upper, sent, got)], axis=0).astype(F32)


def make_body(batch):
    def body(
        hidden_in,
        lengths,
        attn_gain,
        attn_query,
        attn_key,
        attn_value,
        attn_out,
        ffn_gain,
        ffn_in,
        ffn_out,
        side_state,
        gate_alpha,
        down_w,
        side_attn_gain,
        side_query,
        side_key,
        side_value,
        side_proj,
        side_ffn_gain,
        side_expand,
        side_shrink,
        cotangent,
    ):
        tokens = hidden_in.shape[0]
        rows = tokens // ROW_LEN
        cols = attn_query.shape[1]
        units = ffn_in.shape[1]
        t = lax.axis_index("tensor")
        first = (t * rows).astype(jnp.int32).reshape(1)
        far = [swap(w) for w in (attn_query, attn_key, attn_value, attn_out, ffn_in, ffn_out)]
        tile = pl.BlockSpec((ROW_LEN, D), lambda r, *_: (r, 0))
        scratch = [
            pltpu.VMEM((D, 3 * cols), BF),
            pltpu.VMEM((ROW_LEN, 3 * cols), BF),
            pltpu.VMEM((cols, ROW_LEN), BF),
            pltpu.VMEM((2 * cols // HEAD_DIM, HALF, HALF), BF),
            pltpu.VMEM((cols, ROW_LEN), BF),
            pltpu.VMEM((HALF, HALF), F32),
        ]
        attn_specs = [whole((D, cols))] * 3 + [whole((cols, D))]
        normed, mid = pl.pallas_call(
            first_kernel,
            grid_spec=pltpu.PrefetchScalarGridSpec(
                num_scalar_prefetch=2,
                grid=(rows,),
                in_specs=[
                    whole((ROW_LEN, D)),
                    pl.BlockSpec((ROW_LEN, D), lambda r, *_: (jnp.minimum(r + 1, rows - 1), 0)),
                    whole((D,)),
                ]
                + attn_specs,
                out_specs=[tile, tile],
                scratch_shapes=scratch + [pltpu.VMEM((ROW_LEN, D), F32)] * 2 + [pltpu.VMEM((ROW_LEN, D), BF)],
            ),
            out_shape=[jax.ShapeDtypeStruct((tokens, D), BF), jax.ShapeDtypeStruct((tokens, D), F32)],
            compiler_params=params(60),
            name="own_heads",
        )(first, lengths.T, hidden_in, hidden_in, attn_gain, attn_query, attn_key, attn_value, attn_out)
        mid = pl.pallas_call(
            second_kernel,
            grid_spec=pltpu.PrefetchScalarGridSpec(
                num_scalar_prefetch=2,
                grid=(rows,),
                in_specs=[tile, tile] + attn_specs,
                out_specs=tile,
                scratch_shapes=scratch,
            ),
            out_shape=jax.ShapeDtypeStruct((tokens, D), F32),
            compiler_params=params(60),
            name="far_heads",
        )(first, lengths.T, normed, mid, *far[:4])
        side_tile = pl.BlockSpec((DS, ROW_LEN), lambda r, *_: (0, r))
        backbone, side_out, state_grad, mine, other = pl.pallas_call(
            third_kernel,
            grid_spec=pltpu.PrefetchScalarGridSpec(
                num_scalar_prefetch=2,
                grid=(rows,),
                in_specs=[
                    tile,
                    whole((D,)),
                    whole((D, units)),
                    whole((D, units)),
                    whole((units, D)),
                    whole((units, D)),
                    side_tile,
                    side_tile,
                    whole((DS,)),
                    whole((DS,)),
                    whole((DS,)),
                    whole((DS, D)),
                    whole((DS, DS)),
                    whole((DS, DS)),
                    whole((DS, DS)),
                    whole((DS, DS)),
                    whole((DS, SFF)),
                    whole((DS, SFF)),
                ],
                out_specs=[tile, side_tile, side_tile] + [pl.BlockSpec((DS // 2, GRAD_LANES), lambda r, *_: (0, 0))] * 2,
                scratch_shapes=[
                    pltpu.VMEM((DS, GRAD_LANES), F32),
                    pltpu.VMEM((ROW_LEN, 2 * units), BF),
                    pltpu.VMEM((HALF, HALF), F32),
                    pltpu.VMEM((ROW_LEN, D), F32),
                    pltpu.VMEM((3, DS, ROW_LEN), F32),
                    pltpu.VMEM((3 * DS, DS), BF),
                    pltpu.VMEM((2 * SIDE_HEADS, HALF, HALF), BF),
                    pltpu.VMEM((2 * SIDE_HEADS, HALF, HALF), BF),
                    pltpu.VMEM((2 * SIDE_HEADS, HALF, HALF), BF),
                    pltpu.VMEM((2 * SIDE_HEADS, HALF, HALF), BF),
                    pltpu.VMEM((DS, ROW_LEN), F32),
                    pltpu.VMEM((DS, ROW_LEN), F32),
                    pltpu.VMEM((3 * DS, ROW_LEN), BF),
                    pltpu.VMEM((3 * DS, ROW_LEN), F32),
                    pltpu.VMEM((3, DS, ROW_LEN), F32),
                ],
            ),
            out_shape=[
                jax.ShapeDtypeStruct((tokens, D), BF),
                jax.ShapeDtypeStruct((DS, tokens), F32),
                jax.ShapeDtypeStruct((DS, tokens), F32),
                jax.ShapeDtypeStruct((DS // 2, GRAD_LANES), BF),
                jax.ShapeDtypeStruct((DS // 2, GRAD_LANES), BF),
            ],
            compiler_params=params(60),
            name="forward_and_back",
        )(
            first,
            lengths.T,
            mid,
            ffn_gain,
            ffn_in,
            far[4],
            ffn_out,
            far[5],
            side_state.T,
            cotangent.T,
            gate_alpha,
            side_attn_gain,
            side_ffn_gain,
            down_w.T,
            side_query,
            side_key,
            side_value,
            side_proj,
            side_expand,
            side_shrink.T,
        )
        g = sum_over(mine, other, batch)
        low = D + 2 * SFF
        return (
            backbone,
            side_out.T,
            state_grad.T,
            g[:, :D].T,
            g[:, low + 4 * DS + 2],
            g[:, low + 4 * DS + 1],
            g[:, low : low + DS],
            g[:, low + DS : low + 2 * DS],
            g[:, low + 2 * DS : low + 3 * DS],
            g[:, low + 3 * DS : low + 4 * DS],
            g[:, low + 4 * DS],
            g[:, D : D + SFF],
            g[:, D + SFF : low].T,
        )

    return body


def solution(mesh):
    split = P(("batch", "tensor"), None)
    return jax.shard_map(
        make_body(mesh.shape["batch"]),
        mesh=mesh,
        in_specs=(
            split,
            P("batch", None),
            P(),
            P(None, "tensor"),
            P(None, "tensor"),
            P(None, "tensor"),
            P("tensor", None),
            P(),
            P(None, "tensor"),
            P("tensor", None),
            split,
            P(),
            P(),
            P(),
            P(),
            P(),
            P(),
            P(),
            P(),
            P(),
            P(),
            split,
        ),
        out_specs=(split, split, split) + (P(),) * 10,
        check_vma=False,
    )
```

```python
import jax
import jax.numpy as jnp
from jax import lax
from jax.experimental import pallas as pl
from jax.experimental.pallas import tpu as pltpu
from jax.sharding import PartitionSpec as P

BF = jnp.bfloat16
F32 = jnp.float32
D = 768
HEADS = 12
HEAD_DIM = 64
DS = 96
SIDE_HEADS = 12
SIDE_HEAD_DIM = 8
SFF = 384
ROW_LEN = 512
SEGS = 8
HALF = 256
GRAD_LANES = 2048
LOG2E = 1.4426950408889634
EPS = 1e-06


def dot(a, b, ca=1, cb=0):
    return lax.dot_general(a, b, (((ca,), (cb,)), ((), ())), preferred_element_type=F32)


def gelu(x):
    x2 = x * x
    u = x * (x2 * (0.7978845608028654 * 0.044715) + 0.7978845608028654)
    h = 0.5 * x
    return h + h * jnp.tanh(u)


def gelu_and_slope(x):
    x2 = x * x
    u = x * (x2 * (0.7978845608028654 * 0.044715) + 0.7978845608028654)
    t = jnp.tanh(u)
    h = 0.5 * x
    du = 0.7978845608028654 * 3.0 * 0.044715 * x2 + 0.7978845608028654
    return h + h * t, 0.5 + 0.5 * t + h * (1.0 - t * t) * du


def row_starts(first_ref, lens_ref, r):
    starts, begin = [], jnp.int32(0)
    long_start = jnp.int32(0)
    for j in range(SEGS):
        n = lens_ref[j, first_ref[0] + r]
        starts.append((begin, n))
        long_start = jnp.where(n == HALF, begin, long_start)
        begin = begin + n
    return long_start, [((b - long_start) & (ROW_LEN - 1), n) for b, n in starts]


def fill_bias(bias_ref, docs):
    q = lax.broadcasted_iota(jnp.int32, (1, HALF), 1) + HALF
    low = jnp.zeros((1, HALF), jnp.int32)
    high = jnp.zeros((1, HALF), jnp.int32)
    for b, n in docs:
        inside = (q >= b) & (q < b + n)
        low = jnp.where(inside, b, low)
        high = jnp.where(inside, b + n, high)
    k = lax.broadcasted_iota(jnp.int32, (HALF, HALF), 0) + HALF
    bias_ref[...] = jnp.where((k >= low) & (k < high), 0.0, -1e30)


def turn_rows(src_ref, shift):
    n = src_ref.shape[1]
    part = shift & 7
    first = lax.shift_right_logical(shift, 3)
    groups = []
    for g in range(ROW_LEN // 8 + 1):
        start = pl.multiple_of(((first + g) & (ROW_LEN // 8 - 1)) * 8, 8)
        groups.append(src_ref[pl.ds(start, 8), :])
    wide = jnp.concatenate(groups, axis=0).reshape(ROW_LEN // 8 + 1, 8, n)
    back = (8 - part) & 7
    wide = pltpu.roll(wide, back, 1)
    place = lax.broadcasted_iota(jnp.int32, (ROW_LEN // 8, 8, n), 1)
    turned = jnp.where(place < 8 - part, wide[:-1], wide[1:])
    return turned.reshape(ROW_LEN, n)


def exponentials(s, half, bias_ref, safe):
    if half:
        s = s + bias_ref[...]
    if safe:
        s = s - jnp.max(s, axis=0, keepdims=True)
    e = jnp.exp2(s)
    return e.astype(BF), jnp.sum(e, axis=0, keepdims=True)


def out_of_range(sums):
    low, high = sums[0], sums[0]
    for one in sums[1:]:
        low, high = jnp.minimum(low, one), jnp.maximum(high, one)
    fine = (jnp.min(low) > 1e-20) & (jnp.max(high) < 1e20)
    return jnp.logical_not(fine)


def at(start, size, step):
    return pl.ds(start if isinstance(start, int) else pl.multiple_of(start, step), size)


def frozen_scores(half, h, qkv_ref, e_ref, bias_ref, safe):
    p, j = h // 2, h % 2
    lane = lax.broadcasted_iota(jnp.int32, (1, 128), 1)
    keep = (lane >= 64 * j) & (lane < 64 * (j + 1))
    rows = slice(half * HALF, (half + 1) * HALF)
    q2 = qkv_ref[rows, at(p * 128, 128, 128)]
    k2 = qkv_ref[rows, at(D + p * 128, 128, 128)]
    s = dot(k2 * keep.astype(F32).astype(BF), q2, 1, 1) * (LOG2E / 8.0)
    e_ref[half * HEADS + h], total = exponentials(s, half, bias_ref, safe)
    return total


def frozen_values(half, h, vt_ref, e_ref, ctxt_ref, total):
    rows = slice(half * HALF, (half + 1) * HALF)
    head = at(h * HEAD_DIM, HEAD_DIM, HEAD_DIM)
    ctxt_ref[head, rows] = (dot(vt_ref[head, rows], e_ref[half * HEADS + h]) * (1.0 / total)).astype(BF)


def start_copies(pairs, sems):
    for i, (src, dst) in enumerate(pairs):
        pltpu.make_async_copy(src, dst, sems.at[i]).start()


def wait_copies(pairs, sems, first, last):
    for i in range(first, last):
        src, dst = pairs[i]
        pltpu.make_async_copy(src, dst, sems.at[i]).wait()


def turn_kernel(first_ref, lens_ref, x_ref, gain_ref, turned_ref, normed_ref, raw_ref):
    shift, _ = row_starts(first_ref, lens_ref, pl.program_id(0))
    raw_ref[...] = x_ref[...].astype(F32)
    x = turn_rows(raw_ref, shift)
    turned_ref[...] = x.astype(BF)
    normed_ref[...] = (x * lax.rsqrt(jnp.mean(x * x, axis=1, keepdims=True) + EPS) * gain_ref[...].reshape(1, D)).astype(BF)


def attention_kernel(
    first_ref,
    lens_ref,
    turned_ref,
    normed_ref,
    wqa_ref,
    wqb_ref,
    wka_ref,
    wkb_ref,
    wva_ref,
    wvb_ref,
    woa_ref,
    wob_ref,
    mid_ref,
    wqkv_ref,
    wo_ref,
    qkv_ref,
    vt_ref,
    e_ref,
    ctxt_ref,
    bias_ref,
    sems,
):
    r = pl.program_id(0)
    cols = woa_ref.shape[0]
    copies = [(w, wqkv_ref.at[:, i * cols : (i + 1) * cols]) for i, w in enumerate((wqa_ref, wqb_ref, wka_ref, wkb_ref, wva_ref, wvb_ref))]
    copies += [(woa_ref, wo_ref.at[:cols]), (wob_ref, wo_ref.at[cols:])]

    @pl.when(r == 0)
    def _():
        start_copies(copies, sems)
        wait_copies(copies, sems, 0, 8)

    _, docs = row_starts(first_ref, lens_ref, r)
    fill_bias(bias_ref, docs)
    qkv_ref[...] = dot(normed_ref[...], wqkv_ref[...]).astype(BF)
    vt_ref[...] = qkv_ref[:, 2 * D :].T
    blocks = [(half, h) for half in range(2) for h in range(HEADS)]
    sums = [frozen_scores(half, h, qkv_ref, e_ref, bias_ref, False) for half, h in blocks]
    for (half, h), total in zip(blocks, sums):
        frozen_values(half, h, vt_ref, e_ref, ctxt_ref, total)

    @pl.when(out_of_range(sums))
    def _():
        for half in range(2):

            def again(h, carry):
                frozen_values(half, h, vt_ref, e_ref, ctxt_ref, frozen_scores(half, h, qkv_ref, e_ref, bias_ref, True))
                return carry

            lax.fori_loop(0, HEADS, again, 0)

    mid_ref[...] = turned_ref[...].astype(F32) + dot(ctxt_ref[...].T, wo_ref[...])


def head_mask(h, width):
    lane = lax.broadcasted_iota(jnp.int32, (1, width), 1)
    own = (lane >= 8 * h) & (lane < 8 * h + 8)
    if width > DS:
        own = own | (lane == DS + h) | (lane == DS + 16 + h)
    return own.astype(F32).astype(BF)


def head_rows(product, h):
    low, high = product[:SIDE_HEAD_DIM], product[SIDE_HEAD_DIM:]
    if isinstance(h, int):
        return high if h % 2 else low
    return jnp.where(h % 2 == 1, high, low)


def pair(base, h):
    return at(base + 16 * (h // 2), 16, 16)


def own_rows(h, base=0):
    return at(base + SIDE_HEAD_DIM * h, SIDE_HEAD_DIM, SIDE_HEAD_DIM)


def side_scores(half, h, k, qkvt_ref, e_ref, bias_ref, safe):
    rows = slice(half * HALF, (half + 1) * HALF)
    s = dot(k[rows] * head_mask(h, DS), qkvt_ref[:DS, rows]) * (LOG2E * SIDE_HEAD_DIM**-0.5)
    e_ref[half * SIDE_HEADS + h], total = exponentials(s, half, bias_ref, safe)
    return total


def side_values(half, h, qkvt_ref, e_ref, ctxt_ref, inv_ref, total):
    rows = slice(half * HALF, (half + 1) * HALF)
    inv = 1.0 / total
    mixed = dot(qkvt_ref[pair(2 * DS, h), rows], e_ref[half * SIDE_HEADS + h])
    ctxt_ref[own_rows(h), rows] = head_rows(mixed, h) * inv
    inv_ref[own_rows(h), rows] = jnp.broadcast_to(inv, (SIDE_HEAD_DIM, HALF))


def side_kernel(
    first_ref,
    lens_ref,
    mid_ref,
    w1a_ref,
    w1b_ref,
    w2a_ref,
    w2b_ref,
    fgain_ref,
    side_ref,
    cot_ref,
    alpha_ref,
    gain1_ref,
    gain2_ref,
    downt_ref,
    sq_ref,
    sk_ref,
    sv_ref,
    proj_ref,
    expand_ref,
    shrinkt_ref,
    bb_out_ref,
    out_ref,
    state_ref,
    mine_ref,
    other_ref,
    w2_ref,
    hid_ref,
    nb_ref,
    f_ref,
    grads_ref,
    acc_ref,
    cols_ref,
    wqkvt_ref,
    bias_ref,
    e_ref,
    et_ref,
    ds_ref,
    inv_ref,
    ctxt_ref,
    qkvt_ref,
    dq_ref,
):
    r = pl.program_id(0)
    last = pl.num_programs(0) - 1
    units = w1a_ref.shape[1]

    @pl.when(r == 0)
    def _():
        w2_ref[:units] = w2a_ref[...]
        w2_ref[units:] = w2b_ref[...]
        grads_ref[...] = jnp.zeros_like(grads_ref)
        acc_ref[...] = jnp.zeros_like(acc_ref)
        for i, ref in enumerate((alpha_ref, gain1_ref, gain2_ref)):
            cols_ref[i] = jnp.broadcast_to(jnp.broadcast_to(ref[...].reshape(1, DS), (8, DS)).T[:, 0:1], (DS, ROW_LEN))
        wqkvt_ref[:DS] = sq_ref[...].T
        wqkvt_ref[DS : 2 * DS] = sk_ref[...].T
        wqkvt_ref[2 * DS :] = sv_ref[...].T

    shift, docs = row_starts(first_ref, lens_ref, r)
    back = (ROW_LEN - shift) & (ROW_LEN - 1)
    fill_bias(bias_ref, docs)

    middle = mid_ref[...]
    nb_ref[...] = (middle * lax.rsqrt(jnp.mean(middle * middle, axis=1, keepdims=True) + EPS) * fgain_ref[...].reshape(1, D)).astype(BF)
    for i, w in enumerate((w1a_ref, w1b_ref)):
        for c in range(0, units, 256):
            hid_ref[:, i * units + c : i * units + c + 256] = gelu(dot(nb_ref[...], w[:, c : c + 256])).astype(BF)

    for c in range(0, ROW_LEN, 128):
        f_ref[c : c + 128] = mid_ref[c : c + 128] + dot(hid_ref[c : c + 128], w2_ref[...])
    bb = f_ref[...].astype(BF)
    bb_out_ref[...] = turn_rows(f_ref, back).astype(BF)

    gain1, gain2 = cols_ref[1], cols_ref[2]
    mixing = 1.0 / (1.0 + jnp.exp(cols_ref[0] * -10.0))
    side = pltpu.roll(side_ref[...].astype(F32), back, 1)
    cot = pltpu.roll(cot_ref[...].astype(F32), back, 1)
    cotb = cot.astype(BF)
    lowered = dot(downt_ref[...], bb, 1, 1)
    inputs = mixing * lowered + (1.0 - mixing) * side
    scale1 = lax.rsqrt(jnp.mean(inputs * inputs, axis=0, keepdims=True) + EPS)
    fnt = (inputs * scale1 * gain1).astype(BF)
    qkvt_ref[...] = dot(wqkvt_ref[...], fnt).astype(BF)
    k, v = qkvt_ref[DS : 2 * DS].T, qkvt_ref[2 * DS :].T
    blocks = [(half, h) for half in range(2) for h in range(SIDE_HEADS)]
    sums = [side_scores(half, h, k, qkvt_ref, e_ref, bias_ref, False) for half, h in blocks]
    for (half, h), total in zip(blocks, sums):
        side_values(half, h, qkvt_ref, e_ref, ctxt_ref, inv_ref, total)

    @pl.when(out_of_range(sums))
    def _():
        keys = qkvt_ref[DS : 2 * DS].T
        for half in range(2):

            def again(h, carry):
                side_values(half, h, qkvt_ref, e_ref, ctxt_ref, inv_ref, side_scores(half, h, keys, qkvt_ref, e_ref, bias_ref, True))
                return carry

            lax.fori_loop(0, SIDE_HEADS, again, 0)

    ctx = ctxt_ref[...]
    ctxb = ctx.astype(BF)
    middle_side = inputs + dot(proj_ref[...], ctxb, 0, 0)
    scale2 = lax.rsqrt(jnp.mean(middle_side * middle_side, axis=0, keepdims=True) + EPS)
    snt = (middle_side * scale2 * gain2).astype(BF)
    expanded = dot(expand_ref[...], snt, 0, 0)
    activated, slope = gelu_and_slope(expanded)
    activated = activated.astype(BF)
    side_out = middle_side + dot(shrinkt_ref[...], activated)
    out_ref[...] = pltpu.roll(side_out, shift, 1)

    activated_grad = dot(shrinkt_ref[...], cotb, 0, 0)
    expanded_grad = (activated_grad * slope).astype(BF)
    second_grad = dot(expand_ref[...], expanded_grad)
    w2 = second_grad * gain2
    ms = middle_side * scale2
    mean2 = jnp.mean(w2 * middle_side, axis=0, keepdims=True)
    middle_grad = cot + scale2 * w2 - ms * (scale2 * scale2) * mean2
    acc_ref[0] += second_grad * ms
    branch = middle_grad.astype(BF)
    context_grad = dot(proj_ref[...], branch).astype(BF).astype(F32)
    dop = (context_grad * inv_ref[...]).astype(BF)
    centre = jnp.sum((dop.astype(F32) * ctx).reshape(SIDE_HEADS, 8, ROW_LEN), axis=1)
    centre = jnp.concatenate([centre, jnp.zeros((4, ROW_LEN), F32)], axis=0)
    chigh = centre.astype(BF)
    clow = (centre - chigh.astype(F32)).astype(BF)
    dstack = jnp.concatenate([dop, -chigh, -clow], axis=0)
    vones = jnp.concatenate([v, jnp.ones((ROW_LEN, 32), BF)], axis=1)
    root = SIDE_HEAD_DIM**-0.5
    for n, (half, h) in enumerate(blocks):
        rows = slice(half * HALF, (half + 1) * HALF)
        dp = dot(vones[rows] * head_mask(h, 128), dstack[:, rows])
        ds_ref[n] = (e_ref[n].astype(F32) * dp).astype(BF)
        et_ref[n] = e_ref[n].T
    for n, (half, h) in enumerate(blocks):
        rows = slice(half * HALF, (half + 1) * HALF)
        dq_ref[own_rows(h), rows] = head_rows(dot(qkvt_ref[pair(DS, h), rows], ds_ref[n]), h) * root
        e_ref[n] = ds_ref[n].T
    for n, (half, h) in enumerate(blocks):
        rows = slice(half * HALF, (half + 1) * HALF)
        dq_ref[own_rows(h, 2 * DS), rows] = head_rows(dot(dop[16 * (h // 2) : 16 * (h // 2) + 16, rows], et_ref[n]), h)
    for n, (half, h) in enumerate(blocks):
        rows = slice(half * HALF, (half + 1) * HALF)
        dq_ref[own_rows(h, DS), rows] = head_rows(dot(qkvt_ref[pair(0, h), rows], e_ref[n]), h) * root
    dqkvt = dq_ref[...].astype(BF)
    first_grad = dot(wqkvt_ref[...], dqkvt, 0, 0)
    w1 = first_grad * gain1
    ins = inputs * scale1
    mean1 = jnp.mean(w1 * inputs, axis=0, keepdims=True)
    input_grad = middle_grad + scale1 * w1 - ins * (scale1 * scale1) * mean1
    acc_ref[1] += first_grad * ins
    acc_ref[2] += input_grad * (lowered - side)
    state_ref[...] = pltpu.roll((1.0 - mixing) * input_grad, shift, 1)
    low = D + 2 * SFF
    grads_ref[:, 0:D] += dot((mixing * input_grad).astype(BF), bb)
    grads_ref[:, D : D + SFF] += dot(snt, expanded_grad, 1, 1)
    grads_ref[:, D + SFF : low] += dot(cotb, activated, 1, 1)
    grads_ref[:, low : low + 3 * DS] += dot(fnt, dqkvt, 1, 1)
    grads_ref[:, low + 3 * DS : low + 4 * DS] += dot(ctxb, branch, 1, 1)

    @pl.when(r == last)
    def _():
        gate = 1.0 / (1.0 + jnp.exp(cols_ref[0][:, 0:1] * -10.0))
        total = [jnp.sum(acc_ref[i], axis=1, keepdims=True) for i in range(3)]
        total[2] = total[2] * (gate * (1.0 - gate)) * 10.0
        place = lax.broadcasted_iota(jnp.int32, (DS, 128), 1)
        grads_ref[:, low + 4 * DS :] = jnp.where(place == 0, total[0], jnp.where(place == 1, total[1], jnp.where(place == 2, total[2], 0.0)))
        half = DS // 2
        tensor = (first_ref[0] != 0).astype(jnp.int32)
        mine_ref[...] = grads_ref[pl.ds(pl.multiple_of(tensor * half, 8), half), :].astype(BF)
        other_ref[...] = grads_ref[pl.ds(pl.multiple_of((1 - tensor) * half, 8), half), :].astype(BF)


def whole(shape):
    return pl.BlockSpec(shape, lambda r, *_: (0,) * len(shape), pipeline_mode=pl.Buffered(1))


def params(limit):
    return pltpu.CompilerParams(vmem_limit_bytes=limit * 1024 * 1024, dimension_semantics=("arbitrary",))


def swap(x):
    return lax.ppermute(x, "tensor", [(0, 1), (1, 0)])


def sum_over(mine, other, batch):
    place = lax.axis_index("batch")
    group = place & 3

    def trade(x, bits):
        return lax.ppermute(x, "batch", [(i, i ^ bits) for i in range(batch)])

    def pick(parts, k):
        return jnp.where(k == 0, parts[0], jnp.where(k == 1, parts[1], jnp.where(k == 2, parts[2], parts[3])))

    part = mine.astype(F32) + swap(other).astype(F32)
    bit, grouped = 1, batch >= 4
    if grouped:
        parts = jnp.split(part.astype(BF), 4, axis=1)
        got = [trade(pick(parts, group ^ m), m).astype(F32) for m in (1, 2, 3)]
        part = (pick(parts, group).astype(F32) + got[0]) + (got[1] + got[2])
        bit = 4
    while bit < batch:
        sent = part.astype(BF)
        part = sent.astype(F32) + trade(sent, bit).astype(F32)
        bit *= 2
    sent = part.astype(BF)
    if grouped:
        got = [sent] + [trade(sent, m) for m in (1, 2, 3)]
        sent = jnp.concatenate([pick(got, group ^ j) for j in range(4)], axis=1)
    got = swap(sent)
    upper = lax.axis_index("tensor") != 0
    return jnp.concatenate([jnp.where(upper, got, sent), jnp.where(upper, sent, got)], axis=0).astype(F32)


def make_body(batch):
    def body(
        hidden_in,
        lengths,
        attn_gain,
        attn_query,
        attn_key,
        attn_value,
        attn_out,
        ffn_gain,
        ffn_in,
        ffn_out,
        side_state,
        gate_alpha,
        down_w,
        side_attn_gain,
        side_query,
        side_key,
        side_value,
        side_proj,
        side_ffn_gain,
        side_expand,
        side_shrink,
        cotangent,
    ):
        tokens = hidden_in.shape[0]
        rows = tokens // ROW_LEN
        units = ffn_in.shape[1]
        t = lax.axis_index("tensor")
        first = (t * rows).astype(jnp.int32).reshape(1)
        tile = pl.BlockSpec((ROW_LEN, D), lambda r, *_: (r, 0))
        hbm = pl.BlockSpec(memory_space=pltpu.HBM)
        lens = lengths.T

        def kernel(body, name, limit, in_specs, out_specs, out_shape, scratch):
            return pl.pallas_call(
                body,
                grid_spec=pltpu.PrefetchScalarGridSpec(
                    num_scalar_prefetch=2, grid=(rows,), in_specs=in_specs, out_specs=out_specs, scratch_shapes=scratch
                ),
                out_shape=out_shape,
                compiler_params=params(limit),
                name=name,
            )

        own_attn = (attn_query, attn_key, attn_value, attn_out)
        far_attn = [swap(w) for w in own_attn]
        turned, normed = kernel(
            turn_kernel,
            "turn_rows",
            9,
            [tile, whole((D,))],
            [tile, tile],
            [jax.ShapeDtypeStruct((tokens, D), BF)] * 2,
            [pltpu.VMEM((ROW_LEN, D), F32)],
        )(first, lens, hidden_in, attn_gain)
        far_attn, turned, normed, ffn_in, ffn_out = lax.optimization_barrier((far_attn, turned, normed, ffn_in, ffn_out))
        far_ffn = [swap(w) for w in (ffn_in, ffn_out)]
        mid = kernel(
            attention_kernel,
            "attention",
            22,
            [tile, tile] + [hbm] * 8,
            tile,
            jax.ShapeDtypeStruct((tokens, D), F32),
            [
                pltpu.VMEM((D, 3 * D), BF),
                pltpu.VMEM((D, D), BF),
                pltpu.VMEM((ROW_LEN, 3 * D), BF),
                pltpu.VMEM((D, ROW_LEN), BF),
                pltpu.VMEM((2 * HEADS, HALF, HALF), BF),
                pltpu.VMEM((D, ROW_LEN), BF),
                pltpu.VMEM((HALF, HALF), F32),
                pltpu.SemaphoreType.DMA((8,)),
            ],
        )(first, lens, turned, normed, *[w for both in zip(own_attn, far_attn) for w in both])
        side_tile = pl.BlockSpec((DS, ROW_LEN), lambda r, *_: (0, r))
        side = pltpu.VMEM((DS, ROW_LEN), F32)
        square = pltpu.VMEM((2 * SIDE_HEADS, HALF, HALF), BF)
        backbone, side_out, state_grad, mine, other = kernel(
            side_kernel,
            "forward_and_back",
            30,
            [tile]
            + [whole((D, units))] * 2
            + [whole((units, D))] * 2
            + [whole((D,)), side_tile, side_tile]
            + [whole((DS,))] * 3
            + [whole((DS, D))]
            + [whole((DS, DS))] * 4
            + [whole((DS, SFF))] * 2,
            [tile, side_tile, side_tile] + [pl.BlockSpec((DS // 2, GRAD_LANES), lambda r, *_: (0, 0))] * 2,
            [
                jax.ShapeDtypeStruct((tokens, D), BF),
                jax.ShapeDtypeStruct((DS, tokens), F32),
                jax.ShapeDtypeStruct((DS, tokens), F32),
                jax.ShapeDtypeStruct((DS // 2, GRAD_LANES), BF),
                jax.ShapeDtypeStruct((DS // 2, GRAD_LANES), BF),
            ],
            [
                pltpu.VMEM((2 * units, D), BF),
                pltpu.VMEM((ROW_LEN, 2 * units), BF),
                pltpu.VMEM((ROW_LEN, D), BF),
                pltpu.VMEM((ROW_LEN, D), F32),
                pltpu.VMEM((DS, GRAD_LANES), F32),
                pltpu.VMEM((3, DS, ROW_LEN), F32),
                pltpu.VMEM((3, DS, ROW_LEN), F32),
                pltpu.VMEM((3 * DS, DS), BF),
                pltpu.VMEM((HALF, HALF), F32),
                square,
                square,
                square,
                side,
                side,
                pltpu.VMEM((3 * DS, ROW_LEN), BF),
                pltpu.VMEM((3 * DS, ROW_LEN), F32),
            ],
        )(
            first,
            lens,
            mid,
            ffn_in,
            far_ffn[0],
            ffn_out,
            far_ffn[1],
            ffn_gain,
            side_state.T,
            cotangent.T,
            gate_alpha,
            side_attn_gain,
            side_ffn_gain,
            down_w.T,
            side_query,
            side_key,
            side_value,
            side_proj,
            side_expand,
            side_shrink.T,
        )
        g = sum_over(mine, other, batch)
        low = D + 2 * SFF
        return (
            backbone,
            side_out.T,
            state_grad.T,
            g[:, :D].T,
            g[:, low + 4 * DS + 2],
            g[:, low + 4 * DS + 1],
            g[:, low : low + DS],
            g[:, low + DS : low + 2 * DS],
            g[:, low + 2 * DS : low + 3 * DS],
            g[:, low + 3 * DS : low + 4 * DS],
            g[:, low + 4 * DS],
            g[:, D : D + SFF],
            g[:, D + SFF : low].T,
        )

    return body


def solution(mesh):
    split = P(("batch", "tensor"), None)
    return jax.shard_map(
        make_body(mesh.shape["batch"]),
        mesh=mesh,
        in_specs=(
            split,
            P("batch", None),
            P(),
            P(None, "tensor"),
            P(None, "tensor"),
            P(None, "tensor"),
            P("tensor", None),
            P(),
            P(None, "tensor"),
            P("tensor", None),
            split,
            P(),
            P(),
            P(),
            P(),
            P(),
            P(),
            P(),
            P(),
            P(),
            P(),
            split,
        ),
        out_specs=(split, split, split) + (P(),) * 10,
        check_vma=False,
    )
```

```python
import jax
import jax.numpy as jnp
from jax import lax
from jax.experimental import pallas as pl
from jax.experimental.pallas import tpu as pltpu
from jax.sharding import PartitionSpec as P

BF = jnp.bfloat16
F32 = jnp.float32
D = 768
HEADS = 12
HEAD_DIM = 64
DS = 96
SIDE_HEADS = 12
SIDE_HEAD_DIM = 8
SFF = 384
ROW_LEN = 512
SEGS = 8
HALF = 256
GRAD_LANES = 2048
LAG_FORWARD = 6
LAG_BACK = 4
LOG2E = 1.4426950408889634
EPS = 1e-06


def dot(a, b, ca=1, cb=0):
    return lax.dot_general(a, b, (((ca,), (cb,)), ((), ())), preferred_element_type=F32)


def gelu(x):
    x2 = x * x
    u = x * (x2 * (0.7978845608028654 * 0.044715) + 0.7978845608028654)
    h = 0.5 * x
    return h + h * jnp.tanh(u)


def gelu_and_slope(x):
    x2 = x * x
    u = x * (x2 * (0.7978845608028654 * 0.044715) + 0.7978845608028654)
    t = jnp.tanh(u)
    h = 0.5 * x
    du = 0.7978845608028654 * 3.0 * 0.044715 * x2 + 0.7978845608028654
    return h + h * t, 0.5 + 0.5 * t + h * (1.0 - t * t) * du


def row_starts(first_ref, lens_ref, r):
    starts, begin = [], jnp.int32(0)
    long_start = jnp.int32(0)
    for j in range(SEGS):
        n = lens_ref[j, first_ref[0] + r]
        starts.append((begin, n))
        long_start = jnp.where(n == HALF, begin, long_start)
        begin = begin + n
    return long_start, [((b - long_start) & (ROW_LEN - 1), n) for b, n in starts]


def fill_bias(bias_ref, docs):
    q = lax.broadcasted_iota(jnp.int32, (1, HALF), 1) + HALF
    low = jnp.zeros((1, HALF), jnp.int32)
    high = jnp.zeros((1, HALF), jnp.int32)
    for b, n in docs:
        inside = (q >= b) & (q < b + n)
        low = jnp.where(inside, b, low)
        high = jnp.where(inside, b + n, high)
    k = lax.broadcasted_iota(jnp.int32, (HALF, HALF), 0) + HALF
    bias_ref[...] = jnp.where((k >= low) & (k < high), 0.0, -1e30)


def turn_rows(src_ref, shift):
    n = src_ref.shape[1]
    part = shift & 7
    first = lax.shift_right_logical(shift, 3)
    groups = []
    for g in range(ROW_LEN // 8 + 1):
        start = pl.multiple_of(((first + g) & (ROW_LEN // 8 - 1)) * 8, 8)
        groups.append(src_ref[pl.ds(start, 8), :])
    wide = jnp.concatenate(groups, axis=0).reshape(ROW_LEN // 8 + 1, 8, n)
    back = (8 - part) & 7
    wide = pltpu.roll(wide, back, 1)
    place = lax.broadcasted_iota(jnp.int32, (ROW_LEN // 8, 8, n), 1)
    turned = jnp.where(place < 8 - part, wide[:-1], wide[1:])
    return turned.reshape(ROW_LEN, n)


def exponentials(s, half, bias_ref, safe):
    if half:
        s = s + bias_ref[...]
    if safe:
        s = s - jnp.max(s, axis=0, keepdims=True)
    e = jnp.exp2(s)
    return e.astype(BF), jnp.sum(e, axis=0, keepdims=True)


def out_of_range(sums):
    low, high = sums[0], sums[0]
    for one in sums[1:]:
        low, high = jnp.minimum(low, one), jnp.maximum(high, one)
    fine = (jnp.min(low) > 1e-20) & (jnp.max(high) < 1e20)
    return jnp.logical_not(fine)


def at(start, size, step):
    return pl.ds(start if isinstance(start, int) else pl.multiple_of(start, step), size)


def frozen_scores(half, h, qkv_ref, e_ref, bias_ref, safe):
    p, j = h // 2, h % 2
    lane = lax.broadcasted_iota(jnp.int32, (1, 128), 1)
    keep = (lane >= 64 * j) & (lane < 64 * (j + 1))
    rows = slice(half * HALF, (half + 1) * HALF)
    q2 = qkv_ref[rows, at(p * 128, 128, 128)]
    k2 = qkv_ref[rows, at(D + p * 128, 128, 128)]
    s = dot(k2 * keep.astype(F32).astype(BF), q2, 1, 1) * (LOG2E / 8.0)
    e_ref[half * HEADS + h], total = exponentials(s, half, bias_ref, safe)
    return total


def frozen_values(half, h, vt_ref, e_ref, ctxt_ref, total):
    rows = slice(half * HALF, (half + 1) * HALF)
    head = at(h * HEAD_DIM, HEAD_DIM, HEAD_DIM)
    ctxt_ref[head, rows] = (dot(vt_ref[head, rows], e_ref[half * HEADS + h]) * (1.0 / total)).astype(BF)


def start_copies(pairs, sems):
    for i, (src, dst) in enumerate(pairs):
        pltpu.make_async_copy(src, dst, sems.at[i]).start()


def wait_copies(pairs, sems, first, last):
    for i in range(first, last):
        src, dst = pairs[i]
        pltpu.make_async_copy(src, dst, sems.at[i]).wait()


def turn_kernel(first_ref, lens_ref, x_ref, gain_ref, turned_ref, normed_ref, held_ref, raw_ref, sems):
    r = pl.program_id(0)
    rows = held_ref.shape[0]
    copies = [(x_ref.at[i * ROW_LEN : (i + 1) * ROW_LEN], held_ref.at[i]) for i in range(rows)]

    @pl.when(r == 0)
    def _():
        start_copies(copies, sems)

    pltpu.make_async_copy(x_ref.at[pl.ds(pl.multiple_of(r * ROW_LEN, ROW_LEN), ROW_LEN)], held_ref.at[r], sems.at[r]).wait()
    shift, _ = row_starts(first_ref, lens_ref, r)
    raw_ref[...] = held_ref[r].astype(F32)
    x = turn_rows(raw_ref, shift)
    turned_ref[...] = x.astype(BF)
    normed_ref[...] = (x * lax.rsqrt(jnp.mean(x * x, axis=1, keepdims=True) + EPS) * gain_ref[...].reshape(1, D)).astype(BF)


def attention_kernel(
    first_ref,
    lens_ref,
    turned_ref,
    normed_ref,
    wqa_ref,
    wqb_ref,
    wka_ref,
    wkb_ref,
    wva_ref,
    wvb_ref,
    woa_ref,
    wob_ref,
    mid_ref,
    wqkv_ref,
    wo_ref,
    qkv_ref,
    vt_ref,
    e_ref,
    ctxt_ref,
    bias_ref,
    sems,
):
    r = pl.program_id(0)
    cols = woa_ref.shape[0]
    copies = [(w, wqkv_ref.at[:, i * cols : (i + 1) * cols]) for i, w in enumerate((wqa_ref, wqb_ref, wka_ref, wkb_ref, wva_ref, wvb_ref))]
    copies += [(woa_ref, wo_ref.at[:cols]), (wob_ref, wo_ref.at[cols:])]

    @pl.when(r == 0)
    def _():
        start_copies(copies, sems)
        wait_copies(copies, sems, 0, 8)

    _, docs = row_starts(first_ref, lens_ref, r)
    fill_bias(bias_ref, docs)
    qkv_ref[...] = dot(normed_ref[...], wqkv_ref[...]).astype(BF)
    vt_ref[...] = qkv_ref[:, 2 * D :].T
    blocks = [(half, h) for half in range(2) for h in range(HEADS)]
    sums = [frozen_scores(half, h, qkv_ref, e_ref, bias_ref, False) for half, h in blocks]
    for (half, h), total in zip(blocks, sums):
        frozen_values(half, h, vt_ref, e_ref, ctxt_ref, total)

    @pl.when(out_of_range(sums))
    def _():
        for half in range(2):

            def again(h, carry):
                frozen_values(half, h, vt_ref, e_ref, ctxt_ref, frozen_scores(half, h, qkv_ref, e_ref, bias_ref, True))
                return carry

            lax.fori_loop(0, HEADS, again, 0)

    mid_ref[...] = turned_ref[...].astype(F32) + dot(ctxt_ref[...].T, wo_ref[...])


def head_mask(h, width):
    lane = lax.broadcasted_iota(jnp.int32, (1, width), 1)
    own = (lane >= 8 * h) & (lane < 8 * h + 8)
    if width > DS:
        own = own | (lane == DS + h) | (lane == DS + 16 + h)
    return own.astype(F32).astype(BF)


def head_rows(product, h):
    low, high = product[:SIDE_HEAD_DIM], product[SIDE_HEAD_DIM:]
    if isinstance(h, int):
        return high if h % 2 else low
    return jnp.where(h % 2 == 1, high, low)


def pair(base, h):
    return at(base + 16 * (h // 2), 16, 16)


def own_rows(h, base=0):
    return at(base + SIDE_HEAD_DIM * h, SIDE_HEAD_DIM, SIDE_HEAD_DIM)


def side_scores(half, h, k, qkvt_ref, e_ref, bias_ref, safe):
    rows = slice(half * HALF, (half + 1) * HALF)
    s = dot(k[rows] * head_mask(h, DS), qkvt_ref[:DS, rows]) * (LOG2E * SIDE_HEAD_DIM**-0.5)
    e_ref[half * SIDE_HEADS + h], total = exponentials(s, half, bias_ref, safe)
    return total


def side_values(half, h, qkvt_ref, e_ref, ctxt_ref, inv_ref, total):
    rows = slice(half * HALF, (half + 1) * HALF)
    inv = 1.0 / total
    mixed = dot(qkvt_ref[pair(2 * DS, h), rows], e_ref[half * SIDE_HEADS + h])
    ctxt_ref[own_rows(h), rows] = head_rows(mixed, h) * inv
    inv_ref[own_rows(h), rows] = jnp.broadcast_to(inv, (SIDE_HEAD_DIM, HALF))


def side_kernel(
    first_ref,
    lens_ref,
    mid0_ref,
    mid_ref,
    next_ref,
    w1a_ref,
    w1b_ref,
    w2a_ref,
    w2b_ref,
    fgain_ref,
    side_ref,
    cot_ref,
    alpha_ref,
    gain1_ref,
    gain2_ref,
    downt_ref,
    sq_ref,
    sk_ref,
    sv_ref,
    proj_ref,
    expand_ref,
    shrinkt_ref,
    bb_out_ref,
    out_ref,
    state_ref,
    mine_ref,
    other_ref,
    w2_ref,
    hid_ref,
    nb_ref,
    f_ref,
    grads_ref,
    acc_ref,
    cols_ref,
    wqkvt_ref,
    bias_ref,
    e_ref,
    et_ref,
    ds_ref,
    inv_ref,
    ctxt_ref,
    qkvt_ref,
    dq_ref,
    turned_ref,
):
    r = pl.program_id(0)
    last = pl.num_programs(0) - 1
    units = w1a_ref.shape[1]

    def norm_ahead(ref):
        middle = ref[...]
        nb_ref[...] = (middle * lax.rsqrt(jnp.mean(middle * middle, axis=1, keepdims=True) + EPS) * fgain_ref[...].reshape(1, D)).astype(BF)

    @pl.when(r == 0)
    def _():
        norm_ahead(mid0_ref)
        w2_ref[:units] = w2a_ref[...]
        w2_ref[units:] = w2b_ref[...]
        grads_ref[...] = jnp.zeros_like(grads_ref)
        acc_ref[...] = jnp.zeros_like(acc_ref)
        for i, ref in enumerate((alpha_ref, gain1_ref, gain2_ref)):
            cols_ref[i] = jnp.broadcast_to(jnp.broadcast_to(ref[...].reshape(1, DS), (8, DS)).T[:, 0:1], (DS, ROW_LEN))
        cols_ref[0] = 1.0 / (1.0 + jnp.exp(cols_ref[0] * -10.0))
        wqkvt_ref[:DS] = sq_ref[...].T
        wqkvt_ref[DS : 2 * DS] = sk_ref[...].T
        wqkvt_ref[2 * DS :] = sv_ref[...].T

    shift, docs = row_starts(first_ref, lens_ref, r)
    back = (ROW_LEN - shift) & (ROW_LEN - 1)
    fill_bias(bias_ref, docs)

    turned_ref[0] = pltpu.roll(side_ref[...].astype(F32), back, 1)
    turned_ref[1] = pltpu.roll(cot_ref[...].astype(F32), back, 1)

    for i, w in enumerate((w1a_ref, w1b_ref)):
        for c in range(0, units, 256):
            hid_ref[:, i * units + c : i * units + c + 256] = gelu(dot(nb_ref[...], w[:, c : c + 256])).astype(BF)

    for c in range(0, ROW_LEN, 256):
        f_ref[c : c + 256] = mid_ref[c : c + 256] + dot(hid_ref[c : c + 256], w2_ref[...])
    norm_ahead(next_ref)
    bb = f_ref[...].astype(BF)
    bb_out_ref[...] = turn_rows(f_ref, back).astype(BF)

    mixing, gain1, gain2 = cols_ref[0], cols_ref[1], cols_ref[2]
    lowered = dot(downt_ref[...], bb, 1, 1)
    activated_grad = dot(shrinkt_ref[...], turned_ref[1].astype(BF), 0, 0)
    side = turned_ref[0]
    inputs = mixing * lowered + (1.0 - mixing) * side
    scale1 = lax.rsqrt(jnp.mean(inputs * inputs, axis=0, keepdims=True) + EPS)
    fnt = (inputs * scale1 * gain1).astype(BF)
    qkvt_ref[...] = dot(wqkvt_ref[...], fnt).astype(BF)
    k, v = qkvt_ref[DS : 2 * DS].T, qkvt_ref[2 * DS :].T
    blocks = [(half, h) for half in range(2) for h in range(SIDE_HEADS)]
    sums = []
    for n, (half, h) in enumerate(blocks + [(None, None)] * LAG_FORWARD):
        if n < len(blocks):
            sums.append(side_scores(half, h, k, qkvt_ref, e_ref, bias_ref, False))
        if n >= LAG_FORWARD:
            side_values(*blocks[n - LAG_FORWARD], qkvt_ref, e_ref, ctxt_ref, inv_ref, sums[n - LAG_FORWARD])

    @pl.when(out_of_range(sums))
    def _():
        keys = qkvt_ref[DS : 2 * DS].T
        for half in range(2):

            def again(h, carry):
                side_values(half, h, qkvt_ref, e_ref, ctxt_ref, inv_ref, side_scores(half, h, keys, qkvt_ref, e_ref, bias_ref, True))
                return carry

            lax.fori_loop(0, SIDE_HEADS, again, 0)

    ctx = ctxt_ref[...]
    ctxb = ctx.astype(BF)
    middle_side = inputs + dot(proj_ref[...], ctxb, 0, 0)
    scale2 = lax.rsqrt(jnp.mean(middle_side * middle_side, axis=0, keepdims=True) + EPS)
    snt = (middle_side * scale2 * gain2).astype(BF)
    expanded = dot(expand_ref[...], snt, 0, 0)
    activated, slope = gelu_and_slope(expanded)
    activated = activated.astype(BF)
    expanded_grad = (activated_grad * slope).astype(BF)
    second_grad = dot(expand_ref[...], expanded_grad)
    low = D + 2 * SFF
    cot = turned_ref[1]
    cotb = cot.astype(BF)
    side_out = middle_side + dot(shrinkt_ref[...], activated)
    out_ref[...] = pltpu.roll(side_out, shift, 1)
    grads_ref[:, D : D + SFF] += dot(snt, expanded_grad, 1, 1)
    grads_ref[:, D + SFF : low] += dot(cotb, activated, 1, 1)
    w2 = second_grad * gain2
    ms = middle_side * scale2
    mean2 = jnp.mean(w2 * middle_side, axis=0, keepdims=True)
    middle_grad = cot + scale2 * w2 - ms * (scale2 * scale2) * mean2
    acc_ref[0] += second_grad * ms
    branch = middle_grad.astype(BF)
    context_grad = dot(proj_ref[...], branch).astype(BF).astype(F32)
    grads_ref[:, low + 3 * DS : low + 4 * DS] += dot(ctxb, branch, 1, 1)
    dop = (context_grad * inv_ref[...]).astype(BF)
    centre = jnp.sum((dop.astype(F32) * ctx).reshape(SIDE_HEADS, 8, ROW_LEN), axis=1)
    centre = jnp.concatenate([centre, jnp.zeros((4, ROW_LEN), F32)], axis=0)
    chigh = centre.astype(BF)
    clow = (centre - chigh.astype(F32)).astype(BF)
    dstack = jnp.concatenate([dop, -chigh, -clow], axis=0)
    vones = jnp.concatenate([v, jnp.ones((ROW_LEN, 32), BF)], axis=1)
    root = SIDE_HEAD_DIM**-0.5

    def score_step(n):
        half, h = blocks[n]
        rows = slice(half * HALF, (half + 1) * HALF)
        dp = dot(vones[rows] * head_mask(h, 128), dstack[:, rows])
        ds_ref[n] = (e_ref[n].astype(F32) * dp).astype(BF)
        et_ref[n] = e_ref[n].T

    def query_step(n):
        half, h = blocks[n]
        rows = slice(half * HALF, (half + 1) * HALF)
        dq_ref[own_rows(h), rows] = head_rows(dot(qkvt_ref[pair(DS, h), rows], ds_ref[n]), h) * root
        e_ref[n] = ds_ref[n].T

    def value_step(n):
        half, h = blocks[n]
        rows = slice(half * HALF, (half + 1) * HALF)
        dq_ref[own_rows(h, 2 * DS), rows] = head_rows(dot(dop[16 * (h // 2) : 16 * (h // 2) + 16, rows], et_ref[n]), h)

    def key_step(n):
        half, h = blocks[n]
        rows = slice(half * HALF, (half + 1) * HALF)
        dq_ref[own_rows(h, DS), rows] = head_rows(dot(qkvt_ref[pair(0, h), rows], e_ref[n]), h) * root

    for n in range(len(blocks) + 3 * LAG_BACK):
        for i, step in enumerate((score_step, query_step, value_step, key_step)):
            if 0 <= n - i * LAG_BACK < len(blocks):
                step(n - i * LAG_BACK)
    dqkvt = dq_ref[...].astype(BF)
    first_grad = dot(wqkvt_ref[...], dqkvt, 0, 0)
    grads_ref[:, low : low + 3 * DS] += dot(fnt, dqkvt, 1, 1)
    w1 = first_grad * gain1
    ins = inputs * scale1
    mean1 = jnp.mean(w1 * inputs, axis=0, keepdims=True)
    input_grad = middle_grad + scale1 * w1 - ins * (scale1 * scale1) * mean1
    acc_ref[1] += first_grad * ins
    acc_ref[2] += input_grad * (lowered - side)
    state_ref[...] = pltpu.roll((1.0 - mixing) * input_grad, shift, 1)
    grads_ref[:, 0:D] += dot((mixing * input_grad).astype(BF), bb)

    @pl.when(r == last)
    def _():
        gate = cols_ref[0][:, 0:1]
        total = [jnp.sum(acc_ref[i], axis=1, keepdims=True) for i in range(3)]
        total[2] = total[2] * (gate * (1.0 - gate)) * 10.0
        place = lax.broadcasted_iota(jnp.int32, (DS, 128), 1)
        grads_ref[:, low + 4 * DS :] = jnp.where(place == 0, total[0], jnp.where(place == 1, total[1], jnp.where(place == 2, total[2], 0.0)))
        half = DS // 2
        tensor = (first_ref[0] != 0).astype(jnp.int32)
        mine_ref[...] = grads_ref[pl.ds(pl.multiple_of(tensor * half, 8), half), :].astype(BF)
        other_ref[...] = grads_ref[pl.ds(pl.multiple_of((1 - tensor) * half, 8), half), :].astype(BF)


def whole(shape):
    return pl.BlockSpec(shape, lambda r, *_: (0,) * len(shape), pipeline_mode=pl.Buffered(1))


def params(limit):
    return pltpu.CompilerParams(vmem_limit_bytes=limit * 1024 * 1024, dimension_semantics=("arbitrary",))


def swap(x):
    return lax.ppermute(x, "tensor", [(0, 1), (1, 0)])


def sum_over(mine, other, batch):
    place = lax.axis_index("batch")
    group = place & 3

    def trade(x, bits):
        return lax.ppermute(x, "batch", [(i, i ^ bits) for i in range(batch)])

    def pick(parts, k):
        return jnp.where(k == 0, parts[0], jnp.where(k == 1, parts[1], jnp.where(k == 2, parts[2], parts[3])))

    part = mine.astype(F32) + swap(other).astype(F32)
    bit, grouped = 1, batch >= 4
    if grouped:
        parts = jnp.split(part.astype(BF), 4, axis=1)
        got = [trade(pick(parts, group ^ m), m).astype(F32) for m in (1, 2, 3)]
        part = (pick(parts, group).astype(F32) + got[0]) + (got[1] + got[2])
        bit = 4
    while bit < batch:
        sent = part.astype(BF)
        part = sent.astype(F32) + trade(sent, bit).astype(F32)
        bit *= 2
    sent = part.astype(BF)
    if grouped:
        got = [sent] + [trade(sent, m) for m in (1, 2, 3)]
        sent = jnp.concatenate([pick(got, group ^ j) for j in range(4)], axis=1)
    return sent, swap(sent)


def unpack_kernel(tensor_ref, sent_ref, got_ref, down_ref, alpha_ref, gain1_ref, q_ref, k_ref, v_ref, proj_ref, gain2_ref, expand_ref, shrink_ref):
    upper = tensor_ref[0] != 0

    def both(first, end):
        sent, got = sent_ref[:, first:end].astype(F32), got_ref[:, first:end].astype(F32)
        return jnp.concatenate([jnp.where(upper, got, sent), jnp.where(upper, sent, got)], axis=0)

    low = D + 2 * SFF
    down_ref[...] = both(0, D)
    expand_ref[...] = both(D, D + SFF)
    shrink_ref[...] = both(D + SFF, low)
    squares = both(low, low + 4 * DS)
    for i, ref in enumerate((q_ref, k_ref, v_ref, proj_ref)):
        ref[...] = squares[:, i * DS : (i + 1) * DS]
    vectors = both(low + 4 * DS, low + 4 * DS + 128).T
    for i, ref in enumerate((gain2_ref, gain1_ref, alpha_ref)):
        ref[...] = vectors[i]


def make_body(batch):
    def body(
        hidden_in,
        lengths,
        attn_gain,
        attn_query,
        attn_key,
        attn_value,
        attn_out,
        ffn_gain,
        ffn_in,
        ffn_out,
        side_state,
        gate_alpha,
        down_w,
        side_attn_gain,
        side_query,
        side_key,
        side_value,
        side_proj,
        side_ffn_gain,
        side_expand,
        side_shrink,
        cotangent,
    ):
        tokens = hidden_in.shape[0]
        rows = tokens // ROW_LEN
        units = ffn_in.shape[1]
        t = lax.axis_index("tensor")
        first = (t * rows).astype(jnp.int32).reshape(1)
        tile = pl.BlockSpec((ROW_LEN, D), lambda r, *_: (r, 0))
        hbm = pl.BlockSpec(memory_space=pltpu.HBM)
        lens = lengths.T

        def kernel(body, name, limit, in_specs, out_specs, out_shape, scratch):
            return pl.pallas_call(
                body,
                grid_spec=pltpu.PrefetchScalarGridSpec(
                    num_scalar_prefetch=2, grid=(rows,), in_specs=in_specs, out_specs=out_specs, scratch_shapes=scratch
                ),
                out_shape=out_shape,
                compiler_params=params(limit),
                name=name,
            )

        own_attn = (attn_query, attn_key, attn_value, attn_out)
        far_attn = [swap(w) for w in own_attn]
        own_attn = [pltpu.with_memory_space_constraint(w, pltpu.HBM) for w in own_attn]
        hidden_in = pltpu.with_memory_space_constraint(hidden_in, pltpu.HBM)
        attn_gain = pltpu.with_memory_space_constraint(attn_gain, pltpu.HBM)
        turned, normed = kernel(
            turn_kernel,
            "turn_rows",
            13,
            [hbm, whole((D,))],
            [tile, tile],
            [jax.ShapeDtypeStruct((tokens, D), BF)] * 2,
            [pltpu.VMEM((rows, ROW_LEN, D), BF), pltpu.VMEM((ROW_LEN, D), F32), pltpu.SemaphoreType.DMA((rows,))],
        )(first, lens, hidden_in, attn_gain)
        far_attn, turned, normed, ffn_in, ffn_out = lax.optimization_barrier((far_attn, turned, normed, ffn_in, ffn_out))
        far_ffn = [swap(w) for w in (ffn_in, ffn_out)]
        mid = kernel(
            attention_kernel,
            "attention",
            22,
            [tile, tile] + [hbm] * 8,
            tile,
            jax.ShapeDtypeStruct((tokens, D), F32),
            [
                pltpu.VMEM((D, 3 * D), BF),
                pltpu.VMEM((D, D), BF),
                pltpu.VMEM((ROW_LEN, 3 * D), BF),
                pltpu.VMEM((D, ROW_LEN), BF),
                pltpu.VMEM((2 * HEADS, HALF, HALF), BF),
                pltpu.VMEM((D, ROW_LEN), BF),
                pltpu.VMEM((HALF, HALF), F32),
                pltpu.SemaphoreType.DMA((8,)),
            ],
        )(first, lens, turned, normed, *[w for both in zip(own_attn, far_attn) for w in both])
        side_tile = pl.BlockSpec((DS, ROW_LEN), lambda r, *_: (0, r))
        side = pltpu.VMEM((DS, ROW_LEN), F32)
        square = pltpu.VMEM((2 * SIDE_HEADS, HALF, HALF), BF)
        backbone, side_out, state_grad, mine, other = kernel(
            side_kernel,
            "forward_and_back",
            32,
            [whole((ROW_LEN, D)), tile, pl.BlockSpec((ROW_LEN, D), lambda r, *_: (jnp.minimum(r + 1, rows - 1), 0))]
            + [whole((D, units))] * 2
            + [whole((units, D))] * 2
            + [whole((D,)), side_tile, side_tile]
            + [whole((DS,))] * 3
            + [whole((DS, D))]
            + [whole((DS, DS))] * 4
            + [whole((DS, SFF))] * 2,
            [tile, side_tile, side_tile] + [pl.BlockSpec((DS // 2, GRAD_LANES), lambda r, *_: (0, 0))] * 2,
            [
                jax.ShapeDtypeStruct((tokens, D), BF),
                jax.ShapeDtypeStruct((DS, tokens), F32),
                jax.ShapeDtypeStruct((DS, tokens), F32),
                jax.ShapeDtypeStruct((DS // 2, GRAD_LANES), BF),
                jax.ShapeDtypeStruct((DS // 2, GRAD_LANES), BF),
            ],
            [
                pltpu.VMEM((2 * units, D), BF),
                pltpu.VMEM((ROW_LEN, 2 * units), BF),
                pltpu.VMEM((ROW_LEN, D), BF),
                pltpu.VMEM((ROW_LEN, D), F32),
                pltpu.VMEM((DS, GRAD_LANES), F32),
                pltpu.VMEM((3, DS, ROW_LEN), F32),
                pltpu.VMEM((3, DS, ROW_LEN), F32),
                pltpu.VMEM((3 * DS, DS), BF),
                pltpu.VMEM((HALF, HALF), F32),
                square,
                square,
                square,
                side,
                side,
                pltpu.VMEM((3 * DS, ROW_LEN), BF),
                pltpu.VMEM((3 * DS, ROW_LEN), F32),
                pltpu.VMEM((2, DS, ROW_LEN), F32),
            ],
        )(
            first,
            lens,
            mid,
            mid,
            mid,
            ffn_in,
            far_ffn[0],
            ffn_out,
            far_ffn[1],
            ffn_gain,
            side_state.T,
            cotangent.T,
            gate_alpha,
            side_attn_gain,
            side_ffn_gain,
            down_w.T,
            side_query,
            side_key,
            side_value,
            side_proj,
            side_expand,
            side_shrink.T,
        )
        square_out = jax.ShapeDtypeStruct((DS, DS), F32)
        vector_out = jax.ShapeDtypeStruct((DS,), F32)
        wide_out = jax.ShapeDtypeStruct((DS, SFF), F32)
        vmem = pl.BlockSpec(memory_space=pltpu.VMEM)
        down, alpha, gain1, query, key, value, proj, gain2, expand, shrink = pl.pallas_call(
            unpack_kernel,
            in_specs=[pl.BlockSpec(memory_space=pltpu.SMEM), vmem, vmem],
            out_specs=[vmem] * 10,
            out_shape=[jax.ShapeDtypeStruct((DS, D), F32), vector_out, vector_out]
            + [square_out] * 4
            + [vector_out, wide_out, wide_out],
            compiler_params=pltpu.CompilerParams(vmem_limit_bytes=6 * 1024 * 1024),
            name="unpack",
        )(first, *sum_over(mine, other, batch))
        return backbone, side_out.T, state_grad.T, down.T, alpha, gain1, query, key, value, proj, gain2, expand, shrink.T

    return body


def solution(mesh):
    split = P(("batch", "tensor"), None)
    return jax.shard_map(
        make_body(mesh.shape["batch"]),
        mesh=mesh,
        in_specs=(
            split,
            P("batch", None),
            P(),
            P(None, "tensor"),
            P(None, "tensor"),
            P(None, "tensor"),
            P("tensor", None),
            P(),
            P(None, "tensor"),
            P("tensor", None),
            split,
            P(),
            P(),
            P(),
            P(),
            P(),
            P(),
            P(),
            P(),
            P(),
            P(),
            split,
        ),
        out_specs=(split, split, split) + (P(),) * 10,
        check_vma=False,
    )
```

```python
import jax
import jax.numpy as jnp
from jax import lax
from jax.experimental import pallas as pl
from jax.experimental.pallas import tpu as pltpu
from jax.sharding import PartitionSpec as P

BF = jnp.bfloat16
F32 = jnp.float32
D = 768
HEADS = 12
HEAD_DIM = 64
DS = 96
SIDE_HEADS = 12
SIDE_HEAD_DIM = 8
SFF = 384
ROW_LEN = 512
SEGS = 8
HALF = 256
GRAD_LANES = 2048
LAG_FORWARD = 6
LAG_BACK = 4
LOG2E = 1.4426950408889634
EPS = 1e-06


def dot(a, b, ca=1, cb=0):
    return lax.dot_general(a, b, (((ca,), (cb,)), ((), ())), preferred_element_type=F32)


def gelu(x):
    x2 = x * x
    u = x * (x2 * (0.7978845608028654 * 0.044715) + 0.7978845608028654)
    h = 0.5 * x
    return h + h * jnp.tanh(u)


def gelu_and_slope(x):
    x2 = x * x
    u = x * (x2 * (0.7978845608028654 * 0.044715) + 0.7978845608028654)
    t = jnp.tanh(u)
    h = 0.5 * x
    du = 0.7978845608028654 * 3.0 * 0.044715 * x2 + 0.7978845608028654
    return h + h * t, 0.5 + 0.5 * t + h * (1.0 - t * t) * du


def row_starts(first_ref, lens_ref, r):
    starts, begin = [], jnp.int32(0)
    long_start = jnp.int32(0)
    for j in range(SEGS):
        n = lens_ref[j, first_ref[0] + r]
        starts.append((begin, n))
        long_start = jnp.where(n == HALF, begin, long_start)
        begin = begin + n
    return long_start, [((b - long_start) & (ROW_LEN - 1), n) for b, n in starts]


def fill_bias(bias_ref, docs):
    q = lax.broadcasted_iota(jnp.int32, (1, HALF), 1) + HALF
    low = jnp.zeros((1, HALF), jnp.int32)
    high = jnp.zeros((1, HALF), jnp.int32)
    for b, n in docs:
        inside = (q >= b) & (q < b + n)
        low = jnp.where(inside, b, low)
        high = jnp.where(inside, b + n, high)
    k = lax.broadcasted_iota(jnp.int32, (HALF, HALF), 0) + HALF
    bias_ref[...] = jnp.where((k >= low) & (k < high), 0.0, -1e30)


def turn_rows(src_ref, shift):
    n = src_ref.shape[1]
    part = shift & 7
    first = lax.shift_right_logical(shift, 3)
    groups = []
    for g in range(ROW_LEN // 8 + 1):
        start = pl.multiple_of(((first + g) & (ROW_LEN // 8 - 1)) * 8, 8)
        groups.append(src_ref[pl.ds(start, 8), :])
    wide = jnp.concatenate(groups, axis=0).reshape(ROW_LEN // 8 + 1, 8, n)
    back = (8 - part) & 7
    wide = pltpu.roll(wide, back, 1)
    place = lax.broadcasted_iota(jnp.int32, (ROW_LEN // 8, 8, n), 1)
    turned = jnp.where(place < 8 - part, wide[:-1], wide[1:])
    return turned.reshape(ROW_LEN, n)


def exponentials(s, half, bias_ref, safe):
    if half:
        s = s + bias_ref[...]
    if safe:
        s = s - jnp.max(s, axis=0, keepdims=True)
    return jnp.exp2(s)


def out_of_range(sums):
    low, high = sums[0], sums[0]
    for one in sums[1:]:
        low, high = jnp.minimum(low, one), jnp.maximum(high, one)
    fine = (jnp.min(low) > 1e-20) & (jnp.max(high) < 1e20)
    return jnp.logical_not(fine)


def at(start, size, step):
    return pl.ds(start if isinstance(start, int) else pl.multiple_of(start, step), size)


def frozen_scores(half, h, qkv_ref, e_ref, bias_ref, safe):
    p, j = h // 2, h % 2
    lane = lax.broadcasted_iota(jnp.int32, (1, 128), 1)
    keep = (lane >= 64 * j) & (lane < 64 * (j + 1))
    rows = slice(half * HALF, (half + 1) * HALF)
    q2 = qkv_ref[rows, at(p * 128, 128, 128)]
    k2 = qkv_ref[rows, at(D + p * 128, 128, 128)]
    s = dot(k2 * keep.astype(F32).astype(BF), q2, 1, 1)
    e = exponentials(s, half, bias_ref, safe)
    e_ref[half * HEADS + h] = e.astype(BF)
    return jnp.sum(e, axis=0, keepdims=True)


def frozen_values(half, h, vt_ref, e_ref, ctxt_ref, total):
    rows = slice(half * HALF, (half + 1) * HALF)
    head = at(h * HEAD_DIM, HEAD_DIM, HEAD_DIM)
    ctxt_ref[head, rows] = (dot(vt_ref[head, rows], e_ref[half * HEADS + h]) * (1.0 / total)).astype(BF)


def start_copies(pairs, sems):
    for i, (src, dst) in enumerate(pairs):
        pltpu.make_async_copy(src, dst, sems.at[i]).start()


def wait_copies(pairs, sems, first, last):
    for i in range(first, last):
        src, dst = pairs[i]
        pltpu.make_async_copy(src, dst, sems.at[i]).wait()


def turn_kernel(first_ref, lens_ref, x_ref, wq_ref, wk_ref, wv_ref, turned_ref, joined_ref, held_ref, raw_ref, sems, joined_sems):
    r = pl.program_id(0)
    rows = held_ref.shape[0]
    copies = [(x_ref.at[i * ROW_LEN : (i + 1) * ROW_LEN], held_ref.at[i]) for i in range(rows)]
    joins = [(w, joined_ref.at[i]) for i, w in enumerate((wq_ref, wk_ref, wv_ref))]

    @pl.when(r == 0)
    def _():
        start_copies(copies, sems)
        start_copies(joins, joined_sems)

    pltpu.make_async_copy(x_ref.at[pl.ds(pl.multiple_of(r * ROW_LEN, ROW_LEN), ROW_LEN)], held_ref.at[r], sems.at[r]).wait()
    shift, _ = row_starts(first_ref, lens_ref, r)
    raw_ref[...] = held_ref[r].astype(F32)
    turned_ref[...] = turn_rows(raw_ref, shift).astype(BF)

    @pl.when(r == rows - 1)
    def _():
        wait_copies(joins, joined_sems, 0, 3)


def attention_kernel(
    first_ref,
    lens_ref,
    turned0_ref,
    turned_ref,
    gain_ref,
    joined_ref,
    wq_ref,
    wk_ref,
    wv_ref,
    ctxt_ref,
    wqkv_ref,
    qkv_ref,
    vt_ref,
    e_ref,
    bias_ref,
    nb_ref,
    sems,
):
    r = pl.program_id(0)
    cols = wq_ref.shape[1]
    copies = []
    for i, far in enumerate((wq_ref, wk_ref, wv_ref)):
        copies += [(joined_ref.at[i], wqkv_ref.at[:, i * D : i * D + cols]), (far, wqkv_ref.at[:, i * D + cols : (i + 1) * D])]

    def norm_ahead(ref):
        x = ref[...].astype(F32)
        nb_ref[...] = (x * lax.rsqrt(jnp.mean(x * x, axis=1, keepdims=True) + EPS) * gain_ref[...].reshape(1, D)).astype(BF)

    @pl.when(r == 0)
    def _():
        start_copies(copies, sems)
        norm_ahead(turned0_ref)
        wait_copies(copies, sems, 0, 6)

    _, docs = row_starts(first_ref, lens_ref, r)
    fill_bias(bias_ref, docs)
    qkv_ref[:, :D] = (dot(nb_ref[...], wqkv_ref[:, :D]) * (LOG2E * HEAD_DIM**-0.5)).astype(BF)
    qkv_ref[:, D:] = dot(nb_ref[...], wqkv_ref[:, D:]).astype(BF)
    norm_ahead(turned_ref)
    vt_ref[...] = qkv_ref[:, 2 * D :].T
    blocks = [(half, h) for half in range(2) for h in range(HEADS)]
    sums = [frozen_scores(half, h, qkv_ref, e_ref, bias_ref, False) for half, h in blocks]
    for (half, h), total in zip(blocks, sums):
        frozen_values(half, h, vt_ref, e_ref, ctxt_ref, total)

    @pl.when(out_of_range(sums))
    def _():
        for half in range(2):

            def again(h, carry):
                frozen_values(half, h, vt_ref, e_ref, ctxt_ref, frozen_scores(half, h, qkv_ref, e_ref, bias_ref, True))
                return carry

            lax.fori_loop(0, HEADS, again, 0)


def head_mask(h, width):
    lane = lax.broadcasted_iota(jnp.int32, (1, width), 1)
    own = (lane >= 8 * h) & (lane < 8 * h + 8)
    if width > DS:
        own = own | (lane == DS + h) | (lane == DS + 16 + h)
    return own.astype(F32).astype(BF)


def head_rows(product, h):
    low, high = product[:SIDE_HEAD_DIM], product[SIDE_HEAD_DIM:]
    if isinstance(h, int):
        return high if h % 2 else low
    return jnp.where(h % 2 == 1, high, low)


def pair(base, h):
    return at(base + 16 * (h // 2), 16, 16)


def own_rows(h, base=0):
    return at(base + SIDE_HEAD_DIM * h, SIDE_HEAD_DIM, SIDE_HEAD_DIM)


def side_scores(half, h, k, qkvt_ref, e_ref, bias_ref, safe):
    rows = slice(half * HALF, (half + 1) * HALF)
    s = dot(k[rows] * head_mask(h, DS), qkvt_ref[:DS, rows])
    e_ref[half * SIDE_HEADS + h] = exponentials(s, half, bias_ref, safe).astype(BF)


def side_values(half, h, vt_ref, e_ref, ctxt_ref, inv_ref):
    rows = slice(half * HALF, (half + 1) * HALF)
    mixed = dot(vt_ref[at(16 * h, 16, 16), rows], e_ref[half * SIDE_HEADS + h])
    total = mixed[8:9]
    inv = 1.0 / total
    ctxt_ref[own_rows(h), rows] = mixed[:8] * inv
    inv_ref[own_rows(h), rows] = jnp.broadcast_to(inv, (SIDE_HEAD_DIM, HALF))
    return total


def side_kernel(
    first_ref,
    lens_ref,
    ctx0_ref,
    turned0_ref,
    ctx_ref,
    turned_ref,
    woa_ref,
    wob_ref,
    w1a_ref,
    w1b_ref,
    w2a_ref,
    w2b_ref,
    fgain_ref,
    side_ref,
    cot_ref,
    alpha_ref,
    gain1_ref,
    gain2_ref,
    downt_ref,
    sq_ref,
    sk_ref,
    sv_ref,
    proj_ref,
    expand_ref,
    shrinkt_ref,
    bb_out_ref,
    out_ref,
    state_ref,
    mine_ref,
    other_ref,
    wo_ref,
    w2_ref,
    mid_ref,
    hid_ref,
    nb_ref,
    f_ref,
    grads_ref,
    acc_ref,
    cols_ref,
    wqkvt_ref,
    bias_ref,
    e_ref,
    et_ref,
    ds_ref,
    inv_ref,
    ctxt_ref,
    qkvt_ref,
    dq_ref,
    rolled_ref,
    vt_ref,
):
    r = pl.program_id(0)
    last = pl.num_programs(0) - 1
    units = w1a_ref.shape[1]

    def middle_ahead(ctx, turned, half):
        rows = slice(half * HALF, (half + 1) * HALF)
        mid_ref[rows] = turned[rows].astype(F32) + dot(ctx[:, rows].T, wo_ref[...])

    def norm_ahead():
        middle = mid_ref[...]
        nb_ref[...] = (middle * lax.rsqrt(jnp.mean(middle * middle, axis=1, keepdims=True) + EPS) * fgain_ref[...].reshape(1, D)).astype(BF)

    @pl.when(r == 0)
    def _():
        heads = woa_ref.shape[0]
        wo_ref[:heads] = woa_ref[...]
        wo_ref[heads:] = wob_ref[...]
        middle_ahead(ctx0_ref, turned0_ref, 0)
        middle_ahead(ctx0_ref, turned0_ref, 1)
        norm_ahead()
        w2_ref[:units] = w2a_ref[...]
        w2_ref[units:] = w2b_ref[...]
        grads_ref[...] = jnp.zeros_like(grads_ref)
        acc_ref[...] = jnp.zeros_like(acc_ref)
        for i, ref in enumerate((alpha_ref, gain1_ref, gain2_ref)):
            cols_ref[i] = jnp.broadcast_to(jnp.broadcast_to(ref[...].reshape(1, DS), (8, DS)).T[:, 0:1], (DS, ROW_LEN))
        cols_ref[0] = 1.0 / (1.0 + jnp.exp(cols_ref[0] * -10.0))
        wqkvt_ref[:DS] = sq_ref[...].T
        wqkvt_ref[DS : 2 * DS] = sk_ref[...].T
        wqkvt_ref[2 * DS :] = sv_ref[...].T

    shift, docs = row_starts(first_ref, lens_ref, r)
    back = (ROW_LEN - shift) & (ROW_LEN - 1)
    fill_bias(bias_ref, docs)

    rolled_ref[0] = pltpu.roll(side_ref[...].astype(F32), back, 1)
    rolled_ref[1] = pltpu.roll(cot_ref[...].astype(F32), back, 1)

    for i, w in enumerate((w1a_ref, w1b_ref)):
        for c in range(0, units, 256):
            hid_ref[:, i * units + c : i * units + c + 256] = gelu(dot(nb_ref[...], w[:, c : c + 256])).astype(BF)

    for c in range(0, ROW_LEN, 256):
        f_ref[c : c + 256] = mid_ref[c : c + 256] + dot(hid_ref[c : c + 256], w2_ref[...])
    bb = f_ref[...].astype(BF)

    mixing, gain1, gain2 = cols_ref[0], cols_ref[1], cols_ref[2]
    lowered = dot(downt_ref[...], bb, 1, 1)
    activated_grad = dot(shrinkt_ref[...], rolled_ref[1].astype(BF), 0, 0)
    middle_ahead(ctx_ref, turned_ref, 0)
    side = rolled_ref[0]
    inputs = mixing * lowered + (1.0 - mixing) * side
    scale1 = lax.rsqrt(jnp.mean(inputs * inputs, axis=0, keepdims=True) + EPS)
    fnt = (inputs * scale1 * gain1).astype(BF)
    qkv = dot(wqkvt_ref[...], fnt)
    qkvt_ref[:DS] = (qkv[:DS] * (LOG2E * SIDE_HEAD_DIM**-0.5)).astype(BF)
    qkvt_ref[DS:] = qkv[DS:].astype(BF)
    ones = jnp.ones((SIDE_HEADS, 8, ROW_LEN), F32)
    vt_ref[...] = jnp.concatenate([qkv[2 * DS :].reshape(SIDE_HEADS, 8, ROW_LEN), ones], axis=1).reshape(2 * DS, ROW_LEN).astype(BF)
    middle_ahead(ctx_ref, turned_ref, 1)
    k, v = qkvt_ref[DS : 2 * DS].T, qkvt_ref[2 * DS :].T
    norm_ahead()
    blocks = [(half, h) for half in range(2) for h in range(SIDE_HEADS)]
    sums = []
    for n, (half, h) in enumerate(blocks + [(None, None)] * LAG_FORWARD):
        if n < len(blocks):
            side_scores(half, h, k, qkvt_ref, e_ref, bias_ref, False)
        if n >= LAG_FORWARD:
            sums.append(side_values(*blocks[n - LAG_FORWARD], vt_ref, e_ref, ctxt_ref, inv_ref))

    @pl.when(out_of_range(sums))
    def _():
        keys = qkvt_ref[DS : 2 * DS].T
        for half in range(2):

            def again(h, carry):
                side_scores(half, h, keys, qkvt_ref, e_ref, bias_ref, True)
                side_values(half, h, vt_ref, e_ref, ctxt_ref, inv_ref)
                return carry

            lax.fori_loop(0, SIDE_HEADS, again, 0)

    ctx = ctxt_ref[...]
    ctxb = ctx.astype(BF)
    middle_side = inputs + dot(proj_ref[...], ctxb, 0, 0)
    scale2 = lax.rsqrt(jnp.mean(middle_side * middle_side, axis=0, keepdims=True) + EPS)
    snt = (middle_side * scale2 * gain2).astype(BF)
    expanded = dot(expand_ref[...], snt, 0, 0)
    activated, slope = gelu_and_slope(expanded)
    activated = activated.astype(BF)
    expanded_grad = (activated_grad * slope).astype(BF)
    second_grad = dot(expand_ref[...], expanded_grad)
    low = D + 2 * SFF
    cot = rolled_ref[1]
    cotb = cot.astype(BF)
    side_out = middle_side + dot(shrinkt_ref[...], activated)
    out_ref[...] = pltpu.roll(side_out, shift, 1)
    grads_ref[:, D : D + SFF] += dot(snt, expanded_grad, 1, 1)
    grads_ref[:, D + SFF : low] += dot(cotb, activated, 1, 1)
    w2 = second_grad * gain2
    ms = middle_side * scale2
    mean2 = jnp.mean(w2 * middle_side, axis=0, keepdims=True)
    middle_grad = cot + scale2 * w2 - ms * (scale2 * scale2) * mean2
    acc_ref[0] += second_grad * ms
    branch = middle_grad.astype(BF)
    context_grad = dot(proj_ref[...], branch).astype(BF).astype(F32)
    grads_ref[:, low + 3 * DS : low + 4 * DS] += dot(ctxb, branch, 1, 1)
    dop = (context_grad * inv_ref[...]).astype(BF)
    centre = jnp.sum((dop.astype(F32) * ctx).reshape(SIDE_HEADS, 8, ROW_LEN), axis=1)
    centre = jnp.concatenate([centre, jnp.zeros((4, ROW_LEN), F32)], axis=0)
    chigh = centre.astype(BF)
    clow = (centre - chigh.astype(F32)).astype(BF)
    dstack = jnp.concatenate([dop, -chigh, -clow], axis=0)
    vones = jnp.concatenate([v, jnp.ones((ROW_LEN, 32), BF)], axis=1)
    root = SIDE_HEAD_DIM**-0.5

    def score_step(n):
        half, h = blocks[n]
        rows = slice(half * HALF, (half + 1) * HALF)
        dp = dot(vones[rows] * head_mask(h, 128), dstack[:, rows])
        ds_ref[n] = (e_ref[n].astype(F32) * dp).astype(BF)
        et_ref[n] = e_ref[n].T

    def query_step(n):
        half, h = blocks[n]
        rows = slice(half * HALF, (half + 1) * HALF)
        dq_ref[own_rows(h), rows] = head_rows(dot(qkvt_ref[pair(DS, h), rows], ds_ref[n]), h) * root
        e_ref[n] = ds_ref[n].T

    def value_step(n):
        half, h = blocks[n]
        rows = slice(half * HALF, (half + 1) * HALF)
        dq_ref[own_rows(h, 2 * DS), rows] = head_rows(dot(dop[16 * (h // 2) : 16 * (h // 2) + 16, rows], et_ref[n]), h)

    def key_step(n):
        half, h = blocks[n]
        rows = slice(half * HALF, (half + 1) * HALF)
        dq_ref[own_rows(h, DS), rows] = head_rows(dot(qkvt_ref[pair(0, h), rows], e_ref[n]), h) * (1.0 / LOG2E)

    for n in range(len(blocks) + 3 * LAG_BACK):
        for i, step in enumerate((score_step, query_step, value_step, key_step)):
            if 0 <= n - i * LAG_BACK < len(blocks):
                step(n - i * LAG_BACK)
    dqkvt = dq_ref[...].astype(BF)
    bb_out_ref[...] = turn_rows(f_ref, back).astype(BF)
    first_grad = dot(wqkvt_ref[...], dqkvt, 0, 0)
    grads_ref[:, low : low + 3 * DS] += dot(fnt, dqkvt, 1, 1)
    w1 = first_grad * gain1
    ins = inputs * scale1
    mean1 = jnp.mean(w1 * inputs, axis=0, keepdims=True)
    input_grad = middle_grad + scale1 * w1 - ins * (scale1 * scale1) * mean1
    acc_ref[1] += first_grad * ins
    acc_ref[2] += input_grad * (lowered - side)
    state_ref[...] = pltpu.roll((1.0 - mixing) * input_grad, shift, 1)
    grads_ref[:, 0:D] += dot((mixing * input_grad).astype(BF), bb)

    @pl.when(r == last)
    def _():
        gate = cols_ref[0][:, 0:1]
        total = [jnp.sum(acc_ref[i], axis=1, keepdims=True) for i in range(3)]
        total[2] = total[2] * (gate * (1.0 - gate)) * 10.0
        place = lax.broadcasted_iota(jnp.int32, (DS, 128), 1)
        grads_ref[:, low + 4 * DS :] = jnp.where(place == 0, total[0], jnp.where(place == 1, total[1], jnp.where(place == 2, total[2], 0.0)))
        half = DS // 2
        tensor = (first_ref[0] != 0).astype(jnp.int32)
        mine_ref[...] = grads_ref[pl.ds(pl.multiple_of(tensor * half, 8), half), :].astype(BF)
        other_ref[...] = grads_ref[pl.ds(pl.multiple_of((1 - tensor) * half, 8), half), :].astype(BF)


def whole(shape):
    return pl.BlockSpec(shape, lambda r, *_: (0,) * len(shape), pipeline_mode=pl.Buffered(1))


def params(limit):
    return pltpu.CompilerParams(vmem_limit_bytes=limit * 1024 * 1024, dimension_semantics=("arbitrary",))


def swap(x):
    return lax.ppermute(x, "tensor", [(0, 1), (1, 0)])


def sum_over(mine, other, batch):
    place = lax.axis_index("batch")
    group = place & 3

    def trade(x, bits):
        return lax.ppermute(x, "batch", [(i, i ^ bits) for i in range(batch)])

    def pick(parts, k):
        return jnp.where(k == 0, parts[0], jnp.where(k == 1, parts[1], jnp.where(k == 2, parts[2], parts[3])))

    part = mine.astype(F32) + swap(other).astype(F32)
    bit, grouped = 1, batch >= 4
    if grouped:
        parts = jnp.split(part.astype(BF), 4, axis=1)
        got = [trade(pick(parts, group ^ m), m).astype(F32) for m in (1, 2, 3)]
        part = (pick(parts, group).astype(F32) + got[0]) + (got[1] + got[2])
        bit = 4
    while bit < batch:
        sent = part.astype(BF)
        part = sent.astype(F32) + trade(sent, bit).astype(F32)
        bit *= 2
    sent = part.astype(BF)
    if grouped:
        got = [sent] + [trade(sent, m) for m in (1, 2, 3)]
        sent = jnp.concatenate([pick(got, group ^ j) for j in range(4)], axis=1)
    return sent, swap(sent)


def unpack_kernel(tensor_ref, sent_ref, got_ref, down_ref, alpha_ref, gain1_ref, q_ref, k_ref, v_ref, proj_ref, gain2_ref, expand_ref, shrink_ref):
    upper = tensor_ref[0] != 0

    def both(first, end):
        sent, got = sent_ref[:, first:end].astype(F32), got_ref[:, first:end].astype(F32)
        return jnp.concatenate([jnp.where(upper, got, sent), jnp.where(upper, sent, got)], axis=0)

    low = D + 2 * SFF
    down_ref[...] = both(0, D)
    expand_ref[...] = both(D, D + SFF)
    shrink_ref[...] = both(D + SFF, low)
    squares = both(low, low + 4 * DS)
    for i, ref in enumerate((q_ref, k_ref, v_ref, proj_ref)):
        ref[...] = squares[:, i * DS : (i + 1) * DS]
    vectors = both(low + 4 * DS, low + 4 * DS + 128).T
    for i, ref in enumerate((gain2_ref, gain1_ref, alpha_ref)):
        ref[...] = vectors[i]


def make_body(batch):
    def body(
        hidden_in,
        lengths,
        attn_gain,
        attn_query,
        attn_key,
        attn_value,
        attn_out,
        ffn_gain,
        ffn_in,
        ffn_out,
        side_state,
        gate_alpha,
        down_w,
        side_attn_gain,
        side_query,
        side_key,
        side_value,
        side_proj,
        side_ffn_gain,
        side_expand,
        side_shrink,
        cotangent,
    ):
        tokens = hidden_in.shape[0]
        rows = tokens // ROW_LEN
        units = ffn_in.shape[1]
        t = lax.axis_index("tensor")
        first = (t * rows).astype(jnp.int32).reshape(1)
        tile = pl.BlockSpec((ROW_LEN, D), lambda r, *_: (r, 0))
        hbm = pl.BlockSpec(memory_space=pltpu.HBM)
        lens = pltpu.with_memory_space_constraint(lengths.T, pltpu.HBM)

        def kernel(body, name, limit, in_specs, out_specs, out_shape, scratch):
            return pl.pallas_call(
                body,
                grid_spec=pltpu.PrefetchScalarGridSpec(
                    num_scalar_prefetch=2, grid=(rows,), in_specs=in_specs, out_specs=out_specs, scratch_shapes=scratch
                ),
                out_shape=out_shape,
                compiler_params=params(limit),
                name=name,
            )

        own_attn = (attn_query, attn_key, attn_value)
        far_attn = [swap(w) for w in own_attn]
        own_attn = [pltpu.with_memory_space_constraint(w, pltpu.HBM) for w in own_attn]
        hidden_in = pltpu.with_memory_space_constraint(hidden_in, pltpu.HBM)
        attn_gain = pltpu.with_memory_space_constraint(attn_gain, pltpu.HBM)
        turned, joined = kernel(
            turn_kernel,
            "turn_rows",
            11,
            [hbm] * 4,
            [tile, pl.BlockSpec(memory_space=pl.ANY)],
            [jax.ShapeDtypeStruct((tokens, D), BF), jax.ShapeDtypeStruct((3, D, attn_query.shape[1]), BF)],
            [
                pltpu.VMEM((rows, ROW_LEN, D), BF),
                pltpu.VMEM((ROW_LEN, D), F32),
                pltpu.SemaphoreType.DMA((rows,)),
                pltpu.SemaphoreType.DMA((3,)),
            ],
        )(first, lens, hidden_in, *own_attn)
        far_attn, turned, attn_out, ffn_in, ffn_out = lax.optimization_barrier((far_attn, turned, attn_out, ffn_in, ffn_out))
        far_out, far_in, far_shrink = [swap(w) for w in (attn_out, ffn_in, ffn_out)]
        next_tile = pl.BlockSpec((ROW_LEN, D), lambda r, *_: (jnp.minimum(r + 1, rows - 1), 0))
        wide_tile = pl.BlockSpec((D, ROW_LEN), lambda r, *_: (0, r))
        ctx = kernel(
            attention_kernel,
            "attention",
            20,
            [whole((ROW_LEN, D)), next_tile, whole((D,)), pl.BlockSpec(memory_space=pl.ANY)] + [hbm] * 3,
            wide_tile,
            jax.ShapeDtypeStruct((D, tokens), BF),
            [
                pltpu.VMEM((D, 3 * D), BF),
                pltpu.VMEM((ROW_LEN, 3 * D), BF),
                pltpu.VMEM((D, ROW_LEN), BF),
                pltpu.VMEM((2 * HEADS, HALF, HALF), BF),
                pltpu.VMEM((HALF, HALF), F32),
                pltpu.VMEM((ROW_LEN, D), BF),
                pltpu.SemaphoreType.DMA((6,)),
            ],
        )(first, lens, turned, turned, attn_gain, joined, *far_attn)
        side_tile = pl.BlockSpec((DS, ROW_LEN), lambda r, *_: (0, r))
        side = pltpu.VMEM((DS, ROW_LEN), F32)
        square = pltpu.VMEM((2 * SIDE_HEADS, HALF, HALF), BF)
        backbone, side_out, state_grad, mine, other = kernel(
            side_kernel,
            "forward_and_back",
            32,
            [
                whole((D, ROW_LEN)),
                whole((ROW_LEN, D)),
                pl.BlockSpec((D, ROW_LEN), lambda r, *_: (0, jnp.minimum(r + 1, rows - 1))),
                next_tile,
            ]
            + [whole((D // 2, D))] * 2
            + [whole((D, units))] * 2
            + [whole((units, D))] * 2
            + [whole((D,)), side_tile, side_tile]
            + [whole((DS,))] * 3
            + [whole((DS, D))]
            + [whole((DS, DS))] * 4
            + [whole((DS, SFF))] * 2,
            [tile, side_tile, side_tile] + [pl.BlockSpec((DS // 2, GRAD_LANES), lambda r, *_: (0, 0))] * 2,
            [
                jax.ShapeDtypeStruct((tokens, D), BF),
                jax.ShapeDtypeStruct((DS, tokens), F32),
                jax.ShapeDtypeStruct((DS, tokens), F32),
                jax.ShapeDtypeStruct((DS // 2, GRAD_LANES), BF),
                jax.ShapeDtypeStruct((DS // 2, GRAD_LANES), BF),
            ],
            [
                pltpu.VMEM((D, D), BF),
                pltpu.VMEM((2 * units, D), BF),
                pltpu.VMEM((ROW_LEN, D), F32),
                pltpu.VMEM((ROW_LEN, 2 * units), BF),
                pltpu.VMEM((ROW_LEN, D), BF),
                pltpu.VMEM((ROW_LEN, D), F32),
                pltpu.VMEM((DS, GRAD_LANES), F32),
                pltpu.VMEM((3, DS, ROW_LEN), F32),
                pltpu.VMEM((3, DS, ROW_LEN), F32),
                pltpu.VMEM((3 * DS, DS), BF),
                pltpu.VMEM((HALF, HALF), F32),
                square,
                square,
                square,
                side,
                side,
                pltpu.VMEM((3 * DS, ROW_LEN), BF),
                pltpu.VMEM((3 * DS, ROW_LEN), F32),
                pltpu.VMEM((2, DS, ROW_LEN), F32),
                pltpu.VMEM((2 * DS, ROW_LEN), BF),
            ],
        )(
            first,
            lens,
            ctx,
            turned,
            ctx,
            turned,
            attn_out,
            far_out,
            ffn_in,
            far_in,
            ffn_out,
            far_shrink,
            ffn_gain,
            side_state.T,
            cotangent.T,
            gate_alpha,
            side_attn_gain,
            side_ffn_gain,
            down_w.T,
            side_query,
            side_key,
            side_value,
            side_proj,
            side_expand,
            side_shrink.T,
        )
        square_out = jax.ShapeDtypeStruct((DS, DS), F32)
        vector_out = jax.ShapeDtypeStruct((DS,), F32)
        wide_out = jax.ShapeDtypeStruct((DS, SFF), F32)
        vmem = pl.BlockSpec(memory_space=pltpu.VMEM)
        down, alpha, gain1, query, key, value, proj, gain2, expand, shrink = pl.pallas_call(
            unpack_kernel,
            in_specs=[pl.BlockSpec(memory_space=pltpu.SMEM), vmem, vmem],
            out_specs=[vmem] * 10,
            out_shape=[jax.ShapeDtypeStruct((DS, D), F32), vector_out, vector_out]
            + [square_out] * 4
            + [vector_out, wide_out, wide_out],
            compiler_params=pltpu.CompilerParams(vmem_limit_bytes=6 * 1024 * 1024),
            name="unpack",
        )(first, *sum_over(mine, other, batch))
        return backbone, side_out.T, state_grad.T, down.T, alpha, gain1, query, key, value, proj, gain2, expand, shrink.T

    return body


def solution(mesh):
    split = P(("batch", "tensor"), None)
    return jax.shard_map(
        make_body(mesh.shape["batch"]),
        mesh=mesh,
        in_specs=(
            split,
            P("batch", None),
            P(),
            P(None, "tensor"),
            P(None, "tensor"),
            P(None, "tensor"),
            P("tensor", None),
            P(),
            P(None, "tensor"),
            P("tensor", None),
            split,
            P(),
            P(),
            P(),
            P(),
            P(),
            P(),
            P(),
            P(),
            P(),
            P(),
            split,
        ),
        out_specs=(split, split, split) + (P(),) * 10,
        check_vma=False,
    )
```

```python
import jax
import jax.numpy as jnp
from jax import lax
from jax.experimental import pallas as pl
from jax.experimental.pallas import tpu as pltpu
from jax.sharding import PartitionSpec as P

BF = jnp.bfloat16
F32 = jnp.float32
D = 768
HEADS = 12
HEAD_DIM = 64
DS = 96
SIDE_HEADS = 12
SIDE_HEAD_DIM = 8
SFF = 384
ROW_LEN = 512
SEGS = 8
HALF = 256
GRAD_LANES = 2048
LAG_FORWARD = 6
LAG_BACK = 4
LOG2E = 1.4426950408889634
EPS = 1e-06


def dot(a, b, ca=1, cb=0):
    return lax.dot_general(a, b, (((ca,), (cb,)), ((), ())), preferred_element_type=F32)


def gelu(x):
    x2 = x * x
    u = x * (x2 * (0.7978845608028654 * 0.044715) + 0.7978845608028654)
    h = 0.5 * x
    return h + h * jnp.tanh(u)


def gelu_and_slope(x):
    x2 = x * x
    u = x * (x2 * (0.7978845608028654 * 0.044715) + 0.7978845608028654)
    p = 0.5 + 0.5 * jnp.tanh(u)
    out = x * p
    return out, p + out * (1.0 - p) * (x2 * (1.5957691216057308 * 3.0 * 0.044715) + 1.5957691216057308)


def row_starts(first_ref, lens_ref, r):
    starts, begin = [], jnp.int32(0)
    long_start = jnp.int32(0)
    for j in range(SEGS):
        n = lens_ref[j, first_ref[0] + r]
        starts.append((begin, n))
        long_start = jnp.where(n == HALF, begin, long_start)
        begin = begin + n
    return long_start, [((b - long_start) & (ROW_LEN - 1), n) for b, n in starts]


def fill_bias(bias_ref, docs):
    q = lax.broadcasted_iota(jnp.int32, (1, HALF), 1) + HALF
    low = jnp.zeros((1, HALF), jnp.int32)
    high = jnp.zeros((1, HALF), jnp.int32)
    for b, n in docs:
        inside = (q >= b) & (q < b + n)
        low = jnp.where(inside, b, low)
        high = jnp.where(inside, b + n, high)
    k = lax.broadcasted_iota(jnp.int32, (HALF, HALF), 0) + HALF
    bias_ref[...] = jnp.where((k >= low) & (k < high), 0.0, -1e30)


def turn_rows(src_ref, shift):
    n = src_ref.shape[1]
    part = shift & 7
    first = lax.shift_right_logical(shift, 3)
    groups = []
    for g in range(ROW_LEN // 8 + 1):
        start = pl.multiple_of(((first + g) & (ROW_LEN // 8 - 1)) * 8, 8)
        groups.append(src_ref[pl.ds(start, 8), :])
    wide = jnp.concatenate(groups, axis=0).reshape(ROW_LEN // 8 + 1, 8, n)
    back = (8 - part) & 7
    wide = pltpu.roll(wide, back, 1)
    place = lax.broadcasted_iota(jnp.int32, (ROW_LEN // 8, 8, n), 1)
    turned = jnp.where(place < 8 - part, wide[:-1], wide[1:])
    return turned.reshape(ROW_LEN, n)


def exponentials(s, half, bias_ref, safe):
    if half:
        s = s + bias_ref[...]
    if safe:
        s = s - jnp.max(s, axis=0, keepdims=True)
    return jnp.exp2(s)


def out_of_range(sums):
    low, high = sums[0], sums[0]
    for one in sums[1:]:
        low, high = jnp.minimum(low, one), jnp.maximum(high, one)
    fine = (jnp.min(low) > 1e-20) & (jnp.max(high) < 1e20)
    return jnp.logical_not(fine)


def at(start, size, step):
    return pl.ds(start if isinstance(start, int) else pl.multiple_of(start, step), size)


def frozen_scores(half, h, qkv_ref, e_ref, bias_ref, safe):
    p, j = h // 2, h % 2
    lane = lax.broadcasted_iota(jnp.int32, (1, 128), 1)
    keep = (lane >= 64 * j) & (lane < 64 * (j + 1))
    rows = slice(half * HALF, (half + 1) * HALF)
    q2 = qkv_ref[rows, at(p * 128, 128, 128)]
    k2 = qkv_ref[rows, at(D + p * 128, 128, 128)]
    s = dot(k2 * keep.astype(F32).astype(BF), q2, 1, 1) * (LOG2E * HEAD_DIM**-0.5)
    e = exponentials(s, half, bias_ref, safe)
    e_ref[half * HEADS + h] = e.astype(BF)
    return jnp.sum(e, axis=0, keepdims=True)


def frozen_values(half, h, vt_ref, e_ref, ctxt_ref, total):
    rows = slice(half * HALF, (half + 1) * HALF)
    head = at(h * HEAD_DIM, HEAD_DIM, HEAD_DIM)
    ctxt_ref[head, rows] = (dot(vt_ref[head, rows], e_ref[half * HEADS + h]) * (1.0 / total)).astype(BF)


def start_copies(pairs, sems):
    for i, (src, dst) in enumerate(pairs):
        pltpu.make_async_copy(src, dst, sems.at[i]).start()


def wait_copies(pairs, sems, first, last):
    for i in range(first, last):
        src, dst = pairs[i]
        pltpu.make_async_copy(src, dst, sems.at[i]).wait()


def turn_kernel(first_ref, lens_ref, x_ref, wq_ref, wk_ref, wv_ref, turned_ref, joined_ref, held_ref, raw_ref, sems, joined_sems):
    r = pl.program_id(0)
    rows = held_ref.shape[0]
    copies = [(x_ref.at[i * ROW_LEN : (i + 1) * ROW_LEN], held_ref.at[i]) for i in range(rows)]
    joins = [(w, joined_ref.at[i]) for i, w in enumerate((wq_ref, wk_ref, wv_ref))]

    @pl.when(r == 0)
    def _():
        start_copies(copies, sems)
        start_copies(joins, joined_sems)

    pltpu.make_async_copy(x_ref.at[pl.ds(pl.multiple_of(r * ROW_LEN, ROW_LEN), ROW_LEN)], held_ref.at[r], sems.at[r]).wait()
    shift, _ = row_starts(first_ref, lens_ref, r)
    raw_ref[...] = held_ref[r].astype(F32)
    turned_ref[...] = turn_rows(raw_ref, shift).astype(BF)

    @pl.when(r == rows - 1)
    def _():
        wait_copies(joins, joined_sems, 0, 3)


def attention_kernel(
    first_ref,
    lens_ref,
    turned0_ref,
    turned_ref,
    gain_ref,
    joined_ref,
    wq_ref,
    wk_ref,
    wv_ref,
    ctxt_ref,
    wqkv_ref,
    qkv_ref,
    vt_ref,
    e_ref,
    bias_ref,
    nb_ref,
):
    r = pl.program_id(0)
    cols = wq_ref.shape[1]

    def norm_ahead(ref):
        x = ref[...].astype(F32)
        nb_ref[...] = (x * lax.rsqrt(jnp.mean(x * x, axis=1, keepdims=True) + EPS) * gain_ref[...].reshape(1, D)).astype(BF)

    @pl.when(r == 0)
    def _():
        norm_ahead(turned0_ref)
        for i, far in enumerate((wq_ref, wk_ref, wv_ref)):
            wqkv_ref[:, i * D : i * D + cols] = joined_ref[i]
            wqkv_ref[:, i * D + cols : (i + 1) * D] = far[...]

    _, docs = row_starts(first_ref, lens_ref, r)
    fill_bias(bias_ref, docs)
    qkv_ref[...] = dot(nb_ref[...], wqkv_ref[...]).astype(BF)
    norm_ahead(turned_ref)
    vt_ref[...] = qkv_ref[:, 2 * D :].T
    blocks = [(half, h) for half in range(2) for h in range(HEADS)]
    sums = [frozen_scores(half, h, qkv_ref, e_ref, bias_ref, False) for half, h in blocks]
    for (half, h), total in zip(blocks, sums):
        frozen_values(half, h, vt_ref, e_ref, ctxt_ref, total)

    @pl.when(out_of_range(sums))
    def _():
        for half in range(2):

            def again(h, carry):
                frozen_values(half, h, vt_ref, e_ref, ctxt_ref, frozen_scores(half, h, qkv_ref, e_ref, bias_ref, True))
                return carry

            lax.fori_loop(0, HEADS, again, 0)


def head_mask(h, width):
    lane = lax.broadcasted_iota(jnp.int32, (1, width), 1)
    own = (lane >= 8 * h) & (lane < 8 * h + 8)
    if width > DS:
        own = own | (lane == DS + h) | (lane == DS + 16 + h)
    return own.astype(F32).astype(BF)


def head_rows(product, h):
    low, high = product[:SIDE_HEAD_DIM], product[SIDE_HEAD_DIM:]
    if isinstance(h, int):
        return high if h % 2 else low
    return jnp.where(h % 2 == 1, high, low)


def pair(base, h):
    return at(base + 16 * (h // 2), 16, 16)


def own_rows(h, base=0):
    return at(base + SIDE_HEAD_DIM * h, SIDE_HEAD_DIM, SIDE_HEAD_DIM)


def side_scores(half, h, k, qkvt_ref, e_ref, bias_ref, safe):
    rows = slice(half * HALF, (half + 1) * HALF)
    s = dot(k[rows] * head_mask(h, DS), qkvt_ref[:DS, rows]) * (LOG2E * SIDE_HEAD_DIM**-0.5)
    e_ref[half * SIDE_HEADS + h] = exponentials(s, half, bias_ref, safe).astype(BF)


def side_values(half, h, vt_ref, e_ref, ctxt_ref, inv_ref):
    rows = slice(half * HALF, (half + 1) * HALF)
    mixed = dot(vt_ref[at(16 * h, 16, 16), rows], e_ref[half * SIDE_HEADS + h])
    total = mixed[8:9]
    inv = 1.0 / total
    ctxt_ref[own_rows(h), rows] = mixed[:8] * inv
    inv_ref[own_rows(h), rows] = jnp.broadcast_to(inv, (SIDE_HEAD_DIM, HALF))
    return total


def side_kernel(
    first_ref,
    lens_ref,
    ctx0_ref,
    turned0_ref,
    ctx_ref,
    turned_ref,
    woa_ref,
    wob_ref,
    w1a_ref,
    w1b_ref,
    w2a_ref,
    w2b_ref,
    fgain_ref,
    side_ref,
    cot_ref,
    alpha_ref,
    gain1_ref,
    gain2_ref,
    downt_ref,
    sq_ref,
    sk_ref,
    sv_ref,
    proj_ref,
    expand_ref,
    shrinkt_ref,
    bb_out_ref,
    out_ref,
    state_ref,
    mine_ref,
    other_ref,
    wo_ref,
    w2_ref,
    mid_ref,
    hid_ref,
    nb_ref,
    f_ref,
    grads_ref,
    acc_ref,
    cols_ref,
    wqkvt_ref,
    bias_ref,
    e_ref,
    et_ref,
    ds_ref,
    inv_ref,
    ctxt_ref,
    qkvt_ref,
    dq_ref,
    rolled_ref,
    vt_ref,
):
    r = pl.program_id(0)
    last = pl.num_programs(0) - 1
    units = w1a_ref.shape[1]

    def middle_ahead(ctx, turned, half):
        rows = slice(half * HALF, (half + 1) * HALF)
        mid_ref[rows] = turned[rows].astype(F32) + dot(ctx[:, rows].T, wo_ref[...])

    def norm_ahead():
        middle = mid_ref[...]
        nb_ref[...] = (middle * lax.rsqrt(jnp.mean(middle * middle, axis=1, keepdims=True) + EPS) * fgain_ref[...].reshape(1, D)).astype(BF)

    @pl.when(r == 0)
    def _():
        heads = woa_ref.shape[0]
        wo_ref[:heads] = woa_ref[...]
        wo_ref[heads:] = wob_ref[...]
        middle_ahead(ctx0_ref, turned0_ref, 0)
        middle_ahead(ctx0_ref, turned0_ref, 1)
        norm_ahead()
        w2_ref[:units] = w2a_ref[...]
        w2_ref[units:] = w2b_ref[...]
        grads_ref[...] = jnp.zeros_like(grads_ref)
        acc_ref[...] = jnp.zeros_like(acc_ref)
        for i, ref in enumerate((alpha_ref, gain1_ref, gain2_ref)):
            cols_ref[i] = jnp.broadcast_to(jnp.broadcast_to(ref[...].reshape(1, DS), (8, DS)).T[:, 0:1], (DS, ROW_LEN))
        cols_ref[0] = 1.0 / (1.0 + jnp.exp(cols_ref[0] * -10.0))
        wqkvt_ref[:DS] = sq_ref[...].T
        wqkvt_ref[DS : 2 * DS] = sk_ref[...].T
        wqkvt_ref[2 * DS :] = sv_ref[...].T

    shift, docs = row_starts(first_ref, lens_ref, r)
    back = (ROW_LEN - shift) & (ROW_LEN - 1)
    fill_bias(bias_ref, docs)

    rolled_ref[0] = pltpu.roll(side_ref[...].astype(F32), back, 1)
    rolled_ref[1] = pltpu.roll(cot_ref[...].astype(F32), back, 1)

    for i, w in enumerate((w1a_ref, w1b_ref)):
        for c in range(0, units, 256):
            hid_ref[:, i * units + c : i * units + c + 256] = gelu(dot(nb_ref[...], w[:, c : c + 256])).astype(BF)

    for c in range(0, ROW_LEN, 256):
        f_ref[c : c + 256] = mid_ref[c : c + 256] + dot(hid_ref[c : c + 256], w2_ref[...])
    bb = f_ref[...].astype(BF)

    mixing, gain1, gain2 = cols_ref[0], cols_ref[1], cols_ref[2]
    lowered = dot(downt_ref[...], bb, 1, 1)
    activated_grad = dot(shrinkt_ref[...], rolled_ref[1].astype(BF), 0, 0)
    middle_ahead(ctx_ref, turned_ref, 0)
    side = rolled_ref[0]
    inputs = mixing * lowered + (1.0 - mixing) * side
    scale1 = lax.rsqrt(jnp.mean(inputs * inputs, axis=0, keepdims=True) + EPS)
    fnt = (inputs * scale1 * gain1).astype(BF)
    qkv = dot(wqkvt_ref[...], fnt)
    qkvt_ref[...] = qkv.astype(BF)
    ones = jnp.ones((SIDE_HEADS, 8, ROW_LEN), F32)
    vt_ref[...] = jnp.concatenate([qkv[2 * DS :].reshape(SIDE_HEADS, 8, ROW_LEN), ones], axis=1).reshape(2 * DS, ROW_LEN).astype(BF)
    middle_ahead(ctx_ref, turned_ref, 1)
    k, v = qkvt_ref[DS : 2 * DS].T, qkvt_ref[2 * DS :].T
    norm_ahead()
    blocks = [(half, h) for half in range(2) for h in range(SIDE_HEADS)]
    sums = []
    for n, (half, h) in enumerate(blocks + [(None, None)] * LAG_FORWARD):
        if n < len(blocks):
            side_scores(half, h, k, qkvt_ref, e_ref, bias_ref, False)
        if n >= LAG_FORWARD:
            sums.append(side_values(*blocks[n - LAG_FORWARD], vt_ref, e_ref, ctxt_ref, inv_ref))

    @pl.when(out_of_range(sums))
    def _():
        keys = qkvt_ref[DS : 2 * DS].T
        for half in range(2):

            def again(h, carry):
                side_scores(half, h, keys, qkvt_ref, e_ref, bias_ref, True)
                side_values(half, h, vt_ref, e_ref, ctxt_ref, inv_ref)
                return carry

            lax.fori_loop(0, SIDE_HEADS, again, 0)

    ctx = ctxt_ref[...]
    ctxb = ctx.astype(BF)
    middle_side = inputs + dot(proj_ref[...], ctxb, 0, 0)
    scale2 = lax.rsqrt(jnp.mean(middle_side * middle_side, axis=0, keepdims=True) + EPS)
    snt = (middle_side * scale2 * gain2).astype(BF)
    expanded = dot(expand_ref[...], snt, 0, 0)
    activated, slope = gelu_and_slope(expanded)
    activated = activated.astype(BF)
    expanded_grad = (activated_grad * slope).astype(BF)
    second_grad = dot(expand_ref[...], expanded_grad)
    low = D + 2 * SFF
    cot = rolled_ref[1]
    cotb = cot.astype(BF)
    side_out = middle_side + dot(shrinkt_ref[...], activated)
    out_ref[...] = pltpu.roll(side_out, shift, 1)
    grads_ref[:, D : D + SFF] += dot(snt, expanded_grad, 1, 1)
    grads_ref[:, D + SFF : low] += dot(cotb, activated, 1, 1)
    w2 = second_grad * gain2
    ms = middle_side * scale2
    mean2 = jnp.mean(w2 * middle_side, axis=0, keepdims=True)
    middle_grad = cot + scale2 * w2 - ms * (scale2 * scale2) * mean2
    acc_ref[0] += second_grad * ms
    branch = middle_grad.astype(BF)
    context_grad = dot(proj_ref[...], branch).astype(BF).astype(F32)
    grads_ref[:, low + 3 * DS : low + 4 * DS] += dot(ctxb, branch, 1, 1)
    dop = (context_grad * inv_ref[...]).astype(BF)
    centre = jnp.sum((dop.astype(F32) * ctx).reshape(SIDE_HEADS, 8, ROW_LEN), axis=1)
    centre = jnp.concatenate([centre, jnp.zeros((4, ROW_LEN), F32)], axis=0)
    chigh = centre.astype(BF)
    clow = (centre - chigh.astype(F32)).astype(BF)
    dstack = jnp.concatenate([dop, -chigh, -clow], axis=0)
    vones = jnp.concatenate([v, jnp.ones((ROW_LEN, 32), BF)], axis=1)
    root = SIDE_HEAD_DIM**-0.5

    def score_step(n):
        half, h = blocks[n]
        rows = slice(half * HALF, (half + 1) * HALF)
        dp = dot(vones[rows] * head_mask(h, 128), dstack[:, rows])
        ds_ref[n] = (e_ref[n].astype(F32) * dp).astype(BF)
        et_ref[n] = e_ref[n].T

    def query_step(n):
        half, h = blocks[n]
        rows = slice(half * HALF, (half + 1) * HALF)
        dq_ref[own_rows(h), rows] = head_rows(dot(qkvt_ref[pair(DS, h), rows], ds_ref[n]), h) * root
        e_ref[n] = ds_ref[n].T

    def value_step(n):
        half, h = blocks[n]
        rows = slice(half * HALF, (half + 1) * HALF)
        dq_ref[own_rows(h, 2 * DS), rows] = head_rows(dot(dop[16 * (h // 2) : 16 * (h // 2) + 16, rows], et_ref[n]), h)

    def key_step(n):
        half, h = blocks[n]
        rows = slice(half * HALF, (half + 1) * HALF)
        dq_ref[own_rows(h, DS), rows] = head_rows(dot(qkvt_ref[pair(0, h), rows], e_ref[n]), h) * root

    for n in range(len(blocks) + 3 * LAG_BACK):
        for i, step in enumerate((score_step, query_step, value_step, key_step)):
            if 0 <= n - i * LAG_BACK < len(blocks):
                step(n - i * LAG_BACK)
    dqkvt = dq_ref[...].astype(BF)
    bb_out_ref[...] = turn_rows(f_ref, back).astype(BF)
    first_grad = dot(wqkvt_ref[...], dqkvt, 0, 0)
    grads_ref[:, low : low + 3 * DS] += dot(fnt, dqkvt, 1, 1)
    w1 = first_grad * gain1
    ins = inputs * scale1
    mean1 = jnp.mean(w1 * inputs, axis=0, keepdims=True)
    input_grad = middle_grad + scale1 * w1 - ins * (scale1 * scale1) * mean1
    acc_ref[1] += first_grad * ins
    acc_ref[2] += input_grad * (lowered - side)
    state_ref[...] = pltpu.roll((1.0 - mixing) * input_grad, shift, 1)
    grads_ref[:, 0:D] += dot((mixing * input_grad).astype(BF), bb)

    @pl.when(r == last)
    def _():
        gate = cols_ref[0][:, 0:1]
        total = [jnp.sum(acc_ref[i], axis=1, keepdims=True) for i in range(3)]
        total[2] = total[2] * (gate * (1.0 - gate)) * 10.0
        place = lax.broadcasted_iota(jnp.int32, (DS, 128), 1)
        grads_ref[:, low + 4 * DS :] = jnp.where(place == 0, total[0], jnp.where(place == 1, total[1], jnp.where(place == 2, total[2], 0.0)))
        half = DS // 2
        tensor = (first_ref[0] != 0).astype(jnp.int32)
        mine_ref[...] = grads_ref[pl.ds(pl.multiple_of(tensor * half, 8), half), :].astype(BF)
        other_ref[...] = grads_ref[pl.ds(pl.multiple_of((1 - tensor) * half, 8), half), :].astype(BF)


def whole(shape):
    return pl.BlockSpec(shape, lambda r, *_: (0,) * len(shape), pipeline_mode=pl.Buffered(1))


def params(limit):
    return pltpu.CompilerParams(vmem_limit_bytes=limit * 1024 * 1024, dimension_semantics=("arbitrary",))


def swap(x):
    return lax.ppermute(x, "tensor", [(0, 1), (1, 0)])


def sum_over(mine, other, batch):
    place = lax.axis_index("batch")
    group = place & 3

    def trade(x, bits):
        return lax.ppermute(x, "batch", [(i, i ^ bits) for i in range(batch)])

    def pick(parts, k):
        return jnp.where(k == 0, parts[0], jnp.where(k == 1, parts[1], jnp.where(k == 2, parts[2], parts[3])))

    part = mine.astype(F32) + swap(other).astype(F32)
    bit, grouped = 1, batch >= 4
    if grouped:
        parts = jnp.split(part.astype(BF), 4, axis=1)
        got = [trade(pick(parts, group ^ m), m).astype(F32) for m in (1, 2, 3)]
        part = (pick(parts, group).astype(F32) + got[0]) + (got[1] + got[2])
        bit = 4
    while bit < batch:
        sent = part.astype(BF)
        part = sent.astype(F32) + trade(sent, bit).astype(F32)
        bit *= 2
    sent = part.astype(BF)
    if grouped:
        got = [sent] + [trade(sent, m) for m in (1, 2, 3)]
        sent = jnp.concatenate([pick(got, group ^ j) for j in range(4)], axis=1)
    return sent, swap(sent)


def unpack_kernel(tensor_ref, sent_ref, got_ref, down_ref, alpha_ref, gain1_ref, q_ref, k_ref, v_ref, proj_ref, gain2_ref, expand_ref, shrink_ref):
    upper = tensor_ref[0] != 0

    def both(first, end):
        sent, got = sent_ref[:, first:end].astype(F32), got_ref[:, first:end].astype(F32)
        return jnp.concatenate([jnp.where(upper, got, sent), jnp.where(upper, sent, got)], axis=0)

    low = D + 2 * SFF
    down_ref[...] = both(0, D)
    expand_ref[...] = both(D, D + SFF)
    shrink_ref[...] = both(D + SFF, low)
    squares = both(low, low + 4 * DS)
    for i, ref in enumerate((q_ref, k_ref, v_ref, proj_ref)):
        ref[...] = squares[:, i * DS : (i + 1) * DS]
    vectors = both(low + 4 * DS, low + 4 * DS + 128).T
    for i, ref in enumerate((gain2_ref, gain1_ref, alpha_ref)):
        ref[...] = vectors[i]


def make_body(batch):
    def body(
        hidden_in,
        lengths,
        attn_gain,
        attn_query,
        attn_key,
        attn_value,
        attn_out,
        ffn_gain,
        ffn_in,
        ffn_out,
        side_state,
        gate_alpha,
        down_w,
        side_attn_gain,
        side_query,
        side_key,
        side_value,
        side_proj,
        side_ffn_gain,
        side_expand,
        side_shrink,
        cotangent,
    ):
        tokens = hidden_in.shape[0]
        rows = tokens // ROW_LEN
        units = ffn_in.shape[1]
        t = lax.axis_index("tensor")
        first = (t * rows).astype(jnp.int32).reshape(1)
        tile = pl.BlockSpec((ROW_LEN, D), lambda r, *_: (r, 0))
        hbm = pl.BlockSpec(memory_space=pltpu.HBM)
        lens = pltpu.with_memory_space_constraint(lengths.T, pltpu.HBM)

        def kernel(body, name, limit, in_specs, out_specs, out_shape, scratch):
            return pl.pallas_call(
                body,
                grid_spec=pltpu.PrefetchScalarGridSpec(
                    num_scalar_prefetch=2, grid=(rows,), in_specs=in_specs, out_specs=out_specs, scratch_shapes=scratch
                ),
                out_shape=out_shape,
                compiler_params=params(limit),
                name=name,
            )

        own_attn = (attn_query, attn_key, attn_value)
        far_attn = [swap(w) for w in own_attn]
        own_attn = [pltpu.with_memory_space_constraint(w, pltpu.HBM) for w in own_attn]
        hidden_in = pltpu.with_memory_space_constraint(hidden_in, pltpu.HBM)
        attn_gain = pltpu.with_memory_space_constraint(attn_gain, pltpu.HBM)
        turned, joined = kernel(
            turn_kernel,
            "turn_rows",
            11,
            [hbm] * 4,
            [tile, pl.BlockSpec(memory_space=pl.ANY)],
            [jax.ShapeDtypeStruct((tokens, D), BF), jax.ShapeDtypeStruct((3, D, attn_query.shape[1]), BF)],
            [
                pltpu.VMEM((rows, ROW_LEN, D), BF),
                pltpu.VMEM((ROW_LEN, D), F32),
                pltpu.SemaphoreType.DMA((rows,)),
                pltpu.SemaphoreType.DMA((3,)),
            ],
        )(first, lens, hidden_in, *own_attn)
        far_attn, turned, attn_out, ffn_in, ffn_out = lax.optimization_barrier((far_attn, turned, attn_out, ffn_in, ffn_out))
        far_out, far_in, far_shrink = [swap(w) for w in (attn_out, ffn_in, ffn_out)]
        next_tile = pl.BlockSpec((ROW_LEN, D), lambda r, *_: (jnp.minimum(r + 1, rows - 1), 0))
        wide_tile = pl.BlockSpec((D, ROW_LEN), lambda r, *_: (0, r))
        ctx = kernel(
            attention_kernel,
            "attention",
            20,
            [whole((ROW_LEN, D)), next_tile, whole((D,)), whole((3, D, D // 2))] + [whole((D, D // 2))] * 3,
            wide_tile,
            jax.ShapeDtypeStruct((D, tokens), BF),
            [
                pltpu.VMEM((D, 3 * D), BF),
                pltpu.VMEM((ROW_LEN, 3 * D), BF),
                pltpu.VMEM((D, ROW_LEN), BF),
                pltpu.VMEM((2 * HEADS, HALF, HALF), BF),
                pltpu.VMEM((HALF, HALF), F32),
                pltpu.VMEM((ROW_LEN, D), BF),
            ],
        )(first, lens, turned, turned, attn_gain, joined, *far_attn)
        side_tile = pl.BlockSpec((DS, ROW_LEN), lambda r, *_: (0, r))
        side = pltpu.VMEM((DS, ROW_LEN), F32)
        square = pltpu.VMEM((2 * SIDE_HEADS, HALF, HALF), BF)
        backbone, side_out, state_grad, mine, other = kernel(
            side_kernel,
            "forward_and_back",
            32,
            [
                whole((D, ROW_LEN)),
                whole((ROW_LEN, D)),
                pl.BlockSpec((D, ROW_LEN), lambda r, *_: (0, jnp.minimum(r + 1, rows - 1))),
                next_tile,
            ]
            + [whole((D // 2, D))] * 2
            + [whole((D, units))] * 2
            + [whole((units, D))] * 2
            + [whole((D,)), side_tile, side_tile]
            + [whole((DS,))] * 3
            + [whole((DS, D))]
            + [whole((DS, DS))] * 4
            + [whole((DS, SFF))] * 2,
            [tile, side_tile, side_tile] + [pl.BlockSpec((DS // 2, GRAD_LANES), lambda r, *_: (0, 0))] * 2,
            [
                jax.ShapeDtypeStruct((tokens, D), BF),
                jax.ShapeDtypeStruct((DS, tokens), F32),
                jax.ShapeDtypeStruct((DS, tokens), F32),
                jax.ShapeDtypeStruct((DS // 2, GRAD_LANES), BF),
                jax.ShapeDtypeStruct((DS // 2, GRAD_LANES), BF),
            ],
            [
                pltpu.VMEM((D, D), BF),
                pltpu.VMEM((2 * units, D), BF),
                pltpu.VMEM((ROW_LEN, D), F32),
                pltpu.VMEM((ROW_LEN, 2 * units), BF),
                pltpu.VMEM((ROW_LEN, D), BF),
                pltpu.VMEM((ROW_LEN, D), F32),
                pltpu.VMEM((DS, GRAD_LANES), F32),
                pltpu.VMEM((3, DS, ROW_LEN), F32),
                pltpu.VMEM((3, DS, ROW_LEN), F32),
                pltpu.VMEM((3 * DS, DS), BF),
                pltpu.VMEM((HALF, HALF), F32),
                square,
                square,
                square,
                side,
                side,
                pltpu.VMEM((3 * DS, ROW_LEN), BF),
                pltpu.VMEM((3 * DS, ROW_LEN), F32),
                pltpu.VMEM((2, DS, ROW_LEN), F32),
                pltpu.VMEM((2 * DS, ROW_LEN), BF),
            ],
        )(
            first,
            lens,
            ctx,
            turned,
            ctx,
            turned,
            attn_out,
            far_out,
            ffn_in,
            far_in,
            ffn_out,
            far_shrink,
            ffn_gain,
            side_state.T,
            cotangent.T,
            gate_alpha,
            side_attn_gain,
            side_ffn_gain,
            down_w.T,
            side_query,
            side_key,
            side_value,
            side_proj,
            side_expand,
            side_shrink.T,
        )
        square_out = jax.ShapeDtypeStruct((DS, DS), F32)
        vector_out = jax.ShapeDtypeStruct((DS,), F32)
        wide_out = jax.ShapeDtypeStruct((DS, SFF), F32)
        vmem = pl.BlockSpec(memory_space=pltpu.VMEM)
        down, alpha, gain1, query, key, value, proj, gain2, expand, shrink = pl.pallas_call(
            unpack_kernel,
            in_specs=[pl.BlockSpec(memory_space=pltpu.SMEM), vmem, vmem],
            out_specs=[vmem] * 10,
            out_shape=[jax.ShapeDtypeStruct((DS, D), F32), vector_out, vector_out]
            + [square_out] * 4
            + [vector_out, wide_out, wide_out],
            compiler_params=pltpu.CompilerParams(vmem_limit_bytes=6 * 1024 * 1024),
            name="unpack",
        )(first, *sum_over(mine, other, batch))
        return backbone, side_out.T, state_grad.T, down.T, alpha, gain1, query, key, value, proj, gain2, expand, shrink.T

    return body


def solution(mesh):
    split = P(("batch", "tensor"), None)
    return jax.shard_map(
        make_body(mesh.shape["batch"]),
        mesh=mesh,
        in_specs=(
            split,
            P("batch", None),
            P(),
            P(None, "tensor"),
            P(None, "tensor"),
            P(None, "tensor"),
            P("tensor", None),
            P(),
            P(None, "tensor"),
            P("tensor", None),
            split,
            P(),
            P(),
            P(),
            P(),
            P(),
            P(),
            P(),
            P(),
            P(),
            P(),
            split,
        ),
        out_specs=(split, split, split) + (P(),) * 10,
        check_vma=False,
    )
```

```python
import jax
import jax.numpy as jnp
from jax import lax
from jax.experimental import pallas as pl
from jax.experimental.pallas import tpu as pltpu
from jax.sharding import PartitionSpec as P

BF = jnp.bfloat16
F32 = jnp.float32
D = 768
HEADS = 12
HEAD_DIM = 64
DS = 96
SIDE_HEADS = 12
SIDE_HEAD_DIM = 8
SFF = 384
ROW_LEN = 512
SEGS = 8
HALF = 256
GRAD_LANES = 2048
LAG_FORWARD = 6
LAG_BACK = 4
LOG2E = 1.4426950408889634
EPS = 1e-06


def dot(a, b, ca=1, cb=0):
    return lax.dot_general(a, b, (((ca,), (cb,)), ((), ())), preferred_element_type=F32)


def gelu(x):
    x2 = x * x
    u = x * (x2 * (0.7978845608028654 * 0.044715) + 0.7978845608028654)
    h = 0.5 * x
    return h + h * jnp.tanh(u)


def gelu_and_slope(x):
    x2 = x * x
    u = x * (x2 * (0.7978845608028654 * 0.044715) + 0.7978845608028654)
    p = 0.5 + 0.5 * jnp.tanh(u)
    out = x * p
    return out, p + out * (1.0 - p) * (x2 * (1.5957691216057308 * 3.0 * 0.044715) + 1.5957691216057308)


def row_starts(first_ref, lens_ref, r):
    starts, begin = [], jnp.int32(0)
    long_start = jnp.int32(0)
    for j in range(SEGS):
        n = lens_ref[j, first_ref[0] + r]
        starts.append((begin, n))
        long_start = jnp.where(n == HALF, begin, long_start)
        begin = begin + n
    return long_start, [((b - long_start) & (ROW_LEN - 1), n) for b, n in starts]


def fill_bias(bias_ref, docs):
    q = lax.broadcasted_iota(jnp.int32, (1, HALF), 1) + HALF
    low = jnp.zeros((1, HALF), jnp.int32)
    high = jnp.zeros((1, HALF), jnp.int32)
    for b, n in docs:
        inside = (q >= b) & (q < b + n)
        low = jnp.where(inside, b, low)
        high = jnp.where(inside, b + n, high)
    k = lax.broadcasted_iota(jnp.int32, (HALF, HALF), 0) + HALF
    bias_ref[...] = jnp.where((k >= low) & (k < high), 0.0, -1e30)


def turn_rows(src_ref, shift):
    n = src_ref.shape[1]
    part = shift & 7
    first = lax.shift_right_logical(shift, 3)
    groups = []
    for g in range(ROW_LEN // 8 + 1):
        start = pl.multiple_of(((first + g) & (ROW_LEN // 8 - 1)) * 8, 8)
        groups.append(src_ref[pl.ds(start, 8), :])
    wide = jnp.concatenate(groups, axis=0).reshape(ROW_LEN // 8 + 1, 8, n)
    back = (8 - part) & 7
    wide = pltpu.roll(wide, back, 1)
    place = lax.broadcasted_iota(jnp.int32, (ROW_LEN // 8, 8, n), 1)
    turned = jnp.where(place < 8 - part, wide[:-1], wide[1:])
    return turned.reshape(ROW_LEN, n)


def exponentials(s, half, bias_ref, safe):
    if half:
        s = s + bias_ref[...]
    if safe:
        s = s - jnp.max(s, axis=0, keepdims=True)
    return jnp.exp2(s)


def out_of_range(sums):
    low, high = sums[0], sums[0]
    for one in sums[1:]:
        low, high = jnp.minimum(low, one), jnp.maximum(high, one)
    fine = (jnp.min(low) > 1e-20) & (jnp.max(high) < 1e20)
    return jnp.logical_not(fine)


def at(start, size, step):
    return pl.ds(start if isinstance(start, int) else pl.multiple_of(start, step), size)


def frozen_scores(half, h, qkv_ref, e_ref, bias_ref, safe):
    p, j = h // 2, h % 2
    lane = lax.broadcasted_iota(jnp.int32, (1, 128), 1)
    keep = (lane >= 64 * j) & (lane < 64 * (j + 1))
    rows = slice(half * HALF, (half + 1) * HALF)
    q2 = qkv_ref[rows, at(p * 128, 128, 128)]
    k2 = qkv_ref[rows, at(D + p * 128, 128, 128)]
    s = dot(k2 * keep.astype(F32).astype(BF), q2, 1, 1) * (LOG2E * HEAD_DIM**-0.5)
    e = exponentials(s, half, bias_ref, safe)
    e_ref[half * HEADS + h] = e.astype(BF)
    return jnp.sum(e, axis=0, keepdims=True)


def frozen_values(half, h, vt_ref, e_ref, ctxt_ref, total):
    rows = slice(half * HALF, (half + 1) * HALF)
    head = at(h * HEAD_DIM, HEAD_DIM, HEAD_DIM)
    ctxt_ref[head, rows] = (dot(vt_ref[head, rows], e_ref[half * HEADS + h]) * (1.0 / total)).astype(BF)


def start_copies(pairs, sems):
    for i, (src, dst) in enumerate(pairs):
        pltpu.make_async_copy(src, dst, sems.at[i]).start()


def wait_copies(pairs, sems, first, last):
    for i in range(first, last):
        src, dst = pairs[i]
        pltpu.make_async_copy(src, dst, sems.at[i]).wait()


def turn_kernel(first_ref, lens_ref, x_ref, wq_ref, wk_ref, wv_ref, turned_ref, joined_ref, held_ref, raw_ref, sems, joined_sems):
    r = pl.program_id(0)
    rows = held_ref.shape[0]
    copies = [(x_ref.at[i * ROW_LEN : (i + 1) * ROW_LEN], held_ref.at[i]) for i in range(rows)]
    joins = [(w, joined_ref.at[i]) for i, w in enumerate((wq_ref, wk_ref, wv_ref))]

    @pl.when(r == 0)
    def _():
        start_copies(copies, sems)

    @pl.when(r == min(1, rows - 1))
    def _():
        start_copies(joins, joined_sems)

    pltpu.make_async_copy(x_ref.at[pl.ds(pl.multiple_of(r * ROW_LEN, ROW_LEN), ROW_LEN)], held_ref.at[r], sems.at[r]).wait()
    shift, _ = row_starts(first_ref, lens_ref, r)
    raw_ref[...] = held_ref[r].astype(F32)
    turned_ref[...] = turn_rows(raw_ref, shift).astype(BF)

    @pl.when(r == rows - 1)
    def _():
        wait_copies(joins, joined_sems, 0, 3)


def attention_kernel(
    first_ref,
    lens_ref,
    turned0_ref,
    turned_ref,
    gain_ref,
    joined_ref,
    wq_ref,
    wk_ref,
    wv_ref,
    ctxt_ref,
    wqkv_ref,
    qkv_ref,
    vt_ref,
    e_ref,
    bias_ref,
    nb_ref,
):
    r = pl.program_id(0)
    cols = wq_ref.shape[1]

    def norm_ahead(ref):
        x = ref[...].astype(F32)
        nb_ref[...] = (x * lax.rsqrt(jnp.mean(x * x, axis=1, keepdims=True) + EPS) * gain_ref[...].reshape(1, D)).astype(BF)

    @pl.when(r == 0)
    def _():
        norm_ahead(turned0_ref)
        for i, far in enumerate((wq_ref, wk_ref, wv_ref)):
            wqkv_ref[:, i * D : i * D + cols] = joined_ref[i]
            wqkv_ref[:, i * D + cols : (i + 1) * D] = far[...]

    _, docs = row_starts(first_ref, lens_ref, r)
    fill_bias(bias_ref, docs)
    qkv_ref[...] = dot(nb_ref[...], wqkv_ref[...]).astype(BF)
    norm_ahead(turned_ref)
    vt_ref[...] = qkv_ref[:, 2 * D :].T
    blocks = [(half, h) for half in range(2) for h in range(HEADS)]
    sums = [frozen_scores(half, h, qkv_ref, e_ref, bias_ref, False) for half, h in blocks]
    for (half, h), total in zip(blocks, sums):
        frozen_values(half, h, vt_ref, e_ref, ctxt_ref, total)

    @pl.when(out_of_range(sums))
    def _():
        for half in range(2):

            def again(h, carry):
                frozen_values(half, h, vt_ref, e_ref, ctxt_ref, frozen_scores(half, h, qkv_ref, e_ref, bias_ref, True))
                return carry

            lax.fori_loop(0, HEADS, again, 0)


def head_mask(h, width):
    lane = lax.broadcasted_iota(jnp.int32, (1, width), 1)
    own = (lane >= 8 * h) & (lane < 8 * h + 8)
    if width > DS:
        own = own | (lane == DS + h) | (lane == DS + 16 + h)
    return own.astype(F32).astype(BF)


def head_rows(product, h):
    low, high = product[:SIDE_HEAD_DIM], product[SIDE_HEAD_DIM:]
    if isinstance(h, int):
        return high if h % 2 else low
    return jnp.where(h % 2 == 1, high, low)


def pair(base, h):
    return at(base + 16 * (h // 2), 16, 16)


def own_rows(h, base=0):
    return at(base + SIDE_HEAD_DIM * h, SIDE_HEAD_DIM, SIDE_HEAD_DIM)


def side_scores(half, h, k, qkvt_ref, e_ref, bias_ref, safe):
    rows = slice(half * HALF, (half + 1) * HALF)
    s = dot(k[rows] * head_mask(h, DS), qkvt_ref[:DS, rows]) * (LOG2E * SIDE_HEAD_DIM**-0.5)
    e_ref[half * SIDE_HEADS + h] = exponentials(s, half, bias_ref, safe).astype(BF)


def side_values(half, h, vt_ref, e_ref, ctxt_ref, inv_ref):
    rows = slice(half * HALF, (half + 1) * HALF)
    mixed = dot(vt_ref[at(16 * h, 16, 16), rows], e_ref[half * SIDE_HEADS + h])
    total = mixed[8:9]
    inv = 1.0 / total
    ctxt_ref[own_rows(h), rows] = mixed[:8] * inv
    inv_ref[own_rows(h), rows] = jnp.broadcast_to(inv, (SIDE_HEAD_DIM, HALF))
    return total


def side_kernel(
    first_ref,
    lens_ref,
    ctx0_ref,
    turned0_ref,
    ctx_ref,
    turned_ref,
    woa_ref,
    wob_ref,
    w1a_ref,
    w1b_ref,
    w2a_ref,
    w2b_ref,
    fgain_ref,
    side_ref,
    cot_ref,
    alpha_ref,
    gain1_ref,
    gain2_ref,
    downt_ref,
    sq_ref,
    sk_ref,
    sv_ref,
    proj_ref,
    expand_ref,
    shrinkt_ref,
    bb_out_ref,
    out_ref,
    state_ref,
    mine_ref,
    other_ref,
    wo_ref,
    w2_ref,
    mid_ref,
    hid_ref,
    nb_ref,
    f_ref,
    grads_ref,
    acc_ref,
    cols_ref,
    wqkvt_ref,
    bias_ref,
    e_ref,
    et_ref,
    ds_ref,
    inv_ref,
    ctxt_ref,
    qkvt_ref,
    dq_ref,
    rolled_ref,
    vt_ref,
):
    r = pl.program_id(0)
    last = pl.num_programs(0) - 1
    units = w1a_ref.shape[1]

    def middle_ahead(ctx, turned, half):
        rows = slice(half * HALF, (half + 1) * HALF)
        mid_ref[rows] = turned[rows].astype(F32) + dot(ctx[:, rows].T, wo_ref[...])

    def norm_ahead():
        middle = mid_ref[...]
        nb_ref[...] = (middle * lax.rsqrt(jnp.mean(middle * middle, axis=1, keepdims=True) + EPS) * fgain_ref[...].reshape(1, D)).astype(BF)

    @pl.when(r == 0)
    def _():
        heads = woa_ref.shape[0]
        wo_ref[:heads] = woa_ref[...]
        wo_ref[heads:] = wob_ref[...]
        middle_ahead(ctx0_ref, turned0_ref, 0)
        middle_ahead(ctx0_ref, turned0_ref, 1)
        norm_ahead()
        w2_ref[:units] = w2a_ref[...]
        w2_ref[units:] = w2b_ref[...]
        grads_ref[...] = jnp.zeros_like(grads_ref)
        acc_ref[...] = jnp.zeros_like(acc_ref)
        for i, ref in enumerate((alpha_ref, gain1_ref, gain2_ref)):
            cols_ref[i] = jnp.broadcast_to(jnp.broadcast_to(ref[...].reshape(1, DS), (8, DS)).T[:, 0:1], (DS, ROW_LEN))
        cols_ref[0] = 1.0 / (1.0 + jnp.exp(cols_ref[0] * -10.0))
        wqkvt_ref[:DS] = sq_ref[...].T
        wqkvt_ref[DS : 2 * DS] = sk_ref[...].T
        wqkvt_ref[2 * DS :] = sv_ref[...].T

    shift, docs = row_starts(first_ref, lens_ref, r)
    back = (ROW_LEN - shift) & (ROW_LEN - 1)
    fill_bias(bias_ref, docs)

    rolled_ref[0] = pltpu.roll(side_ref[...].astype(F32), back, 1)
    rolled_ref[1] = pltpu.roll(cot_ref[...].astype(F32), back, 1)

    for i, w in enumerate((w1a_ref, w1b_ref)):
        for c in range(0, units, 256):
            hid_ref[:, i * units + c : i * units + c + 256] = gelu(dot(nb_ref[...], w[:, c : c + 256])).astype(BF)

    for c in range(0, ROW_LEN, 256):
        f_ref[c : c + 256] = mid_ref[c : c + 256] + dot(hid_ref[c : c + 256], w2_ref[...])
    bb = f_ref[...].astype(BF)

    mixing, gain1, gain2 = cols_ref[0], cols_ref[1], cols_ref[2]
    lowered = dot(downt_ref[...], bb, 1, 1)
    activated_grad = dot(shrinkt_ref[...], rolled_ref[1].astype(BF), 0, 0)
    middle_ahead(ctx_ref, turned_ref, 0)
    side = rolled_ref[0]
    inputs = mixing * lowered + (1.0 - mixing) * side
    scale1 = lax.rsqrt(jnp.mean(inputs * inputs, axis=0, keepdims=True) + EPS)
    fnt = (inputs * scale1 * gain1).astype(BF)
    qkv = dot(wqkvt_ref[...], fnt)
    qkvt_ref[...] = qkv.astype(BF)
    ones = jnp.ones((SIDE_HEADS, 8, ROW_LEN), F32)
    vt_ref[...] = jnp.concatenate([qkv[2 * DS :].reshape(SIDE_HEADS, 8, ROW_LEN), ones], axis=1).reshape(2 * DS, ROW_LEN).astype(BF)
    middle_ahead(ctx_ref, turned_ref, 1)
    k, v = qkvt_ref[DS : 2 * DS].T, qkvt_ref[2 * DS :].T
    norm_ahead()
    blocks = [(half, h) for half in range(2) for h in range(SIDE_HEADS)]
    sums = []
    for n, (half, h) in enumerate(blocks + [(None, None)] * LAG_FORWARD):
        if n < len(blocks):
            side_scores(half, h, k, qkvt_ref, e_ref, bias_ref, False)
        if n >= LAG_FORWARD:
            sums.append(side_values(*blocks[n - LAG_FORWARD], vt_ref, e_ref, ctxt_ref, inv_ref))

    @pl.when(out_of_range(sums))
    def _():
        keys = qkvt_ref[DS : 2 * DS].T
        for half in range(2):

            def again(h, carry):
                side_scores(half, h, keys, qkvt_ref, e_ref, bias_ref, True)
                side_values(half, h, vt_ref, e_ref, ctxt_ref, inv_ref)
                return carry

            lax.fori_loop(0, SIDE_HEADS, again, 0)

    ctx = ctxt_ref[...]
    ctxb = ctx.astype(BF)
    middle_side = inputs + dot(proj_ref[...], ctxb, 0, 0)
    scale2 = lax.rsqrt(jnp.mean(middle_side * middle_side, axis=0, keepdims=True) + EPS)
    snt = (middle_side * scale2 * gain2).astype(BF)
    expanded = dot(expand_ref[...], snt, 0, 0)
    activated, slope = gelu_and_slope(expanded)
    activated = activated.astype(BF)
    expanded_grad = (activated_grad * slope).astype(BF)
    second_grad = dot(expand_ref[...], expanded_grad)
    low = D + 2 * SFF
    cot = rolled_ref[1]
    cotb = cot.astype(BF)
    side_out = middle_side + dot(shrinkt_ref[...], activated)
    out_ref[...] = pltpu.roll(side_out, shift, 1)
    grads_ref[:, D : D + SFF] += dot(snt, expanded_grad, 1, 1)
    grads_ref[:, D + SFF : low] += dot(cotb, activated, 1, 1)
    w2 = second_grad * gain2
    ms = middle_side * scale2
    mean2 = jnp.mean(w2 * middle_side, axis=0, keepdims=True)
    middle_grad = cot + scale2 * w2 - ms * (scale2 * scale2) * mean2
    acc_ref[0] += second_grad * ms
    branch = middle_grad.astype(BF)
    context_grad = dot(proj_ref[...], branch).astype(BF).astype(F32)
    grads_ref[:, low + 3 * DS : low + 4 * DS] += dot(ctxb, branch, 1, 1)
    dop = (context_grad * inv_ref[...]).astype(BF)
    centre = jnp.sum((dop.astype(F32) * ctx).reshape(SIDE_HEADS, 8, ROW_LEN), axis=1)
    centre = jnp.concatenate([centre, jnp.zeros((4, ROW_LEN), F32)], axis=0)
    chigh = centre.astype(BF)
    clow = (centre - chigh.astype(F32)).astype(BF)
    dstack = jnp.concatenate([dop, -chigh, -clow], axis=0)
    vones = jnp.concatenate([v, jnp.ones((ROW_LEN, 32), BF)], axis=1)
    root = SIDE_HEAD_DIM**-0.5

    def score_step(n):
        half, h = blocks[n]
        rows = slice(half * HALF, (half + 1) * HALF)
        dp = dot(vones[rows] * head_mask(h, 128), dstack[:, rows])
        ds_ref[n] = (e_ref[n].astype(F32) * dp).astype(BF)
        et_ref[n] = e_ref[n].T

    def query_step(n):
        half, h = blocks[n]
        rows = slice(half * HALF, (half + 1) * HALF)
        dq_ref[own_rows(h), rows] = head_rows(dot(qkvt_ref[pair(DS, h), rows], ds_ref[n]), h) * root
        e_ref[n] = ds_ref[n].T

    def value_step(n):
        half, h = blocks[n]
        rows = slice(half * HALF, (half + 1) * HALF)
        dq_ref[own_rows(h, 2 * DS), rows] = head_rows(dot(dop[16 * (h // 2) : 16 * (h // 2) + 16, rows], et_ref[n]), h)

    def key_step(n):
        half, h = blocks[n]
        rows = slice(half * HALF, (half + 1) * HALF)
        dq_ref[own_rows(h, DS), rows] = head_rows(dot(qkvt_ref[pair(0, h), rows], e_ref[n]), h) * root

    for n in range(len(blocks) + 3 * LAG_BACK):
        for i, step in enumerate((score_step, query_step, value_step, key_step)):
            if 0 <= n - i * LAG_BACK < len(blocks):
                step(n - i * LAG_BACK)
    dqkvt = dq_ref[...].astype(BF)
    bb_out_ref[...] = turn_rows(f_ref, back).astype(BF)
    first_grad = dot(wqkvt_ref[...], dqkvt, 0, 0)
    grads_ref[:, low : low + 3 * DS] += dot(fnt, dqkvt, 1, 1)
    w1 = first_grad * gain1
    ins = inputs * scale1
    mean1 = jnp.mean(w1 * inputs, axis=0, keepdims=True)
    input_grad = middle_grad + scale1 * w1 - ins * (scale1 * scale1) * mean1
    acc_ref[1] += first_grad * ins
    acc_ref[2] += input_grad * (lowered - side)
    state_ref[...] = pltpu.roll((1.0 - mixing) * input_grad, shift, 1)
    grads_ref[:, 0:D] += dot((mixing * input_grad).astype(BF), bb)

    @pl.when(r == last)
    def _():
        gate = cols_ref[0][:, 0:1]
        total = [jnp.sum(acc_ref[i], axis=1, keepdims=True) for i in range(3)]
        total[2] = total[2] * (gate * (1.0 - gate)) * 10.0
        place = lax.broadcasted_iota(jnp.int32, (DS, 128), 1)
        grads_ref[:, low + 4 * DS :] = jnp.where(place == 0, total[0], jnp.where(place == 1, total[1], jnp.where(place == 2, total[2], 0.0)))
        half = DS // 2
        tensor = (first_ref[0] != 0).astype(jnp.int32)
        mine_ref[...] = grads_ref[pl.ds(pl.multiple_of(tensor * half, 8), half), :].astype(BF)
        other_ref[...] = grads_ref[pl.ds(pl.multiple_of((1 - tensor) * half, 8), half), :].astype(BF)


def whole(shape):
    return pl.BlockSpec(shape, lambda r, *_: (0,) * len(shape), pipeline_mode=pl.Buffered(1))


def params(limit):
    return pltpu.CompilerParams(vmem_limit_bytes=limit * 1024 * 1024, dimension_semantics=("arbitrary",))


def swap(x):
    return lax.ppermute(x, "tensor", [(0, 1), (1, 0)])


def sum_over(mine, other, batch):
    place = lax.axis_index("batch")
    group = place & 3

    def trade(x, bits):
        return lax.ppermute(x, "batch", [(i, i ^ bits) for i in range(batch)])

    def pick(parts, k):
        return jnp.where(k == 0, parts[0], jnp.where(k == 1, parts[1], jnp.where(k == 2, parts[2], parts[3])))

    part = mine.astype(F32) + swap(other).astype(F32)
    bit, grouped = 1, batch >= 4
    if grouped:
        parts = jnp.split(part.astype(BF), 4, axis=1)
        got = [trade(pick(parts, group ^ m), m).astype(F32) for m in (1, 2, 3)]
        part = (pick(parts, group).astype(F32) + got[0]) + (got[1] + got[2])
        bit = 4
    while bit < batch:
        sent = part.astype(BF)
        part = sent.astype(F32) + trade(sent, bit).astype(F32)
        bit *= 2
    sent = part.astype(BF)
    if grouped:
        got = [sent] + [trade(sent, m) for m in (1, 2, 3)]
        sent = jnp.concatenate([pick(got, group ^ j) for j in range(4)], axis=1)
    return sent, swap(sent)


def unpack_kernel(tensor_ref, sent_ref, got_ref, down_ref, alpha_ref, gain1_ref, q_ref, k_ref, v_ref, proj_ref, gain2_ref, expand_ref, shrink_ref):
    upper = tensor_ref[0] != 0

    def both(first, end):
        sent, got = sent_ref[:, first:end].astype(F32), got_ref[:, first:end].astype(F32)
        return jnp.concatenate([jnp.where(upper, got, sent), jnp.where(upper, sent, got)], axis=0)

    low = D + 2 * SFF
    down_ref[...] = both(0, D)
    expand_ref[...] = both(D, D + SFF)
    shrink_ref[...] = both(D + SFF, low)
    squares = both(low, low + 4 * DS)
    for i, ref in enumerate((q_ref, k_ref, v_ref, proj_ref)):
        ref[...] = squares[:, i * DS : (i + 1) * DS]
    vectors = both(low + 4 * DS, low + 4 * DS + 128).T
    for i, ref in enumerate((gain2_ref, gain1_ref, alpha_ref)):
        ref[...] = vectors[i]


def make_body(batch):
    def body(
        hidden_in,
        lengths,
        attn_gain,
        attn_query,
        attn_key,
        attn_value,
        attn_out,
        ffn_gain,
        ffn_in,
        ffn_out,
        side_state,
        gate_alpha,
        down_w,
        side_attn_gain,
        side_query,
        side_key,
        side_value,
        side_proj,
        side_ffn_gain,
        side_expand,
        side_shrink,
        cotangent,
    ):
        tokens = hidden_in.shape[0]
        rows = tokens // ROW_LEN
        units = ffn_in.shape[1]
        t = lax.axis_index("tensor")
        first = (t * rows).astype(jnp.int32).reshape(1)
        tile = pl.BlockSpec((ROW_LEN, D), lambda r, *_: (r, 0))
        hbm = pl.BlockSpec(memory_space=pltpu.HBM)
        lens = pltpu.with_memory_space_constraint(lengths.T, pltpu.HBM)

        def kernel(body, name, limit, in_specs, out_specs, out_shape, scratch):
            return pl.pallas_call(
                body,
                grid_spec=pltpu.PrefetchScalarGridSpec(
                    num_scalar_prefetch=2, grid=(rows,), in_specs=in_specs, out_specs=out_specs, scratch_shapes=scratch
                ),
                out_shape=out_shape,
                compiler_params=params(limit),
                name=name,
            )

        own_attn = (attn_query, attn_key, attn_value)
        far_attn = [swap(w) for w in own_attn]
        own_attn = [pltpu.with_memory_space_constraint(w, pltpu.HBM) for w in own_attn]
        hidden_in = pltpu.with_memory_space_constraint(hidden_in, pltpu.HBM)
        attn_gain = pltpu.with_memory_space_constraint(attn_gain, pltpu.HBM)
        turned, joined = kernel(
            turn_kernel,
            "turn_rows",
            11,
            [hbm] * 4,
            [tile, pl.BlockSpec(memory_space=pl.ANY)],
            [jax.ShapeDtypeStruct((tokens, D), BF), jax.ShapeDtypeStruct((3, D, attn_query.shape[1]), BF)],
            [
                pltpu.VMEM((rows, ROW_LEN, D), BF),
                pltpu.VMEM((ROW_LEN, D), F32),
                pltpu.SemaphoreType.DMA((rows,)),
                pltpu.SemaphoreType.DMA((3,)),
            ],
        )(first, lens, hidden_in, *own_attn)
        far_attn, turned, attn_out, ffn_in, ffn_out = lax.optimization_barrier((far_attn, turned, attn_out, ffn_in, ffn_out))
        far_out, far_in, far_shrink = [swap(w) for w in (attn_out, ffn_in, ffn_out)]
        next_tile = pl.BlockSpec((ROW_LEN, D), lambda r, *_: (jnp.minimum(r + 1, rows - 1), 0))
        wide_tile = pl.BlockSpec((D, ROW_LEN), lambda r, *_: (0, r))
        ctx = kernel(
            attention_kernel,
            "attention",
            20,
            [whole((ROW_LEN, D)), next_tile, whole((D,)), whole((3, D, D // 2))] + [whole((D, D // 2))] * 3,
            wide_tile,
            jax.ShapeDtypeStruct((D, tokens), BF),
            [
                pltpu.VMEM((D, 3 * D), BF),
                pltpu.VMEM((ROW_LEN, 3 * D), BF),
                pltpu.VMEM((D, ROW_LEN), BF),
                pltpu.VMEM((2 * HEADS, HALF, HALF), BF),
                pltpu.VMEM((HALF, HALF), F32),
                pltpu.VMEM((ROW_LEN, D), BF),
            ],
        )(first, lens, turned, turned, attn_gain, joined, *far_attn)
        side_tile = pl.BlockSpec((DS, ROW_LEN), lambda r, *_: (0, r))
        side = pltpu.VMEM((DS, ROW_LEN), F32)
        square = pltpu.VMEM((2 * SIDE_HEADS, HALF, HALF), BF)
        backbone, side_out, state_grad, mine, other = kernel(
            side_kernel,
            "forward_and_back",
            32,
            [
                whole((D, ROW_LEN)),
                whole((ROW_LEN, D)),
                pl.BlockSpec((D, ROW_LEN), lambda r, *_: (0, jnp.minimum(r + 1, rows - 1))),
                next_tile,
            ]
            + [whole((D // 2, D))] * 2
            + [whole((D, units))] * 2
            + [whole((units, D))] * 2
            + [whole((D,)), side_tile, side_tile]
            + [whole((DS,))] * 3
            + [whole((DS, D))]
            + [whole((DS, DS))] * 4
            + [whole((DS, SFF))] * 2,
            [tile, side_tile, side_tile] + [pl.BlockSpec((DS // 2, GRAD_LANES), lambda r, *_: (0, 0))] * 2,
            [
                jax.ShapeDtypeStruct((tokens, D), BF),
                jax.ShapeDtypeStruct((DS, tokens), F32),
                jax.ShapeDtypeStruct((DS, tokens), F32),
                jax.ShapeDtypeStruct((DS // 2, GRAD_LANES), BF),
                jax.ShapeDtypeStruct((DS // 2, GRAD_LANES), BF),
            ],
            [
                pltpu.VMEM((D, D), BF),
                pltpu.VMEM((2 * units, D), BF),
                pltpu.VMEM((ROW_LEN, D), F32),
                pltpu.VMEM((ROW_LEN, 2 * units), BF),
                pltpu.VMEM((ROW_LEN, D), BF),
                pltpu.VMEM((ROW_LEN, D), F32),
                pltpu.VMEM((DS, GRAD_LANES), F32),
                pltpu.VMEM((3, DS, ROW_LEN), F32),
                pltpu.VMEM((3, DS, ROW_LEN), F32),
                pltpu.VMEM((3 * DS, DS), BF),
                pltpu.VMEM((HALF, HALF), F32),
                square,
                square,
                square,
                side,
                side,
                pltpu.VMEM((3 * DS, ROW_LEN), BF),
                pltpu.VMEM((3 * DS, ROW_LEN), F32),
                pltpu.VMEM((2, DS, ROW_LEN), F32),
                pltpu.VMEM((2 * DS, ROW_LEN), BF),
            ],
        )(
            first,
            lens,
            ctx,
            turned,
            ctx,
            turned,
            attn_out,
            far_out,
            ffn_in,
            far_in,
            ffn_out,
            far_shrink,
            ffn_gain,
            side_state.T,
            cotangent.T,
            gate_alpha,
            side_attn_gain,
            side_ffn_gain,
            down_w.T,
            side_query,
            side_key,
            side_value,
            side_proj,
            side_expand,
            side_shrink.T,
        )
        square_out = jax.ShapeDtypeStruct((DS, DS), F32)
        vector_out = jax.ShapeDtypeStruct((DS,), F32)
        wide_out = jax.ShapeDtypeStruct((DS, SFF), F32)
        vmem = pl.BlockSpec(memory_space=pltpu.VMEM)
        down, alpha, gain1, query, key, value, proj, gain2, expand, shrink = pl.pallas_call(
            unpack_kernel,
            in_specs=[pl.BlockSpec(memory_space=pltpu.SMEM), vmem, vmem],
            out_specs=[vmem] * 10,
            out_shape=[jax.ShapeDtypeStruct((DS, D), F32), vector_out, vector_out]
            + [square_out] * 4
            + [vector_out, wide_out, wide_out],
            compiler_params=pltpu.CompilerParams(vmem_limit_bytes=6 * 1024 * 1024),
            name="unpack",
        )(first, *sum_over(mine, other, batch))
        return backbone, side_out.T, state_grad.T, down.T, alpha, gain1, query, key, value, proj, gain2, expand, shrink.T

    return body


def solution(mesh):
    split = P(("batch", "tensor"), None)
    return jax.shard_map(
        make_body(mesh.shape["batch"]),
        mesh=mesh,
        in_specs=(
            split,
            P("batch", None),
            P(),
            P(None, "tensor"),
            P(None, "tensor"),
            P(None, "tensor"),
            P("tensor", None),
            P(),
            P(None, "tensor"),
            P("tensor", None),
            split,
            P(),
            P(),
            P(),
            P(),
            P(),
            P(),
            P(),
            P(),
            P(),
            P(),
            split,
        ),
        out_specs=(split, split, split) + (P(),) * 10,
        check_vma=False,
    )
```
